32 devices in a mesh: dp: 4 (over x, core), fsdp: 8 (over z, y).
Axes of the slice: x: 2, y: 2, z: 4, core: 2. Of those that a mesh axis runs over, the one named last changes fastest.
Arguments:
- block_input: bfloat16 [32, 512, 576], P(('dp', 'fsdp')), may hold values from -18 to 18
- lengths: int32 [32], P(('dp', 'fsdp')), may hold values from 128 to 512, as said below
- attention_gain: float32 [576], replicated, may hold values from 0.1 to 1.9
- query_weight: bfloat16 [576, 576], P('dp', 'fsdp'), may hold values from -0.25 to 0.25
- key_matrix: bfloat16 [576, 192], P('dp', 'fsdp'), may hold values from -0.25 to 0.25
- value_matrix: bfloat16 [576, 192], P('dp', 'fsdp'), may hold values from -0.25 to 0.25
- output_weight: bfloat16 [576, 576], P('dp', 'fsdp'), may hold values from -1 to 1
- mlp_gain: float32 [576], replicated, may hold values from 0.1 to 1.9
- gate_weight: bfloat16 [576, 1536], P('dp', 'fsdp'), may hold values from -0.25 to 0.25
- up_weight: bfloat16 [576, 1536], P('dp', 'fsdp'), may hold values from -0.25 to 0.25
- down_weight: bfloat16 [1536, 576], P('dp', 'fsdp'), may hold values from -0.15625 to 0.15625
- cotangent: bfloat16 [32, 512, 576], P(('dp', 'fsdp')), may hold values from -6 to 6
Outputs:
- block_output: bfloat16 [32, 512, 576], P(('dp', 'fsdp'))
- input_grad: float32 [32, 512, 576], P(('dp', 'fsdp'))
- grad_attention_gain: float32 [576], replicated
- grad_query: float32 [576, 576], P('dp', 'fsdp')
- grad_key: float32 [576, 192], P('dp', 'fsdp')
- grad_value: float32 [576, 192], P('dp', 'fsdp')
- grad_output: float32 [576, 576], P('dp', 'fsdp')
- grad_mlp_gain: float32 [576], replicated
- grad_gate: float32 [576, 1536], P('dp', 'fsdp')
- grad_up: float32 [576, 1536], P('dp', 'fsdp')
- grad_down: float32 [1536, 576], P('dp', 'fsdp')
- stream_rms: float32 [2, 3], replicated
The draws below stay inside these ranges and needn't reach their ends.
Inputs may be any that keep to these rules, and one draw needn't show every extreme that they name: `lengths`: slots are filled from their first place; some slot has exactly 512 valid tokens and some slot exactly 128.
All inputs are finite; a program needn't handle non-finite values.
Results may differ from the reference program's by a relative error of at most 0.022.
Values may be sent and summed in bfloat16 or wider, within the bound.
A program may use at most 192 MiB of HBM per device.

```python
import math
import jax
import jax.numpy as jnp
from jax import lax

MODEL_WIDTH = 576
QUERY_HEADS = 9
KEY_VALUE_HEADS = 3
HEAD_SIZE = 64
FF = 1536
SLOT_PLACES = 512
LMIN = 128
SLOTS = 32


def draw_block_input(key, part):
    key = jax.random.fold_in(key, 11)
    entry_key = jax.random.fold_in(key, 0)
    rise = jnp.arange(SLOTS, dtype=jnp.float32) / max(SLOTS - 1, 1)
    entries = jax.random.truncated_normal(entry_key, -4.5, 4.5, (SLOTS, SLOT_PLACES, MODEL_WIDTH), jnp.float32)
    slot_scale = 0.6 * jnp.exp(jnp.log(3.0) * rise)
    value_rows = entries * slot_scale[:, None, None]
    return value_rows.astype(jnp.bfloat16)


def draw_lengths(key, part):
    key = jax.random.fold_in(key, 23)
    step_key, long_key, short_key = jax.random.split(key, 3)
    steps = jax.random.randint(step_key, (SLOTS,), 0, 64).astype(jnp.int32)
    sizes = LMIN + (SLOT_PLACES - LMIN) * (steps * steps + 128 * steps) // 12288
    longest = jax.random.randint(long_key, (), 0, SLOTS).astype(jnp.int32)
    shortest = (longest + 1 + jax.random.randint(short_key, (), 0, SLOTS - 1).astype(jnp.int32)) % SLOTS
    places = jnp.arange(SLOTS, dtype=jnp.int32)
    sizes = jnp.where(places == longest, SLOT_PLACES, sizes)
    sizes = jnp.where(places == shortest, LMIN, sizes)
    return sizes.astype(jnp.int32)


def spiked(values, own_key, source, target, blocks, factor):
    owner, partner = [(jnp.arange(values.shape[axis_at]) // (values.shape[axis_at] // blocks)).reshape([-1 if axis == axis_at else 1 for axis in range(values.ndim)]) for axis_at in (source, target)]
    chosen = jax.random.permutation(own_key, blocks)[partner]
    strong = (owner == chosen) | (owner == (partner + blocks // 2) % blocks)
    return jnp.where(strong, factor * values, values)


def block_levels(stream_key, dims, pieces, low, high):
    def one(dim, blocks):
        draws = jax.random.uniform(jax.random.fold_in(jax.random.fold_in(stream_key, 6), dim), (blocks,), jnp.float32, low / len(pieces), high / len(pieces))
        return jnp.repeat(jnp.exp(draws), dims[dim] // blocks).reshape((-1,) + (1,) * (len(dims) - dim - 1))

    level = one(*pieces[0])
    for cut in pieces[1:]:
        level = level * one(*cut)
    return level


def bell_draw(stream_key, extent, spread, most, cuts=(), kind=jnp.bfloat16):
    drawn = jax.random.normal(stream_key, extent, jnp.float32) * spread
    if len(cuts) > 0:
        drawn = block_levels(stream_key, extent, cuts, -0.22, 0.18) * drawn
    return jnp.clip(drawn, min=-most, max=most).astype(kind)


def gaussian_with(own_key, shape, width, most, cuts, heavy, kind=jnp.bfloat16):
    array = width * jax.random.normal(own_key, shape, jnp.float32)
    if cuts:
        array = array * block_levels(own_key, shape, cuts, -0.22, 0.18)
    return jnp.clip(spiked(array, jax.random.fold_in(own_key, 3), *heavy), -most, most).astype(kind)


def setup_inputs(seed: int = 0) -> dict:
    seeds = jax.random.split(jax.random.key(seed), 13)
    block_input = draw_block_input(jax.random.fold_in(seeds[12], 71), 0)
    lengths = draw_lengths(jax.random.fold_in(seeds[12], 71), 0)
    attention_gain = jnp.clip(1.0 + 0.18 * jax.random.normal(seeds[2], (MODEL_WIDTH,), jnp.float32), 0.1, 1.9)
    query_weight = bell_draw(seeds[3], (MODEL_WIDTH, MODEL_WIDTH), MODEL_WIDTH ** -0.5, 0.25, ((0, 4), (1, 8)))
    key_matrix = bell_draw(seeds[4], (MODEL_WIDTH, KEY_VALUE_HEADS * HEAD_SIZE), MODEL_WIDTH ** -0.5, 0.25, ((0, 4), (1, 8)))
    value_matrix = bell_draw(seeds[5], (MODEL_WIDTH, KEY_VALUE_HEADS * HEAD_SIZE), MODEL_WIDTH ** -0.5, 0.25, ((0, 4), (1, 8)))
    output_weight = bell_draw(seeds[6], (MODEL_WIDTH, MODEL_WIDTH), (MODEL_WIDTH // 16) ** -0.5, 1.0, ((0, 4), (1, 8)))
    mlp_gain = jnp.clip(1.0 + 0.18 * jax.random.normal(seeds[7], (MODEL_WIDTH,), jnp.float32), 0.1, 1.9)
    gate_weight = bell_draw(seeds[8], (MODEL_WIDTH, FF), MODEL_WIDTH ** -0.5, 0.25, ((0, 4), (1, 8)))
    up_weight = bell_draw(seeds[9], (MODEL_WIDTH, FF), MODEL_WIDTH ** -0.5, 0.25, ((0, 4), (1, 8)))
    down_weight = bell_draw(seeds[10], (FF, MODEL_WIDTH), FF ** -0.5, 0.15625, ((0, 4), (1, 8)))
    cotangent = gaussian_with(seeds[11], (SLOTS, SLOT_PLACES, MODEL_WIDTH), 1.0, 6.0, ((0, 32),), (0, 2, 32, 2.75))
    return dict(block_input=block_input, lengths=lengths, attention_gain=attention_gain, query_weight=query_weight, key_matrix=key_matrix, value_matrix=value_matrix, output_weight=output_weight, mlp_gain=mlp_gain, gate_weight=gate_weight, up_weight=up_weight, down_weight=down_weight, cotangent=cotangent)


ROPE_BASE = 10000.0
NORM_EPS = 1e-05
FULL_PRECISION = lax.Precision.HIGHEST

@jax.custom_vjp
def lower_precision(v):
    return lax.optimization_barrier(v.astype(jnp.bfloat16)).astype(jnp.float32)

@jax.custom_vjp
def lower_precision_back(v):
    return v

def low_keep(v):
    return (lower_precision(v), None)

def low_pass(kept, grad):
    return (grad,)

def back_keep(v):
    return (v, None)

def back_low(kept, grad):
    return (lower_precision(grad),)
lower_precision.defvjp(low_keep, low_pass)
lower_precision_back.defvjp(back_keep, back_low)

def rms_scale(stream, gain_vector):
    return stream * lax.rsqrt(lax.optimization_barrier(jnp.mean(stream * stream, axis=-1, keepdims=True)) + NORM_EPS) * gain_vector

def apply_rotation(value_rows, head_count):
    place_count = value_rows.shape[-2]
    half_width = HEAD_SIZE // 2
    inverse = ROPE_BASE ** (-(2.0 * jnp.arange(half_width, dtype=jnp.float32)) / HEAD_SIZE)
    angles = jnp.arange(place_count, dtype=jnp.float32)[:, None] * inverse[None, :]
    cos_table = jnp.cos(angles)[:, None, :]
    sin_table = jnp.sin(angles)[:, None, :]
    shaped = value_rows.reshape(value_rows.shape[:-1] + (head_count, HEAD_SIZE))
    first_half = shaped[..., :half_width]
    second_half = shaped[..., half_width:]
    turned = jnp.concatenate([first_half * cos_table - second_half * sin_table, second_half * cos_table + first_half * sin_table], axis=-1)
    return turned.reshape(value_rows.shape)

def attend_slot(packed):
    query_rows, rotated_keys, value_rows, length = packed
    place_count = query_rows.shape[0]
    heads_of_query = query_rows.reshape(place_count, KEY_VALUE_HEADS, QUERY_HEADS // KEY_VALUE_HEADS, HEAD_SIZE)
    heads_of_key = rotated_keys.reshape(place_count, KEY_VALUE_HEADS, HEAD_SIZE)
    heads_of_value = value_rows.reshape(place_count, KEY_VALUE_HEADS, HEAD_SIZE)
    scores = lower_precision_back(jnp.einsum('qngd,knd->ngqk', heads_of_query, heads_of_key, precision=FULL_PRECISION))
    places = jnp.arange(place_count, dtype=jnp.int32)
    allowed = (places[None, :] <= places[:, None]) & (places[None, :] < length)
    logits = jnp.where(allowed, scores * HEAD_SIZE ** (-0.5), -1e+30)
    highest = lax.optimization_barrier(jnp.max(logits, axis=-1, keepdims=True))
    expo_terms = jnp.exp(logits - highest)
    probability = lower_precision(expo_terms / lax.optimization_barrier(jnp.sum(expo_terms, axis=-1, keepdims=True)))
    mixed_heads = jnp.einsum('ngqk,knd->qngd', probability, heads_of_value, precision=FULL_PRECISION)
    return mixed_heads.reshape(place_count, QUERY_HEADS * HEAD_SIZE)

def apply_projection(value_rows, weight_matrix):
    return jnp.einsum('avi,iq->avq', value_rows, weight_matrix, precision=FULL_PRECISION)

def block_forward(block_rows, group_lengths, attention_gain, query_weight, key_matrix, value_matrix, output_weight, mlp_gain, gate_weight, up_weight, down_weight):
    places = jnp.arange(block_rows.shape[1], dtype=jnp.int32)
    is_valid = (places[None, :] < group_lengths[:, None])[..., None]
    stream = block_rows
    totals = []
    for repeat in range(2):
        normalized = lower_precision(rms_scale(stream, attention_gain))
        query_rows = lower_precision(apply_rotation(lower_precision_back(apply_projection(normalized, query_weight)), QUERY_HEADS))
        rotated_keys = lower_precision(apply_rotation(lower_precision_back(apply_projection(normalized, key_matrix)), KEY_VALUE_HEADS))
        value_rows = lower_precision(lower_precision_back(apply_projection(normalized, value_matrix)))
        attended = lax.map(jax.checkpoint(attend_slot), (query_rows, rotated_keys, value_rows, group_lengths))
        attended = lower_precision(lower_precision_back(attended))
        attn_branch = lower_precision_back(apply_projection(attended, output_weight))
        middle = stream + attn_branch
        normed_mlp = lower_precision(rms_scale(middle, mlp_gain))
        gate_value = lower_precision_back(apply_projection(normed_mlp, gate_weight))
        upward = lower_precision_back(apply_projection(normed_mlp, up_weight))
        hidden = lower_precision(jax.nn.silu(gate_value) * upward)
        mlp_branch = lower_precision_back(apply_projection(hidden, down_weight))
        for branch in (stream, attn_branch, mlp_branch):
            totals.append(jnp.sum(jnp.where(is_valid, branch * branch, 0.0)))
        stream = middle + mlp_branch
    return (jnp.where(is_valid, stream, 0.0), jnp.stack(totals))

def reference(block_input, lengths, attention_gain, query_weight, key_matrix, value_matrix, output_weight, mlp_gain, gate_weight, up_weight, down_weight, cotangent):
    group_size = math.gcd(SLOTS, max(1, 4096 // SLOT_PLACES))
    group_count = SLOTS // group_size
    weights = tuple((weight_matrix.astype(jnp.float32) for weight_matrix in (attention_gain, query_weight, key_matrix, value_matrix, output_weight, mlp_gain, gate_weight, up_weight, down_weight)))
    input_rows = block_input.astype(jnp.float32).reshape(group_count, group_size, SLOT_PLACES, MODEL_WIDTH)
    cotangent_rows = cotangent.astype(jnp.float32).reshape(group_count, group_size, SLOT_PLACES, MODEL_WIDTH)
    length_rows = lengths.reshape(group_count, group_size)

    def one_group(running, packed):
        grad_sums, stat_sums = running
        group_rows, group_lengths, group_seed = packed

        def forward(group_in, *params):
            return block_forward(group_in, group_lengths, *params)
        output, pullback, totals = jax.vjp(forward, group_rows, *weights, has_aux=True)
        gradients = pullback(group_seed)
        fresh_sums = tuple((total_now + fresh for total_now, fresh in zip(grad_sums, gradients[1:])))
        return ((fresh_sums, stat_sums + totals), (output.astype(jnp.bfloat16), gradients[0]))
    zero_sums = tuple((jnp.zeros(weight_matrix.shape, jnp.float32) for weight_matrix in weights))
    (grad_sums, stat_sums), (outputs, input_grads) = lax.scan(one_group, (zero_sums, jnp.zeros((6,), jnp.float32)), (input_rows, length_rows, cotangent_rows))
    token_count = jnp.sum(lengths).astype(jnp.float32)
    stream_rms = jnp.sqrt(stat_sums.reshape(2, 3) / (token_count * MODEL_WIDTH))
    return (outputs.reshape(SLOTS, SLOT_PLACES, MODEL_WIDTH), input_grads.reshape(SLOTS, SLOT_PLACES, MODEL_WIDTH), grad_sums[0], grad_sums[1], grad_sums[2], grad_sums[3], grad_sums[4], grad_sums[5], grad_sums[6], grad_sums[7], grad_sums[8], stream_rms)
```

```python
import functools
import jax
import jax.numpy as jnp
import numpy as np
from jax import lax
from jax.experimental import pallas as pl
from jax.experimental.pallas import tpu as pltpu
from jax.sharding import PartitionSpec as P

D = 576
NQ = 9
NK = 3
GROUP = NQ // NK
H = 64
HALF = H // 2
FF = 1536
T = 512
NF = 8
QB = D // NF
KB = NK * H // NF
FB = FF // NF
OB = 80
EPS = 1e-05
ROPE_BASE = 10000.0
SCALE = H ** (-0.5)
NEG = -1e30
BLK = 256
VMEM_LIMIT = 63 * 2**20
BF = jnp.bfloat16
F32 = jnp.float32


def dot(a, b, ca, cb):
    return lax.dot_general(a, b, (((ca,), (cb,)), ((), ())), preferred_element_type=F32)


def rope_tables():
    inverse = ROPE_BASE ** (-(2.0 * np.arange(HALF, dtype=np.float64)) / H)
    angles = inverse[:, None] * np.arange(T, dtype=np.float64)[None, :]
    return np.cos(angles).astype(np.float32), np.sin(angles).astype(np.float32)


def parts_of(row):
    hi = row.astype(BF).astype(F32)
    rest = row - hi
    mid = rest.astype(BF).astype(F32)
    return [hi, mid, rest - mid]


def lane_tiles():
    return [slice(128 * i, 128 * i + 128) for i in range(T // 128)]


class Work:
    def __init__(self, order, refs):
        self.order = order
        self.__dict__.update(refs)

    def start(self):
        count = self.length[0]
        place = lax.broadcasted_iota(jnp.int32, (8, T), 1)
        valid = (place < count).astype(F32)
        self.valid[...] = valid
        for ts in lane_tiles():
            self.S[0, :, ts] = self.x[ts, :].astype(F32).T
            self.G[:, ts] = self.ct[ts, :].astype(F32).T * valid[0:1, ts]
        self.gacc[...] = jnp.zeros_like(self.gacc)
        self.QA[:, :, H:, :] = jnp.zeros((2, NQ, H, T), BF)
        self.DOA[:, H:, :] = jnp.zeros((NQ, H, T), BF)

    def norm(self, src, r, gain, dst, rho_ref, row):
        for ts in lane_tiles():
            v = src[r, :, ts]
            total = jnp.sum(v * v, axis=0, keepdims=True)
            if row is not None:
                self.stat[row : row + 1, ts] = total
            rho = lax.rsqrt(total * (1.0 / D) + EPS)
            rho_ref[r, 0:1, ts] = rho
            dst[r, :, ts] = (v * rho * gain[...]).astype(BF)

    def natural_rows(self, ref, base, width, first, count):
        pieces = []
        row = first
        while row < first + count:
            f, i = row // width, row % width
            n = min(width - i, first + count - row)
            at = 128 * self.order.index(f) + base + i
            pieces.append(ref[at : at + n, :])
            row += n
        return pieces[0] if len(pieces) == 1 else jnp.concatenate(pieces, axis=0)

    def project(self, r):
        self.norm(self.S, r, self.ga, self.XA, self.rhoA, 3 * r)
        for c in range(2):
            cs = slice(512 * c, 512 * c + 512)
            self.Y[cs, :] = dot(self.WA[:, cs], self.XA[r], 0, 0)
        cos, sin = self.cos[...], self.sin[...]
        one = jnp.ones((1, T), F32)
        place = lax.broadcasted_iota(jnp.int32, (1, T), 1)
        bias = jnp.where(place < self.length[0], 0.0, NEG)
        for h in range(NQ + NK):
            base, width, at = (0, QB, h) if h < NQ else (QB, KB, h - NQ)
            a = self.natural_rows(self.Y, base, width, H * at, HALF)
            b = self.natural_rows(self.Y, base, width, H * at + HALF, HALF)
            first, second = a * cos - b * sin, b * cos + a * sin
            if h < NQ:
                self.QA[r, h, 0:HALF, :] = (first * SCALE).astype(BF)
                self.QA[r, h, HALF:H, :] = (second * SCALE).astype(BF)
                self.QA[r, h, H : H + 16, :] = jnp.concatenate([one, jnp.zeros((15, T), F32)], axis=0).astype(BF)
            else:
                g = h - NQ
                key = jnp.concatenate([first, second], axis=0)
                self.KT[r, g] = key.astype(BF)
                v = jnp.concatenate(
                    [
                        self.natural_rows(self.Y, QB + KB, KB, H * g, HALF),
                        self.natural_rows(self.Y, QB + KB, KB, H * g + HALF, HALF),
                    ],
                    axis=0,
                )
                self.VT[g] = v.astype(BF)
                ones3 = jnp.ones((3, T), F32)
                tail = jnp.zeros((H - 4, T), F32)
                ktall = jnp.concatenate([key, bias, ones3, tail], axis=0)
                vtall = jnp.concatenate([v, jnp.zeros((1, T), F32), ones3, tail], axis=0)
                for ts in lane_tiles():
                    self.KTOK[r, g, ts, :] = ktall[:, ts].T.astype(BF)
                    self.VTOK[r, g, ts, :] = vtall[:, ts].T.astype(BF)

    def diagonal(self):
        key = lax.broadcasted_iota(jnp.int32, (BLK, BLK), 0)
        query = lax.broadcasted_iota(jnp.int32, (BLK, BLK), 1)
        return key <= query

    def attend(self, r):
        low, high = slice(0, BLK), slice(BLK, T)

        def head(h, carry):
            g = h // GROUP
            allowed = self.diagonal()
            at = pl.ds(pl.multiple_of(h * H, H), H)
            s = dot(self.KTOK[r, g, low, :], self.QA[r, h, :, low], 1, 0)
            s = jnp.where(allowed, s, NEG)
            top = jnp.max(s, axis=0, keepdims=True)
            p = jnp.exp(s - top)
            total = jnp.sum(p, axis=0, keepdims=True)
            o = dot(self.VT[g, :, low], p.astype(BF), 1, 0)
            self.AT[r, at, low] = (o * (1.0 / total)).astype(BF)
            lse0 = top + jnp.log(total)
            s0 = dot(self.KTOK[r, g, low, :], self.QA[r, h, :, high], 1, 0)
            s1 = dot(self.KTOK[r, g, high, :], self.QA[r, h, :, high], 1, 0)
            s1 = jnp.where(allowed, s1, NEG)
            top = jnp.maximum(jnp.max(s0, axis=0, keepdims=True), jnp.max(s1, axis=0, keepdims=True))
            p0 = jnp.exp(s0 - top)
            p1 = jnp.exp(s1 - top)
            total = jnp.sum(p0, axis=0, keepdims=True) + jnp.sum(p1, axis=0, keepdims=True)
            o = dot(self.VT[g, :, low], p0.astype(BF), 1, 0) + dot(self.VT[g, :, high], p1.astype(BF), 1, 0)
            self.AT[r, at, high] = (o * (1.0 / total)).astype(BF)
            lse1 = top + jnp.log(total)
            lse = jnp.concatenate([lse0, lse1], axis=1)
            rows = [jnp.ones((1, T), F32)] + parts_of(-lse) + [jnp.zeros((12, T), F32)]
            self.QA[r, h, H : H + 16, :] = jnp.concatenate(rows, axis=0).astype(BF)
            return carry

        lax.fori_loop(0, NQ, head, 0)

    def out_project(self, r):
        for c in range(2):
            cs = slice(512 * c, 512 * c + 512)
            self.Y[cs, :] = dot(self.WO[:, cs], self.AT[r], 0, 0)
        squares = jnp.zeros((8, T), F32)
        for b in range(NF):
            f = self.order[b]
            y = self.Y[128 * b : 128 * b + QB, :]
            rows = slice(QB * f, QB * f + QB)
            self.M[r, rows, :] = self.S[r, rows, :] + y
            for i in range(QB // 8):
                squares = squares + y[8 * i : 8 * i + 8] * y[8 * i : 8 * i + 8]
        self.stat[3 * r + 1 : 3 * r + 2, :] = jnp.sum(squares, axis=0, keepdims=True)

    def mlp(self, r):
        self.norm(self.M, r, self.gm, self.XM, self.rhoM, None)

        def block(b, carry):
            f = 2 * lax.rem(b, 4) + b // 4 if self.order[1] == 2 else b
            cols = pl.ds(pl.multiple_of(2 * FB * b, 128), 2 * FB)
            gu = dot(self.WGU[:, cols], self.XM[r], 0, 0)
            gate, up = gu[:FB], gu[FB:]
            rows = pl.ds(pl.multiple_of(FB * f, 64), FB)
            self.GATE[r, rows, :] = gate.astype(BF)
            self.UP[r, rows, :] = up.astype(BF)
            self.HID[r, rows, :] = (gate * jax.nn.sigmoid(gate) * up).astype(BF)
            return carry

        lax.fori_loop(0, NF, block, 0)
        self.Y[0 : OB * NF, :] = dot(self.WDT[...], self.HID[r], 1, 0)
        squares = jnp.zeros((8, T), F32)
        for b in range(NF):
            f = self.order[b]
            y = self.Y[OB * b : OB * b + QB, :]
            rows = slice(QB * f, QB * f + QB)
            after = self.M[r, rows, :] + y
            if r == 0:
                self.S[1, rows, :] = after
            else:
                self.E[rows, :] = after
            for i in range(QB // 8):
                squares = squares + y[8 * i : 8 * i + 8] * y[8 * i : 8 * i + 8]
        self.stat[3 * r + 2 : 3 * r + 3, :] = jnp.sum(squares, axis=0, keepdims=True)

    def write_output(self):
        valid = self.valid[0:1, :]
        for ts in lane_tiles():
            v = jnp.where(valid[:, ts] > 0.0, self.E[:, ts], 0.0)
            self.out[ts, :] = v.T.astype(BF)

    def pack_grad(self, dst, width):
        for b in range(NF):
            f = self.order[b]
            v = self.G[QB * f : QB * f + QB, :]
            v = jnp.concatenate([v, jnp.zeros((width - QB, T), F32)], axis=0)
            dst[width * b : width * b + width, :] = v.astype(BF)

    def add_term(self, dst, index, value, r):
        if r == 0:
            value = value + dst[index].astype(F32)
        dst[index] = value.astype(dst.dtype)

    def norm_back(self, src, r, rho_ref, gain, slot):
        for ts in lane_tiles():
            e, v, rho = self.E[:, ts], src[r, :, ts], rho_ref[r, 0:1, ts]
            u = e * gain[...]
            mean = jnp.sum(u * v, axis=0, keepdims=True) * (1.0 / D)
            self.gacc[slot] += e * (v * rho)
            self.G[:, ts] = self.G[:, ts] + rho * (u - v * (rho * rho * mean))

    def mlp_back(self, r, links=None):
        self.pack_grad(self.GLD, OB)
        for c in range(2):
            cs = slice(768 * c, 768 * c + 768)
            self.add_term(self.DD, (slice(None), cs), dot(self.GLD[...], self.HID[r, cs, :], 1, 1), r)
        if links:
            links.sum_start("D")

        def block(z, carry):
            rows = pl.ds(pl.multiple_of(2 * FB * z, 128), 2 * FB)
            grad = dot(self.WDT[:, rows], self.GLD[...], 0, 0)
            gate = self.GATE[r, rows, :].astype(F32)
            up = self.UP[r, rows, :].astype(F32)
            sig = jax.nn.sigmoid(gate)
            dgate = grad * up * (sig * (1.0 + gate * (1.0 - sig)))
            dup = grad * (gate * sig)
            for k in range(2):
                b = z + 4 * k if self.order[1] == 2 else 2 * z + k
                self.DGU[pl.ds(pl.multiple_of(2 * FB * b, 128), FB), :] = dgate[FB * k : FB * k + FB].astype(BF)
                self.DGU[pl.ds(pl.multiple_of(2 * FB * b + FB, 64), FB), :] = dup[FB * k : FB * k + FB].astype(BF)
            return carry

        lax.fori_loop(0, 4, block, 0)
        for c in range(4):
            cs = slice(768 * c, 768 * c + 768)
            self.add_term(self.DG, (slice(None), cs), dot(self.XM[r], self.DGU[cs, :], 1, 1), r)
        if links:
            links.sum_start("G")
            links.sum_pair("D")
        self.E[...] = dot(self.WGU[...], self.DGU[...], 1, 0)
        self.norm_back(self.M, r, self.rhoM, self.gm, 1)

    def attend_back(self, r, links=None):
        self.pack_grad(self.GLO, 128)
        for c in range(2):
            cs = slice(512 * c, 512 * c + 512)
            self.add_term(self.DO, (slice(None), cs), dot(self.AT[r], self.GLO[cs, :], 1, 1), r)
        if links:
            links.sum_start("O")
            links.sum_pair("G")
            links.sum_cross("D")
        self.E[...] = dot(self.WO[...], self.GLO[...], 1, 0)
        for h in range(NQ):
            rows = slice(H * h, H * h + H)
            do = self.E[rows, :].astype(BF)
            self.DOA[h, 0:H, :] = do
            delta = jnp.sum(do.astype(F32) * self.AT[r, rows, :].astype(F32), axis=0, keepdims=True)
            rows = [jnp.zeros((1, T), F32)] + parts_of(-delta) + [jnp.zeros((12, T), F32)]
            self.DOA[h, H : H + 16, :] = jnp.concatenate(rows, axis=0).astype(BF)
        low, high = slice(0, BLK), slice(BLK, T)
        self.Y[D : D + 2 * NK * H, :] = jnp.zeros((2 * NK * H, T), F32)

        def head(h, carry):
            g = h // GROUP
            allowed = self.diagonal()
            at = pl.ds(pl.multiple_of(h * H, H), H)
            kat = pl.ds(pl.multiple_of(D + g * H, H), H)
            vat = pl.ds(pl.multiple_of(D + NK * H + g * H, H), H)
            q, do = self.QA[r, h], self.DOA[h]
            k0, k1 = self.KTOK[r, g, low, :], self.KTOK[r, g, high, :]
            v0, v1 = self.VTOK[r, g, low, :], self.VTOK[r, g, high, :]
            t0, t1 = self.KT[r, g, :, low], self.KT[r, g, :, high]

            p = jnp.where(allowed, jnp.exp(dot(k0, q[:, low], 1, 0)), 0.0)
            ds = (p * dot(v0, do[:, low], 1, 0)).astype(BF)
            p = p.astype(BF)
            self.Y[at, low] = dot(t0, ds, 1, 0) * SCALE
            dk0 = dot(q[0:H, low], ds, 1, 1)
            dv0 = dot(do[0:H, low], p, 1, 1)

            p = jnp.exp(dot(k0, q[:, high], 1, 0))
            ds = (p * dot(v0, do[:, high], 1, 0)).astype(BF)
            p = p.astype(BF)
            dq = dot(t0, ds, 1, 0)
            dk0 += dot(q[0:H, high], ds, 1, 1)
            dv0 += dot(do[0:H, high], p, 1, 1)

            p = jnp.where(allowed, jnp.exp(dot(k1, q[:, high], 1, 0)), 0.0)
            ds = (p * dot(v1, do[:, high], 1, 0)).astype(BF)
            p = p.astype(BF)
            self.Y[at, high] = (dq + dot(t1, ds, 1, 0)) * SCALE
            self.Y[kat, low] += dk0
            self.Y[vat, low] += dv0
            self.Y[kat, high] += dot(q[0:H, high], ds, 1, 1)
            self.Y[vat, high] += dot(do[0:H, high], p, 1, 1)
            return carry

        for g in range(NK):
            lax.fori_loop(GROUP * g, GROUP * g + GROUP, head, 0)
            if links and g == 0:
                links.sum_pair("O")
            if links and g == 1:
                links.sum_cross("G")
                links.sum_line("D")

    def project_back(self, r, links=None):
        cos, sin = self.cos[...], self.sin[...]
        for h in range(NQ + NK):
            first, second = slice(H * h, H * h + HALF), slice(H * h + HALF, H * h + H)
            a, b = self.Y[first, :], self.Y[second, :]
            self.Y[first, :] = a * cos + b * sin
            self.Y[second, :] = b * cos - a * sin
        for b in range(NF):
            f = self.order[b]
            rows = jnp.concatenate(
                [
                    self.Y[QB * f : QB * f + QB, :],
                    self.Y[D + KB * f : D + KB * f + KB, :],
                    self.Y[D + NK * H + KB * f : D + NK * H + KB * f + KB, :],
                    jnp.zeros((128 - QB - 2 * KB, T), F32),
                ],
                axis=0,
            )
            self.GLO[128 * b : 128 * b + 128, :] = rows.astype(BF)
        for c in range(2):
            cs = slice(512 * c, 512 * c + 512)
            self.add_term(self.DA, (slice(None), cs), dot(self.XA[r], self.GLO[cs, :], 1, 1), r)
        if links:
            links.sum_start("A")
            links.sum_cross("O")
            links.sum_line("G")
        self.E[...] = dot(self.WA[...], self.GLO[...], 1, 0)
        self.norm_back(self.S, r, self.rhoA, self.ga, 0)

    def write_grad(self):
        for ts in lane_tiles():
            self.gin[ts, :] = self.G[:, ts].T

    def small(self):
        valid = self.valid[0:1, :]
        rows = [jnp.sum(self.gacc[i].T, axis=0, keepdims=True) for i in range(2)]
        sums = jnp.sum(jnp.where(valid > 0.0, self.stat[0:6, :], 0.0), axis=1, keepdims=True)
        count = jnp.sum(valid, axis=1, keepdims=True)
        lane = lax.broadcasted_iota(jnp.int32, (6, D), 1)
        return jnp.concatenate(rows + [jnp.where(lane < 128, sums, count)], axis=0)


SCRATCH = dict(
    S=((2, D, T), F32), G=((D, T), F32), E=((D, T), F32), Y=((1024, T), F32),
    XA=((2, D, T), BF), XM=((2, D, T), BF), rhoA=((2, 8, T), F32), rhoM=((2, 8, T), F32),
    QA=((2, NQ, 128, T), BF), KT=((2, NK, H, T), BF), VT=((NK, H, T), BF),
    KTOK=((2, NK, T, 128), BF), VTOK=((2, NK, T, 128), BF), AT=((2, D, T), BF), M=((2, D, T), F32),
    GATE=((2, FF, T), BF), UP=((2, FF, T), BF), HID=((2, FF, T), BF),
    GLD=((OB * NF, T), BF), GLO=((1024, T), BF), DGU=((2 * FF, T), BF), DOA=((NQ, 128, T), BF),
    stat=((8, T), F32), valid=((8, T), F32), gacc=((2, D, 128), F32),
)
WEIGHTS = dict(WA=((D, 1024), BF), WO=((D, 1024), BF), WGU=((D, 2 * FF), BF), WDT=((OB * NF, FF), BF))
GRADS = dict(DA=((D, 1024), BF), DO=((D, 1024), BF), DG=((D, 2 * FF), BF), DD=((OB * NF, FF), BF))

def compute_kernel(order, names, *refs):
    w = Work(order, dict(zip(names, refs)))
    w.start()
    for r in range(2):
        w.project(r)
        w.attend(r)
        w.out_project(r)
        w.mlp(r)
    w.write_output()
    for r in (1, 0):
        w.mlp_back(r)
        w.attend_back(r)
        w.project_back(r)
    w.write_grad()
    w.tiny[...] = w.small()


def local_compute(order, x, length, ga, gm, ct, packed):
    cos, sin = rope_tables()
    ins = dict(length=length, x=x, ct=ct, ga=ga[:, None], gm=gm[:, None], cos=jnp.asarray(cos), sin=jnp.asarray(sin), **packed)
    outs = dict(out=((T, D), BF), gin=((T, D), F32), tiny=((8, D), F32), **GRADS)
    names = list(ins) + list(outs) + list(SCRATCH)
    vmem = pl.BlockSpec(memory_space=pltpu.VMEM)
    results = pl.pallas_call(
        functools.partial(compute_kernel, order, names),
        out_shape=[jax.ShapeDtypeStruct(*s) for s in outs.values()],
        in_specs=[pl.BlockSpec(memory_space=pltpu.SMEM)] + [vmem] * (len(ins) - 1),
        out_specs=[vmem] * len(outs),
        scratch_shapes=[pltpu.VMEM(*s) for s in SCRATCH.values()],
        compiler_params=pltpu.CompilerParams(vmem_limit_bytes=VMEM_LIMIT),
    )(*ins.values())
    return dict(zip(outs, results))


def pack(order, q, k, v, o, g, u, d):
    def cols(w, width):
        return w.reshape(w.shape[0], NF, width)[:, np.array(order)]
    zero = jnp.zeros((D, NF, 128 - QB - 2 * KB), BF)
    wa = jnp.concatenate([cols(q, QB), cols(k, KB), cols(v, KB), zero], axis=2).reshape(D, 1024)
    wo = jnp.pad(cols(o, QB), ((0, 0), (0, 0), (0, 128 - QB))).reshape(D, 1024)
    wgu = jnp.concatenate([cols(g, FB), cols(u, FB)], axis=2).reshape(D, 2 * FF)
    wd = jnp.pad(d.T.reshape(NF, QB, FF)[np.array(order)], ((0, 0), (0, OB - QB), (0, 0))).reshape(OB * NF, FF)
    return dict(WA=wa, WO=wo, WGU=wgu, WDT=wd)


def unpack(order, r):
    back = np.argsort(np.array(order))
    a = r["DA"].astype(F32).reshape(D, NF, 128)[:, back]
    o = r["DO"].astype(F32).reshape(D, NF, 128)[:, back, :QB].reshape(D, D)
    g = r["DG"].astype(F32).reshape(D, NF, 2 * FB)[:, back]
    d = r["DD"].astype(F32).reshape(NF, OB, FF)[back, :QB].reshape(D, FF).T
    return (
        a[:, :, :QB].reshape(D, D), a[:, :, QB : QB + KB].reshape(D, NK * H), a[:, :, QB + KB : QB + 2 * KB].reshape(D, NK * H),
        o, g[:, :, :FB].reshape(D, FF), g[:, :, FB:].reshape(D, FF), d,
    )


PIECES = ("A", "O", "G", "D")
WEIGHT_OF = dict(A="WA", O="WO", G="WGU", D="WDT")
GRAD_OF = dict(A="DA", O="DO", G="DG", D="DD")
WIDTH_OF = dict(A=128, O=128, G=2 * FB)
CUT_OF = dict(A=((0, 80), (80, 64)), O=((0, 64), (64, 80)), G=((0, 64), (64, 80)), D=((0, 256), (256, 128)))
ROWS = D // 4
LANES = FF // 4
MESH = pl.DeviceIdType.MESH


def region(ref, piece, dp, y, z, count, part=None):
    first, size = (0, None) if part is None else CUT_OF[piece][part]
    line = 4 * y + z
    if piece == "D":
        size = LANES if size is None else size
        rows = pl.ds(pl.multiple_of(OB * line, 16), OB * count)
        return ref.at[rows, pl.ds(pl.multiple_of(LANES * dp + first, 128), size)]
    size = ROWS if size is None else size
    width = WIDTH_OF[piece]
    rows = pl.ds(pl.multiple_of(ROWS * dp + first, 16), size)
    return ref.at[rows, pl.ds(pl.multiple_of(width * line, 128), width * count)]


def shape_of(piece, count, part=None):
    size = None if part is None else CUT_OF[piece][part][1]
    if piece == "D":
        return (OB * count, size or LANES)
    return (size or ROWS, WIDTH_OF[piece] * count)


class Links:
    def __init__(self, refs):
        self.__dict__.update(refs)
        self.dp, f = lax.axis_index("dp"), lax.axis_index("fsdp")
        self.x, self.c = self.dp // 2, lax.rem(self.dp, 2)
        self.z, self.y = f // 2, lax.rem(f, 2)
        self.far = 2 * (1 - self.x) + self.c
        self.other = 2 * self.x + 1 - self.c
        self.sib = (self.other, f)
        self.xn = (self.far, f)
        self.yn = (self.dp, 2 * self.z + 1 - self.y)
        self.peer = [None] + [lax.rem(self.z + k, 4) for k in (1, 2, 3)]
        self.zn = [None] + [(self.dp, 2 * self.peer[k] + self.y) for k in (1, 2, 3)]
        self.copies = {}
        self.used = 0

    def barrier(self):
        sem = pltpu.get_barrier_semaphore()
        partners = [self.sib, self.xn, self.yn] + self.zn[1:]
        for device in partners:
            pl.semaphore_signal(sem, inc=1, device_id=device, device_id_type=MESH)
        pl.semaphore_wait(sem, len(partners))

    def send(self, name, src, dst, device):
        copy = pltpu.make_async_remote_copy(
            src_ref=src,
            dst_ref=dst,
            send_sem=self.sent.at[self.used],
            recv_sem=self.came.at[self.used],
            device_id=device,
            device_id_type=MESH,
        )
        self.used += 1
        copy.start()
        self.copies[name] = copy

    def arrived(self, *names):
        for name in names:
            self.copies[name].wait_recv()

    def finish(self):
        for copy in self.copies.values():
            copy.wait_send()


    def own(self, p, y=None, z=0, count=4, part=None, dp=None):
        ref = getattr(self, WEIGHT_OF[p])
        return region(ref, p, self.dp if dp is None else dp, self.y if y is None else y, z, count, part)

    def spread(self, tag, p, part, device, dp=None, y=None, z=0, count=4):
        block = self.own(p, y, z, count, part, dp)
        self.send(("w", p, tag), block, block, device)

    def gather_start(self, p):
        for k in (1, 2, 3):
            self.spread(f"z{k}", p, None, self.zn[k], z=self.z, count=1)

    def gather_line(self, p):
        self.arrived(*[("w", p, f"z{k}") for k in (1, 2, 3)])
        self.spread("x", p, None, self.xn)
        self.spread("y", p, None, self.yn)
        self.spread("s", p, None, self.sib)

    def gather_cross(self, p):
        self.arrived(("w", p, "x"))
        self.spread("xy", p, 0, self.yn, dp=self.far)
        self.spread("sx", p, None, self.sib, dp=self.far)
        self.arrived(("w", p, "y"))
        self.spread("yx", p, 1, self.xn, y=1 - self.y)
        self.spread("sy", p, None, self.sib, y=1 - self.y)

    def gather_rest(self, p):
        self.arrived(("w", p, "xy"))
        self.spread("sxy", p, 0, self.sib, dp=self.far, y=1 - self.y)
        self.arrived(("w", p, "yx"))
        self.spread("syx", p, 1, self.sib, dp=self.far, y=1 - self.y)

    def gather_end(self, p):
        self.arrived(*[("w", p, tag) for tag in ("s", "sx", "sy", "sxy", "syx")])


    def term(self, p, dp, y, z=0, count=4, part=None):
        return region(getattr(self, GRAD_OF[p]), p, dp, y, z, count, part)

    def add(self, p, dp, y, part, came):
        at = self.term(p, dp, y, 0, 4, part)
        at[...] = at[...] + came[...]

    def sum_start(self, p):
        room = getattr(self, "one" + p)
        for i in range(2):
            for y in range(2):
                dp = 2 * i + 1 - self.c
                self.send(("g", p, "s", i, y), self.term(p, dp, y), room.at[i, y], self.sib)

    def sum_pair(self, p):
        room = getattr(self, "one" + p)
        for i in range(2):
            for y in range(2):
                self.arrived(("g", p, "s", i, y))
                self.add(p, 2 * i + self.c, y, None, room.at[i, y])
        ups, across = getattr(self, "twoy" + p), getattr(self, "twox" + p)
        for i, dp in enumerate((self.dp, self.far)):
            self.send(("g", p, "y", i), self.term(p, dp, 1 - self.y, part=0), ups.at[i], self.yn)
        for j, y in enumerate((self.y, 1 - self.y)):
            self.send(("g", p, "x", j), self.term(p, self.far, y, part=1), across.at[j], self.xn)

    def sum_cross(self, p):
        ups, across = getattr(self, "twoy" + p), getattr(self, "twox" + p)
        for i in (1, 0):
            self.arrived(("g", p, "y", i))
            self.add(p, (self.dp, self.far)[i], self.y, 0, ups.at[i])
            if i == 1:
                self.send(("g", p, "yx"), self.term(p, self.far, self.y, part=0), getattr(self, "threex" + p), self.xn)
        for j in (1, 0):
            self.arrived(("g", p, "x", j))
            self.add(p, self.dp, (self.y, 1 - self.y)[j], 1, across.at[j])
            if j == 1:
                self.send(("g", p, "xy"), self.term(p, self.dp, 1 - self.y, part=1), getattr(self, "threey" + p), self.yn)

    def sum_line(self, p):
        self.arrived(("g", p, "yx"))
        self.add(p, self.dp, self.y, 0, getattr(self, "threex" + p))
        self.arrived(("g", p, "xy"))
        self.add(p, self.dp, self.y, 1, getattr(self, "threey" + p))
        for k in (1, 2, 3):
            src = self.term(p, self.dp, self.y, self.peer[k], 1)
            self.send(("g", p, "z", k), src, getattr(self, "four" + p).at[k - 1], self.zn[k])

    def sum_end(self, p):
        total = self.term(p, self.dp, self.y, self.z, 1)[...].astype(F32)
        for k in (1, 2, 3):
            self.arrived(("g", p, "z", k))
            total = total + getattr(self, "four" + p)[k - 1].astype(F32)
        return total


    def tiny_step(self, step):
        if step > 0:
            self.arrived(("t", step - 1))
            self.tinies[step] = self.tinies[step - 1] + self.smallin[step - 1]
        if step < 3:
            self.send(("t", step), self.tinies.at[step], self.smallin.at[step], (self.sib, self.xn, self.yn)[step])
        else:
            for k in (1, 2, 3):
                self.send(("t", step, k), self.tinies.at[3], self.smallz.at[k], self.zn[k])

    def tiny_end(self):
        self.smallz[0] = self.tinies[3]
        for k in (1, 2, 3):
            self.arrived(("t", 3, k))
        total = None
        for z in range(4):
            k = lax.rem(self.z - z + 4, 4)
            term = self.smallz[k]
            total = term if total is None else total + term
        return total


def rooms():
    shapes = {}
    for p in PIECES:
        shapes["one" + p] = ((2, 2) + shape_of(p, 4), BF)
        shapes["twoy" + p] = ((2,) + shape_of(p, 4, 0), BF)
        shapes["twox" + p] = ((2,) + shape_of(p, 4, 1), BF)
        shapes["threex" + p] = (shape_of(p, 4, 0), BF)
        shapes["threey" + p] = (shape_of(p, 4, 1), BF)
        shapes["four" + p] = ((3,) + shape_of(p, 1), BF)
    shapes["tinies"] = ((4, 8, D), F32)
    shapes["smallin"] = ((3, 8, D), F32)
    shapes["smallz"] = ((4, 8, D), F32)
    return shapes


COPIES = 4 * 12 + 4 * 13 + 6


def pack_own(links, refs):
    rows = lambda *names: [refs[n][...].astype(F32) for n in names]
    zero = lambda n: jnp.zeros((ROWS, n), F32)
    links.own("A", z=links.z, count=1)[...] = jnp.concatenate(
        rows("q", "k", "v") + [zero(128 - QB - 2 * KB)], axis=1
    ).astype(BF)
    links.own("O", z=links.z, count=1)[...] = jnp.concatenate(rows("o") + [zero(128 - QB)], axis=1).astype(BF)
    links.own("G", z=links.z, count=1)[...] = jnp.concatenate(rows("g", "u"), axis=1).astype(BF)
    (down,) = rows("d")
    links.own("D", z=links.z, count=1)[...] = jnp.concatenate(
        [down.T, jnp.zeros((OB - QB, LANES), F32)], axis=0
    ).astype(BF)


def whole_kernel(order, names, *args):
    refs = dict(zip(names, args))
    w, links = Work(order, refs), Links(refs)
    links.barrier()
    pack_own(links, refs)
    for p in PIECES:
        links.gather_start(p)
    w.start()
    links.gather_line("A")
    links.gather_line("O")
    links.gather_cross("A")
    links.gather_line("G")
    links.gather_line("D")
    links.gather_cross("O")
    links.gather_rest("A")
    links.gather_end("A")
    w.project(0)
    links.gather_cross("G")
    links.gather_rest("O")
    w.attend(0)
    links.gather_end("O")
    w.out_project(0)
    links.gather_cross("D")
    links.gather_rest("G")
    links.gather_end("G")
    links.gather_rest("D")
    links.gather_end("D")
    w.mlp(0)
    w.project(1)
    w.attend(1)
    w.out_project(1)
    w.mlp(1)
    w.write_output()
    w.mlp_back(1)
    w.attend_back(1)
    w.project_back(1)
    w.mlp_back(0, links)
    w.attend_back(0, links)
    w.project_back(0, links)
    links.tinies[0] = w.small()
    links.tiny_step(0)
    links.sum_pair("A")
    links.sum_line("O")
    links.tiny_step(1)
    links.sum_cross("A")
    links.tiny_step(2)
    w.write_grad()
    total = links.sum_end("D")
    refs["gd"][...] = total[:QB, :].T
    total = links.sum_end("G")
    refs["gg"][...] = total[:, :FB]
    refs["gu"][...] = total[:, FB:]
    links.sum_line("A")
    links.tiny_step(3)
    total = links.sum_end("O")
    refs["go"][...] = total[:, :QB]
    total = links.sum_end("A")
    refs["gq"][...] = total[:, :QB]
    refs["gk"][...] = total[:, QB : QB + KB]
    refs["gv"][...] = total[:, QB + KB : QB + 2 * KB]
    total = links.tiny_end()
    refs["gga"][...] = total[0:1, :]
    refs["ggm"][...] = total[1:2, :]
    lane = lax.broadcasted_iota(jnp.int32, (1, 3), 1)
    for r in range(2):
        first, second, third = [total[2 + 3 * r + i : 3 + 3 * r + i, 0:3] for i in range(3)]
        sums = jnp.where(lane == 0, first, jnp.where(lane == 1, second, third))
        refs["rms"][r : r + 1, :] = jnp.sqrt(sums / (total[2:3, 128:131] * D))
    links.finish()


def whole(x, length, ga, q, k, v, o, gm, g, u, d, ct):
    order = [2 * (b % 4) + b // 4 for b in range(NF)]
    cos, sin = rope_tables()
    ins = dict(
        length=length, x=x[0], ct=ct[0], ga=ga[:, None], gm=gm[:, None], cos=jnp.asarray(cos), sin=jnp.asarray(sin),
        q=q, k=k, v=v, o=o, g=g, u=u, d=d,
    )
    outs = dict(
        out=((T, D), BF), gin=((T, D), F32), gga=((1, D), F32), gq=(q.shape, F32), gk=(k.shape, F32), gv=(v.shape, F32),
        go=(o.shape, F32), ggm=((1, D), F32), gg=(g.shape, F32), gu=(u.shape, F32), gd=(d.shape, F32), rms=((2, 3), F32),
    )
    scratch = dict(SCRATCH, **WEIGHTS, **GRADS, **rooms())
    names = list(ins) + list(outs) + list(scratch) + ["sent", "came"]
    vmem = pl.BlockSpec(memory_space=pltpu.VMEM)
    r = pl.pallas_call(
        functools.partial(whole_kernel, order, names),
        out_shape=[jax.ShapeDtypeStruct(*s) for s in outs.values()],
        in_specs=[pl.BlockSpec(memory_space=pltpu.SMEM)] + [vmem] * (len(ins) - 1),
        out_specs=[vmem] * len(outs),
        scratch_shapes=[pltpu.VMEM(*s) for s in scratch.values()]
        + [pltpu.SemaphoreType.DMA((COPIES,)), pltpu.SemaphoreType.DMA((COPIES,))],
        compiler_params=pltpu.CompilerParams(
            vmem_limit_bytes=VMEM_LIMIT, collective_id=0, has_side_effects=True
        ),
    )(*ins.values())
    r = dict(zip(outs, r))
    return (
        r["out"][None], r["gin"][None], r["gga"][0], r["gq"], r["gk"], r["gv"], r["go"], r["ggm"][0], r["gg"], r["gu"],
        r["gd"], r["rms"],
    )


def by_collectives(x, length, ga, q, k, v, o, gm, g, u, d, ct):
    order = list(range(NF))
    full = [lax.all_gather(lax.all_gather(w, "fsdp", axis=1, tiled=True), "dp", axis=0, tiled=True) for w in (q, k, v, o, g, u, d)]
    packed = pack(order, *full)
    results = [local_compute(order, x[i], length[i : i + 1], ga, gm, ct[i], packed) for i in range(x.shape[0])]
    out = jnp.stack([r["out"] for r in results])
    gin = jnp.stack([r["gin"] for r in results])
    tiny = lax.psum(sum(r["tiny"] for r in results), ("dp", "fsdp"))
    terms = [unpack(order, r) for r in results]
    grads = [
        lax.psum_scatter(
            lax.psum_scatter(sum(t), "dp", scatter_dimension=0, tiled=True), "fsdp", scatter_dimension=1, tiled=True
        )
        for t in zip(*terms)
    ]
    rms = jnp.sqrt(tiny[2:8, 0].reshape(2, 3) / (tiny[2, 128] * D))
    gq, gk, gv, go, gg, gu, gd = grads
    return out, gin, tiny[0], gq, gk, gv, go, tiny[1], gg, gu, gd, rms


def solution(mesh):
    blocks = P("dp", "fsdp")
    slots = P(("dp", "fsdp"), None, None)
    in_specs = (slots, P(("dp", "fsdp")), P(), blocks, blocks, blocks, blocks, P(), blocks, blocks, blocks, slots)
    out_specs = (slots, slots, P(), blocks, blocks, blocks, blocks, P(), blocks, blocks, blocks, P())

    def on_device(*args):
        fits = mesh.shape["dp"] == 4 and mesh.shape["fsdp"] == 8 and args[0].shape[0] == 1
        return (whole if fits else by_collectives)(*args)

    return jax.shard_map(on_device, mesh=mesh, in_specs=in_specs, out_specs=out_specs, check_vma=False)
```

```python
import functools
import jax
import jax.numpy as jnp
import numpy as np
from jax import lax
from jax.experimental import pallas as pl
from jax.experimental.pallas import tpu as pltpu
from jax.sharding import PartitionSpec as P

D = 576
NQ = 9
NK = 3
GROUP = NQ // NK
H = 64
HALF = H // 2
FF = 1536
T = 512
NF = 8
QB = D // NF
KB = NK * H // NF
FB = FF // NF
OB = 80
EPS = 1e-05
ROPE_BASE = 10000.0
SCALE = H ** (-0.5)
NEG = -1e30
BLK = 256
VMEM_LIMIT = 63 * 2**20
ROWS = D // 4
LANES = FF // 4
BF = jnp.bfloat16
F32 = jnp.float32


def dot(a, b, ca, cb):
    return lax.dot_general(a, b, (((ca,), (cb,)), ((), ())), preferred_element_type=F32)


def rope_tables():
    inverse = ROPE_BASE ** (-(2.0 * np.arange(HALF, dtype=np.float64)) / H)
    angles = inverse[:, None] * np.arange(T, dtype=np.float64)[None, :]
    return np.cos(angles).astype(np.float32), np.sin(angles).astype(np.float32)


def parts_of(row):
    hi = row.astype(BF).astype(F32)
    rest = row - hi
    mid = rest.astype(BF).astype(F32)
    return [hi, mid, rest - mid]


def lane_tiles():
    return [slice(128 * i, 128 * i + 128) for i in range(T // 128)]


class Work:
    def __init__(self, order, refs):
        self.order = order
        self.__dict__.update(refs)

    def start(self):
        count = self.length[0]
        place = lax.broadcasted_iota(jnp.int32, (8, T), 1)
        valid = (place < count).astype(F32)
        self.valid[...] = valid
        for ts in lane_tiles():
            self.S[0, :, ts] = self.x[:, ts].astype(F32)
            self.G[:, ts] = jnp.where(valid[0:1, ts] > 0.0, self.ct[:, ts].astype(F32), 0.0)
        self.gainA[...] = jnp.broadcast_to(self.ga[...], (128, D)).T
        self.gainM[...] = jnp.broadcast_to(self.gm[...], (128, D)).T
        self.gacc[...] = jnp.zeros_like(self.gacc)
        self.QA[:, :, H:, :] = jnp.zeros((2, NQ, H, T), BF)
        self.DOA[:, H:, :] = jnp.zeros((NQ, H, T), BF)

    def norm(self, src, r, gain, dst, rho_ref, row):
        for ts in lane_tiles():
            v = src[r, :, ts]
            total = jnp.sum(v * v, axis=0, keepdims=True)
            if row is not None:
                self.stat[row : row + 1, ts] = total
            rho = lax.rsqrt(total * (1.0 / D) + EPS)
            rho_ref[r, 0:1, ts] = rho
            dst[r, :, ts] = (v * rho * gain[...]).astype(BF)

    def natural_rows(self, ref, base, width, first, count):
        pieces = []
        row = first
        while row < first + count:
            f, i = row // width, row % width
            n = min(width - i, first + count - row)
            at = 128 * self.order.index(f) + base + i
            pieces.append(ref[at : at + n, :])
            row += n
        return pieces[0] if len(pieces) == 1 else jnp.concatenate(pieces, axis=0)

    def prepare(self, r):
        self.norm(self.S, r, self.gainA, self.XA, self.rhoA, 3 * r)

    def project(self, r):
        for c in range(2):
            cs = slice(512 * c, 512 * c + 512)
            self.Y[cs, :] = dot(self.WA[:, cs], self.XA[r], 0, 0)
        cos, sin = self.cos[...], self.sin[...]
        one = jnp.ones((1, T), F32)
        place = lax.broadcasted_iota(jnp.int32, (1, T), 1)
        bias = jnp.where(place < self.length[0], 0.0, NEG)
        for h in range(NQ + NK):
            base, width, at = (0, QB, h) if h < NQ else (QB, KB, h - NQ)
            a = self.natural_rows(self.Y, base, width, H * at, HALF)
            b = self.natural_rows(self.Y, base, width, H * at + HALF, HALF)
            first, second = a * cos - b * sin, b * cos + a * sin
            if h < NQ:
                self.QA[r, h, 0:HALF, :] = (first * SCALE).astype(BF)
                self.QA[r, h, HALF:H, :] = (second * SCALE).astype(BF)
                self.QA[r, h, H : H + 16, :] = jnp.concatenate([one, jnp.zeros((15, T), F32)], axis=0).astype(BF)
            else:
                g = h - NQ
                key = jnp.concatenate([first, second], axis=0)
                self.KT[r, g] = key.astype(BF)
                v = jnp.concatenate(
                    [
                        self.natural_rows(self.Y, QB + KB, KB, H * g, HALF),
                        self.natural_rows(self.Y, QB + KB, KB, H * g + HALF, HALF),
                    ],
                    axis=0,
                )
                self.VT[g] = v.astype(BF)
                ones3 = jnp.ones((3, T), F32)
                tail = jnp.zeros((H - 4, T), F32)
                ktall = jnp.concatenate([key, bias, ones3, tail], axis=0)
                vtall = jnp.concatenate([v, jnp.zeros((1, T), F32), ones3, tail], axis=0)
                for ts in lane_tiles():
                    self.KTOK[r, g, ts, :] = ktall[:, ts].T.astype(BF)
                    self.VTOK[r, g, ts, :] = vtall[:, ts].T.astype(BF)

    def diagonal(self):
        key = lax.broadcasted_iota(jnp.int32, (BLK, BLK), 0)
        query = lax.broadcasted_iota(jnp.int32, (BLK, BLK), 1)
        return key <= query

    def attend(self, r, links=None):
        low, high = slice(0, BLK), slice(BLK, T)

        def head(h, carry):
            g = h // GROUP
            allowed = self.diagonal()
            at = pl.ds(pl.multiple_of(h * H, H), H)
            s = dot(self.KTOK[r, g, low, :], self.QA[r, h, :, low], 1, 0)
            s = jnp.where(allowed, s, NEG)
            top = jnp.max(s, axis=0, keepdims=True)
            p = jnp.exp(s - top)
            total = jnp.sum(p, axis=0, keepdims=True)
            o = dot(self.VT[g, :, low], p.astype(BF), 1, 0)
            self.AT[r, at, low] = (o * (1.0 / total)).astype(BF)
            lse0 = top + jnp.log(total)
            s0 = dot(self.KTOK[r, g, low, :], self.QA[r, h, :, high], 1, 0)
            s1 = dot(self.KTOK[r, g, high, :], self.QA[r, h, :, high], 1, 0)
            s1 = jnp.where(allowed, s1, NEG)
            top = jnp.maximum(jnp.max(s0, axis=0, keepdims=True), jnp.max(s1, axis=0, keepdims=True))
            p0 = jnp.exp(s0 - top)
            p1 = jnp.exp(s1 - top)
            total = jnp.sum(p0, axis=0, keepdims=True) + jnp.sum(p1, axis=0, keepdims=True)
            o = dot(self.VT[g, :, low], p0.astype(BF), 1, 0) + dot(self.VT[g, :, high], p1.astype(BF), 1, 0)
            self.AT[r, at, high] = (o * (1.0 / total)).astype(BF)
            lse1 = top + jnp.log(total)
            lse = jnp.concatenate([lse0, lse1], axis=1)
            rows = [jnp.ones((1, T), F32)] + parts_of(-lse) + [jnp.zeros((12, T), F32)]
            self.QA[r, h, H : H + 16, :] = jnp.concatenate(rows, axis=0).astype(BF)
            return carry

        for g in range(NK):
            lax.fori_loop(GROUP * g, GROUP * g + GROUP, head, 0)
            if links:
                links.run(*HEADS[g])

    def out_project(self, r):
        for c in range(2):
            cs = slice(512 * c, 512 * c + 512)
            self.Y[cs, :] = dot(self.WO[:, cs], self.AT[r], 0, 0)
        squares = jnp.zeros((8, T), F32)
        for b in range(NF):
            f = self.order[b]
            y = self.Y[128 * b : 128 * b + QB, :]
            rows = slice(QB * f, QB * f + QB)
            self.M[r, rows, :] = self.S[r, rows, :] + y
            for i in range(QB // 8):
                squares = squares + y[8 * i : 8 * i + 8] * y[8 * i : 8 * i + 8]
        self.stat[3 * r + 1 : 3 * r + 2, :] = jnp.sum(squares, axis=0, keepdims=True)

    def mlp(self, r, links=None):
        self.norm(self.M, r, self.gainM, self.XM, self.rhoM, None)

        def block(b, carry):
            f = 2 * lax.rem(b, 4) + b // 4 if self.order[1] == 2 else b
            cols = pl.ds(pl.multiple_of(2 * FB * b, 128), 2 * FB)
            gu = dot(self.WGU[:, cols], self.XM[r], 0, 0)
            gate, up = gu[:FB], gu[FB:]
            rows = pl.ds(pl.multiple_of(FB * f, 64), FB)
            self.GATE[r, rows, :] = gate.astype(BF)
            self.UP[r, rows, :] = up.astype(BF)
            self.HID[r, rows, :] = (gate * jax.nn.sigmoid(gate) * up).astype(BF)
            return carry

        lax.fori_loop(0, NF, block, 0)
        if links:
            links.run(*BEFORE_DOWN)
        self.Y[0 : OB * NF, :] = dot(self.WDT[...], self.HID[r], 1, 0)
        squares = jnp.zeros((8, T), F32)
        for b in range(NF):
            f = self.order[b]
            y = self.Y[OB * b : OB * b + QB, :]
            rows = slice(QB * f, QB * f + QB)
            after = self.M[r, rows, :] + y
            if r == 0:
                self.S[1, rows, :] = after
            else:
                self.E[rows, :] = after
            for i in range(QB // 8):
                squares = squares + y[8 * i : 8 * i + 8] * y[8 * i : 8 * i + 8]
        self.stat[3 * r + 2 : 3 * r + 3, :] = jnp.sum(squares, axis=0, keepdims=True)

    def write_output(self):
        valid = self.valid[0:1, :]
        for ts in lane_tiles():
            v = jnp.where(valid[:, ts] > 0.0, self.E[:, ts], 0.0)
            self.out[:, ts] = v.astype(BF)

    def pack_grad(self, dst, width):
        for b in range(NF):
            f = self.order[b]
            v = self.G[QB * f : QB * f + QB, :]
            v = jnp.concatenate([v, jnp.zeros((width - QB, T), F32)], axis=0)
            dst[width * b : width * b + width, :] = v.astype(BF)

    def add_term(self, dst, index, value, r):
        if r == 0:
            value = value + dst[index].astype(F32)
        dst[index] = value.astype(dst.dtype)

    def norm_back(self, src, r, rho_ref, gain, slot):
        for ts in lane_tiles():
            e, v, rho = self.E[:, ts], src[r, :, ts], rho_ref[r, 0:1, ts]
            u = e * gain[...]
            mean = jnp.sum(u * v, axis=0, keepdims=True) * (1.0 / D)
            self.gacc[slot] += e * (v * rho)
            self.G[:, ts] = self.G[:, ts] + rho * (u - v * (rho * rho * mean))

    def mlp_back(self, r, links=None):
        self.pack_grad(self.GLD, OB)
        for c in range(2):
            cs = slice(768 * c, 768 * c + 768)
            self.add_term(self.DD, (slice(None), cs), dot(self.GLD[...], self.HID[r, cs, :], 1, 1), r)
        if links:
            links.run(*AFTER_DOWN)

        def block(z, carry):
            rows = pl.ds(pl.multiple_of(2 * FB * z, 128), 2 * FB)
            grad = dot(self.WDT[:, rows], self.GLD[...], 0, 0)
            gate = self.GATE[r, rows, :].astype(F32)
            up = self.UP[r, rows, :].astype(F32)
            sig = jax.nn.sigmoid(gate)
            dgate = grad * up * (sig * (1.0 + gate * (1.0 - sig)))
            dup = grad * (gate * sig)
            for k in range(2):
                b = z + 4 * k if self.order[1] == 2 else 2 * z + k
                self.DGU[pl.ds(pl.multiple_of(2 * FB * b, 128), FB), :] = dgate[FB * k : FB * k + FB].astype(BF)
                self.DGU[pl.ds(pl.multiple_of(2 * FB * b + FB, 64), FB), :] = dup[FB * k : FB * k + FB].astype(BF)
            return carry

        lax.fori_loop(0, 4, block, 0)
        for c in range(4):
            cs = slice(768 * c, 768 * c + 768)
            self.add_term(self.DG, (slice(None), cs), dot(self.XM[r], self.DGU[cs, :], 1, 1), r)
        if links:
            links.run(*AFTER_GATE)
        self.E[...] = dot(self.WGU[...], self.DGU[...], 1, 0)
        self.norm_back(self.M, r, self.rhoM, self.gainM, 1)

    def attend_back(self, r, links=None):
        self.pack_grad(self.GLO, 128)
        for c in range(2):
            cs = slice(512 * c, 512 * c + 512)
            self.add_term(self.DO, (slice(None), cs), dot(self.AT[r], self.GLO[cs, :], 1, 1), r)
        if links:
            links.run(*AFTER_OUT)
        self.E[...] = dot(self.WO[...], self.GLO[...], 1, 0)
        for h in range(NQ):
            rows = slice(H * h, H * h + H)
            do = self.E[rows, :].astype(BF)
            self.DOA[h, 0:H, :] = do
            delta = jnp.sum(do.astype(F32) * self.AT[r, rows, :].astype(F32), axis=0, keepdims=True)
            rows = [jnp.zeros((1, T), F32)] + parts_of(-delta) + [jnp.zeros((12, T), F32)]
            self.DOA[h, H : H + 16, :] = jnp.concatenate(rows, axis=0).astype(BF)
        low, high = slice(0, BLK), slice(BLK, T)
        self.Y[D : D + 2 * NK * H, :] = jnp.zeros((2 * NK * H, T), F32)

        def head(h, carry):
            g = h // GROUP
            allowed = self.diagonal()
            at = pl.ds(pl.multiple_of(h * H, H), H)
            kat = pl.ds(pl.multiple_of(D + g * H, H), H)
            vat = pl.ds(pl.multiple_of(D + NK * H + g * H, H), H)
            q, do = self.QA[r, h], self.DOA[h]
            k0, k1 = self.KTOK[r, g, low, :], self.KTOK[r, g, high, :]
            v0, v1 = self.VTOK[r, g, low, :], self.VTOK[r, g, high, :]
            t0, t1 = self.KT[r, g, :, low], self.KT[r, g, :, high]

            p = jnp.where(allowed, jnp.exp(dot(k0, q[:, low], 1, 0)), 0.0)
            ds = (p * dot(v0, do[:, low], 1, 0)).astype(BF)
            p = p.astype(BF)
            self.Y[at, low] = dot(t0, ds, 1, 0) * SCALE
            dk0 = dot(q[0:H, low], ds, 1, 1)
            dv0 = dot(do[0:H, low], p, 1, 1)

            p = jnp.exp(dot(k0, q[:, high], 1, 0))
            ds = (p * dot(v0, do[:, high], 1, 0)).astype(BF)
            p = p.astype(BF)
            dq = dot(t0, ds, 1, 0)
            dk0 += dot(q[0:H, high], ds, 1, 1)
            dv0 += dot(do[0:H, high], p, 1, 1)

            p = jnp.where(allowed, jnp.exp(dot(k1, q[:, high], 1, 0)), 0.0)
            ds = (p * dot(v1, do[:, high], 1, 0)).astype(BF)
            p = p.astype(BF)
            self.Y[at, high] = (dq + dot(t1, ds, 1, 0)) * SCALE
            self.Y[kat, low] += dk0
            self.Y[vat, low] += dv0
            self.Y[kat, high] += dot(q[0:H, high], ds, 1, 1)
            self.Y[vat, high] += dot(do[0:H, high], p, 1, 1)
            return carry

        for g in range(NK):
            lax.fori_loop(GROUP * g, GROUP * g + GROUP, head, 0)
            if links:
                links.run(*BACK_HEADS[g])

    def project_back(self, r, links=None):
        cos, sin = self.cos[...], self.sin[...]
        for h in range(NQ + NK):
            first, second = slice(H * h, H * h + HALF), slice(H * h + HALF, H * h + H)
            a, b = self.Y[first, :], self.Y[second, :]
            self.Y[first, :] = a * cos + b * sin
            self.Y[second, :] = b * cos - a * sin
        for b in range(NF):
            f = self.order[b]
            rows = jnp.concatenate(
                [
                    self.Y[QB * f : QB * f + QB, :],
                    self.Y[D + KB * f : D + KB * f + KB, :],
                    self.Y[D + NK * H + KB * f : D + NK * H + KB * f + KB, :],
                    jnp.zeros((128 - QB - 2 * KB, T), F32),
                ],
                axis=0,
            )
            self.GLO[128 * b : 128 * b + 128, :] = rows.astype(BF)
        for c in range(2):
            cs = slice(512 * c, 512 * c + 512)
            self.add_term(self.DA, (slice(None), cs), dot(self.XA[r], self.GLO[cs, :], 1, 1), r)
        if links:
            links.run(*AFTER_QKV)
        self.E[...] = dot(self.WA[...], self.GLO[...], 1, 0)
        self.norm_back(self.S, r, self.rhoA, self.gainA, 0)

    def write_grad(self):
        for ts in lane_tiles():
            self.gin[:, ts] = self.G[:, ts]

    def small(self):
        valid = self.valid[0:1, :]
        rows = [jnp.sum(self.gacc[i].T, axis=0, keepdims=True) for i in range(2)]
        sums = jnp.sum(jnp.where(valid > 0.0, self.stat[0:6, :], 0.0), axis=1, keepdims=True)
        count = jnp.sum(valid, axis=1, keepdims=True)
        lane = lax.broadcasted_iota(jnp.int32, (6, D), 1)
        return jnp.concatenate(rows + [jnp.where(lane < 128, sums, count)], axis=0)


SCRATCH = dict(
    S=((2, D, T), F32), G=((D, T), F32), E=((D, T), F32), Y=((1024, T), F32),
    XA=((2, D, T), BF), XM=((2, D, T), BF), rhoA=((2, 8, T), F32), rhoM=((2, 8, T), F32),
    QA=((2, NQ, 128, T), BF), KT=((2, NK, H, T), BF), VT=((NK, H, T), BF),
    KTOK=((2, NK, T, 128), BF), VTOK=((2, NK, T, 128), BF), AT=((2, D, T), BF), M=((2, D, T), F32),
    GATE=((2, FF, T), BF), UP=((2, FF, T), BF), HID=((2, FF, T), BF),
    GLD=((OB * NF, T), BF), GLO=((1024, T), BF), DGU=((2 * FF, T), BF), DOA=((NQ, 128, T), BF),
    stat=((8, T), F32), valid=((8, T), F32), gacc=((2, D, 128), F32), gainA=((D, 128), F32), gainM=((D, 128), F32),
)
WEIGHTS = dict(WA=((D, 1024), BF), WO=((D, 1024), BF), WGU=((D, 2 * FF), BF), WDT=((OB * NF, FF), BF))
GRADS = dict(DA=((D, 1024), BF), DO=((D, 1024), BF), DG=((D, 2 * FF), BF), DD=((OB * NF, FF), BF))

def compute_kernel(order, names, *refs):
    w = Work(order, dict(zip(names, refs)))
    w.start()
    for r in range(2):
        w.prepare(r)
        w.project(r)
        w.attend(r)
        w.out_project(r)
        w.mlp(r)
    w.write_output()
    for r in (1, 0):
        w.mlp_back(r)
        w.attend_back(r)
        w.project_back(r)
    w.write_grad()
    w.tiny[...] = w.small()


def local_compute(order, x, length, ga, gm, ct, packed):
    cos, sin = rope_tables()
    ins = dict(length=length, x=x, ct=ct, ga=ga[None, :], gm=gm[None, :], cos=jnp.asarray(cos), sin=jnp.asarray(sin), **packed)
    outs = dict(out=((D, T), BF), gin=((D, T), F32), tiny=((8, D), F32), **GRADS)
    names = list(ins) + list(outs) + list(SCRATCH)
    vmem = pl.BlockSpec(memory_space=pltpu.VMEM)
    results = pl.pallas_call(
        functools.partial(compute_kernel, order, names),
        out_shape=[jax.ShapeDtypeStruct(*s) for s in outs.values()],
        in_specs=[pl.BlockSpec(memory_space=pltpu.SMEM)] + [vmem] * (len(ins) - 1),
        out_specs=[vmem] * len(outs),
        scratch_shapes=[pltpu.VMEM(*s) for s in SCRATCH.values()],
        compiler_params=pltpu.CompilerParams(vmem_limit_bytes=VMEM_LIMIT),
    )(*ins.values())
    return dict(zip(outs, results))


def pack(order, q, k, v, o, g, u, d):
    def cols(w, width):
        return w.reshape(w.shape[0], NF, width)[:, np.array(order)]
    zero = jnp.zeros((D, NF, 128 - QB - 2 * KB), BF)
    wa = jnp.concatenate([cols(q, QB), cols(k, KB), cols(v, KB), zero], axis=2).reshape(D, 1024)
    wo = jnp.pad(cols(o, QB), ((0, 0), (0, 0), (0, 128 - QB))).reshape(D, 1024)
    wgu = jnp.concatenate([cols(g, FB), cols(u, FB)], axis=2).reshape(D, 2 * FF)
    wd = jnp.pad(d.T.reshape(NF, QB, FF)[np.array(order)], ((0, 0), (0, OB - QB), (0, 0))).reshape(OB * NF, FF)
    return dict(WA=wa, WO=wo, WGU=wgu, WDT=wd)


def unpack(order, r):
    back = np.argsort(np.array(order))
    a = r["DA"].astype(F32).reshape(D, NF, 128)[:, back]
    o = r["DO"].astype(F32).reshape(D, NF, 128)[:, back, :QB].reshape(D, D)
    g = r["DG"].astype(F32).reshape(D, NF, 2 * FB)[:, back]
    d = r["DD"].astype(F32).reshape(NF, OB, FF)[back, :QB].reshape(D, FF).T
    return (
        a[:, :, :QB].reshape(D, D), a[:, :, QB : QB + KB].reshape(D, NK * H), a[:, :, QB + KB : QB + 2 * KB].reshape(D, NK * H),
        o, g[:, :, :FB].reshape(D, FF), g[:, :, FB:].reshape(D, FF), d,
    )


PIECES = ("A", "O", "G0", "G1", "G2", "D0", "D1")
CUT_OF = dict(
    A=("A", 0, ROWS), O=("O", 0, ROWS), G0=("G", 0, 48), G1=("G", 48, 48), G2=("G", 96, 48), D0=("D", 0, 256), D1=("D", 256, 128)
)
WEIGHT_OF = dict(A="WA", O="WO", G="WGU", D="WDT")
GRAD_OF = dict(A="DA", O="DO", G="DG", D="DD")
WIDTH_OF = dict(A=128, O=128, G=2 * FB)
MESH = pl.DeviceIdType.MESH


def region(refs, piece, dp, y, z, count):
    matrix, first, size = CUT_OF[piece]
    ref, line = refs[matrix], 4 * y + z
    if matrix == "D":
        rows = pl.ds(pl.multiple_of(OB * line, 16), OB * count)
        return ref.at[rows, pl.ds(pl.multiple_of(LANES * dp + first, 128), size)]
    width = WIDTH_OF[matrix]
    rows = pl.ds(pl.multiple_of(ROWS * dp + first, 16), size)
    return ref.at[rows, pl.ds(pl.multiple_of(width * line, 128), width * count)]


def shape_of(piece, count):
    matrix, first, size = CUT_OF[piece]
    return (OB * count, size) if matrix == "D" else (size, WIDTH_OF[matrix] * count)


class Links:
    def __init__(self, refs):
        self.__dict__.update(refs)
        self.weights = {m: refs[n] for m, n in WEIGHT_OF.items()}
        self.grads = {m: refs[n] for m, n in GRAD_OF.items()}
        self.dp, f = lax.axis_index("dp"), lax.axis_index("fsdp")
        self.x, self.c = self.dp // 2, lax.rem(self.dp, 2)
        self.z, self.y = f // 2, lax.rem(f, 2)
        self.far = 2 * (1 - self.x) + self.c
        self.other = 2 * self.x + 1 - self.c
        self.sib = (self.other, f)
        self.xn = (self.far, f)
        self.yn = (self.dp, 2 * self.z + 1 - self.y)
        self.peer = [None] + [lax.rem(self.z + k, 4) for k in (1, 2, 3)]
        self.zn = [None] + [(self.dp, 2 * self.peer[k] + self.y) for k in (1, 2, 3)]
        self.copies = {}
        self.used = 0

    def barrier(self):
        sem = pltpu.get_barrier_semaphore()
        partners = [self.sib, self.xn, self.yn] + self.zn[1:]
        for device in partners:
            pl.semaphore_signal(sem, inc=1, device_id=device, device_id_type=MESH)
        pl.semaphore_wait(sem, len(partners))

    def send(self, name, src, dst, device):
        copy = pltpu.make_async_remote_copy(
            src_ref=src,
            dst_ref=dst,
            send_sem=self.sent.at[self.used],
            recv_sem=self.came.at[self.used],
            device_id=device,
            device_id_type=MESH,
        )
        self.used += 1
        copy.start()
        self.copies[name] = copy

    def arrived(self, *names):
        for name in names:
            self.copies[name].wait_recv()

    def finish(self):
        for copy in self.copies.values():
            copy.wait_send()

    def run(self, *steps):
        for step in steps:
            kind, piece = step.split()
            getattr(self, kind)(piece)


    def spread(self, tag, p, device, dp=None, y=None, z=0, count=4):
        block = region(self.weights, p, self.dp if dp is None else dp, self.y if y is None else y, z, count)
        self.send(("w", p, tag), block, block, device)

    def share(self, p):
        for k in (1, 3, 2):
            self.spread(f"z{k}", p, self.zn[k], z=self.z, count=1)

    def line(self, p):
        self.arrived(*[("w", p, f"z{k}") for k in (1, 2, 3)])
        self.spread("x", p, self.xn)
        self.spread("y", p, self.yn)
        self.spread("s", p, self.sib)

    def cross(self, p):
        self.arrived(("w", p, "x"))
        self.spread("xy", p, self.yn, dp=self.far, count=2)
        self.spread("sx", p, self.sib, dp=self.far)
        self.arrived(("w", p, "y"))
        self.spread("yx", p, self.xn, y=1 - self.y, z=2, count=2)
        self.spread("sy", p, self.sib, y=1 - self.y)

    def rest(self, p):
        self.arrived(("w", p, "xy"))
        self.spread("sxy", p, self.sib, dp=self.far, y=1 - self.y, count=2)
        self.arrived(("w", p, "yx"))
        self.spread("syx", p, self.sib, dp=self.far, y=1 - self.y, z=2, count=2)

    def end(self, p):
        self.arrived(*[("w", p, tag) for tag in ("s", "sx", "sy", "sxy", "syx")])


    def term(self, p, dp, y, z=0, count=4):
        return region(self.grads, p, dp, y, z, count)

    def add(self, p, dp, y, z, count, came):
        at = self.term(p, dp, y, z, count)
        at[...] = at[...] + came[...]

    def sibs(self, p):
        room = getattr(self, "one" + p)
        for i in range(2):
            for y in range(2):
                dp = 2 * i + 1 - self.c
                self.send(("g", p, "s", i, y), self.term(p, dp, y), room.at[i, y], self.sib)

    def pair(self, p):
        room = getattr(self, "one" + p)
        for i in range(2):
            for y in range(2):
                self.arrived(("g", p, "s", i, y))
                self.add(p, 2 * i + self.c, y, 0, 4, room.at[i, y])
        ups, across = getattr(self, "twoy" + p), getattr(self, "twox" + p)
        for i, dp in enumerate((self.dp, self.far)):
            self.send(("g", p, "y", i), self.term(p, dp, 1 - self.y, 0, 2), ups.at[i], self.yn)
        for j, y in enumerate((self.y, 1 - self.y)):
            self.send(("g", p, "x", j), self.term(p, self.far, y, 2, 2), across.at[j], self.xn)

    def twos(self, p):
        ups, across = getattr(self, "twoy" + p), getattr(self, "twox" + p)
        for i in (1, 0):
            self.arrived(("g", p, "y", i))
            self.add(p, (self.dp, self.far)[i], self.y, 0, 2, ups.at[i])
            if i == 1:
                self.send(("g", p, "yx"), self.term(p, self.far, self.y, 0, 2), getattr(self, "threex" + p), self.xn)
        for j in (1, 0):
            self.arrived(("g", p, "x", j))
            self.add(p, self.dp, (self.y, 1 - self.y)[j], 2, 2, across.at[j])
            if j == 1:
                self.send(("g", p, "xy"), self.term(p, self.dp, 1 - self.y, 2, 2), getattr(self, "threey" + p), self.yn)

    def fours(self, p):
        self.arrived(("g", p, "yx"))
        self.add(p, self.dp, self.y, 0, 2, getattr(self, "threex" + p))
        self.arrived(("g", p, "xy"))
        self.add(p, self.dp, self.y, 2, 2, getattr(self, "threey" + p))
        for k in (1, 3, 2):
            src = self.term(p, self.dp, self.y, self.peer[k], 1)
            self.send(("g", p, "z", k), src, getattr(self, "four" + p).at[k - 1], self.zn[k])

    def total(self, p):
        total = self.term(p, self.dp, self.y, self.z, 1)[...].astype(F32)
        for k in (1, 2, 3):
            self.arrived(("g", p, "z", k))
            total = total + getattr(self, "four" + p)[k - 1].astype(F32)
        matrix, first, size = CUT_OF[p]
        if matrix == "D":
            self.sumD[:, first : first + size] = total[:QB, :]
        else:
            at = dict(A=0, O=128, G=256)[matrix]
            self.sumN[first : first + size, at : at + WIDTH_OF[matrix]] = total


    def tiny(self, step):
        step = int(step)
        if step > 0:
            self.arrived(("t", step - 1))
            self.tinies[step] = self.tinies[step - 1] + self.tinyin[step - 1]
        if step < 3:
            self.send(("t", step), self.tinies.at[step], self.tinyin.at[step], (self.sib, self.xn, self.yn)[step])
        else:
            for k in (1, 2, 3):
                self.send(("t", step, k), self.tinies.at[3], self.tinyz.at[k], self.zn[k])

    def tiny_end(self):
        self.tinyz[0] = self.tinies[3]
        for k in (1, 2, 3):
            self.arrived(("t", 3, k))
        total = None
        for z in range(4):
            term = self.tinyz[lax.rem(self.z - z + 4, 4)]
            total = term if total is None else total + term
        self.sumT[...] = total


def rooms():
    shapes = {}
    for p in PIECES:
        shapes["one" + p] = ((2, 2) + shape_of(p, 4), BF)
        for room in ("twoy", "twox"):
            shapes[room + p] = ((2,) + shape_of(p, 2), BF)
        for room in ("threex", "threey"):
            shapes[room + p] = (shape_of(p, 2), BF)
        shapes["four" + p] = ((3,) + shape_of(p, 1), BF)
    shapes["tinies"] = ((4, 8, D), F32)
    shapes["tinyin"] = ((3, 8, D), F32)
    shapes["tinyz"] = ((4, 8, D), F32)
    return shapes


COPIES = len(PIECES) * (12 + 13) + 6


def pack_own(links, refs):
    rows = lambda *names: [refs[n][...].astype(F32) for n in names]
    zero = lambda n: jnp.zeros((ROWS, n), F32)
    q, k, v, o, g, u, d = rows("q", "k", "v", "o", "g", "u", "d")
    whole = dict(
        A=jnp.concatenate([q, k.T, v.T, zero(128 - QB - 2 * KB)], axis=1),
        O=jnp.concatenate([o, zero(128 - QB)], axis=1),
        G=jnp.concatenate([g, u], axis=1),
        D=jnp.concatenate([d, jnp.zeros((OB - QB, LANES), F32)], axis=0),
    )
    for p in PIECES:
        matrix, first, size = CUT_OF[p]
        own = whole[matrix][:, first : first + size] if matrix == "D" else whole[matrix][first : first + size]
        region(links.weights, p, links.dp, links.y, links.z, 1)[...] = own.astype(BF)


BEGIN = ("share A", "share O", "share G0", "share G1", "share G2", "share D0", "share D1")
BEFORE_PROJECT = ("line A", "line O", "cross A", "line G0", "cross O", "rest A", "line G1", "end A")
AFTER_PROJECT = ("cross G0", "rest O", "line G2")
HEADS = (("cross G1", "rest G0"), ("line D0",), ("cross G2", "rest G1"))
BEFORE_OUT = ("end O", "line D1")
BEFORE_MLP = ("cross D0", "rest G2", "end G0", "end G1", "end G2")
BEFORE_DOWN = ("cross D1", "rest D0", "rest D1", "end D0", "end D1")
AFTER_DOWN = ("sibs D0", "sibs D1")
AFTER_GATE = ("sibs G0", "sibs G1", "sibs G2", "pair D0", "pair D1")
AFTER_OUT = ("sibs O", "pair G0", "pair G1", "pair G2", "twos D0", "twos D1")
BACK_HEADS = (("pair O", "fours D0"), ("twos G0", "fours D1"), ("twos G1", "fours G0"))
AFTER_QKV = ("sibs A", "twos G2", "fours G1", "twos O", "fours G2")
LAST = ("tiny 0", "pair A", "fours O", "tiny 1", "twos A", "tiny 2")
VERY_LAST = ("total D0", "total D1", "total G0", "total G1", "total G2", "fours A", "tiny 3", "total O", "total A")


def whole_kernel(order, names, *args):
    refs = dict(zip(names, args))
    w, links = Work(order, refs), Links(refs)
    links.barrier()
    pack_own(links, refs)
    links.run(*BEGIN)
    w.start()
    w.prepare(0)
    links.run(*BEFORE_PROJECT)
    w.project(0)
    links.run(*AFTER_PROJECT)
    w.attend(0, links)
    links.run(*BEFORE_OUT)
    w.out_project(0)
    links.run(*BEFORE_MLP)
    w.mlp(0, links)
    w.prepare(1)
    w.project(1)
    w.attend(1)
    w.out_project(1)
    w.mlp(1)
    w.write_output()
    w.mlp_back(1)
    w.attend_back(1)
    w.project_back(1)
    w.mlp_back(0, links)
    w.attend_back(0, links)
    w.project_back(0, links)
    links.tinies[0] = w.small()
    links.run(*LAST)
    w.write_grad()
    links.run(*VERY_LAST)
    links.tiny_end()
    links.finish()


def finish_kernel(*refs):
    out, gin, sums, sumd, tiny, oout, ogin, ga, q, k, v, o, gm, g, u, d, rms = refs
    oout[...] = out[...]
    ogin[...] = gin[...]
    q[...] = sums[:, :QB]
    k[...] = sums[:, QB : QB + KB].T
    v[...] = sums[:, QB + KB : QB + 2 * KB].T
    o[...] = sums[:, 128 : 128 + QB]
    g[...] = sums[:, 256 : 256 + FB]
    u[...] = sums[:, 256 + FB : 256 + 2 * FB]
    d[...] = sumd[...]
    ga[...] = tiny[0:1, :]
    gm[...] = tiny[1:2, :]
    lane = lax.broadcasted_iota(jnp.int32, (1, 3), 1)
    for r in range(2):
        first, second, third = [tiny[2 + 3 * r + i : 3 + 3 * r + i, 0:3] for i in range(3)]
        squares = jnp.where(lane == 0, first, jnp.where(lane == 1, second, third))
        rms[r : r + 1, :] = jnp.sqrt(squares / (tiny[2:3, 128:131] * D))


def whole(x, length, ga, q, k, v, o, gm, g, u, d, ct):
    order = [2 * (b % 4) + b // 4 for b in range(NF)]
    cos, sin = rope_tables()
    ins = dict(
        length=length, x=x[0].T, ct=ct[0].T, ga=ga[None, :], gm=gm[None, :], cos=jnp.asarray(cos), sin=jnp.asarray(sin),
        q=q, k=k.T, v=v.T, o=o, g=g, u=u, d=d.T,
    )
    outs = dict(
        out=((D, T), BF), gin=((D, T), F32), sumN=((ROWS, 256 + 2 * FB), F32), sumD=((QB, LANES), F32), sumT=((8, D), F32)
    )
    scratch = dict(SCRATCH, **WEIGHTS, **GRADS, **rooms())
    names = list(ins) + list(outs) + list(scratch) + ["sent", "came"]
    vmem = pl.BlockSpec(memory_space=pltpu.VMEM)
    r = pl.pallas_call(
        functools.partial(whole_kernel, order, names),
        out_shape=[jax.ShapeDtypeStruct(*s) for s in outs.values()],
        in_specs=[pl.BlockSpec(memory_space=pltpu.SMEM)] + [vmem] * (len(ins) - 1),
        out_specs=[vmem] * len(outs),
        scratch_shapes=[pltpu.VMEM(*s) for s in scratch.values()]
        + [pltpu.SemaphoreType.DMA((COPIES,)), pltpu.SemaphoreType.DMA((COPIES,))],
        compiler_params=pltpu.CompilerParams(
            vmem_limit_bytes=VMEM_LIMIT, collective_id=0, has_side_effects=True
        ),
    )(*ins.values())
    rows = [
        ((D, T), BF), ((D, T), F32), ((1, D), F32), (q.shape, F32), (k.shape[::-1], F32), (v.shape[::-1], F32),
        (o.shape, F32), ((1, D), F32), (g.shape, F32), (u.shape, F32), (d.shape[::-1], F32), ((2, 3), F32),
    ]
    out, gin, ga, q, k, v, o, gm, g, u, d, rms = pl.pallas_call(
        finish_kernel,
        out_shape=[jax.ShapeDtypeStruct(*s) for s in rows],
        in_specs=[vmem] * len(outs),
        out_specs=[vmem] * len(rows),
    )(*r)
    return out.T[None], gin.T[None], ga[0], q, k.T, v.T, o, gm[0], g, u, d.T, rms


def by_collectives(x, length, ga, q, k, v, o, gm, g, u, d, ct):
    order = list(range(NF))
    full = [lax.all_gather(lax.all_gather(w, "fsdp", axis=1, tiled=True), "dp", axis=0, tiled=True) for w in (q, k, v, o, g, u, d)]
    packed = pack(order, *full)
    results = [local_compute(order, x[i].T, length[i : i + 1], ga, gm, ct[i].T, packed) for i in range(x.shape[0])]
    out = jnp.stack([r["out"].T for r in results])
    gin = jnp.stack([r["gin"].T for r in results])
    tiny = lax.psum(sum(r["tiny"] for r in results), ("dp", "fsdp"))
    terms = [unpack(order, r) for r in results]
    grads = [
        lax.psum_scatter(
            lax.psum_scatter(sum(t), "dp", scatter_dimension=0, tiled=True), "fsdp", scatter_dimension=1, tiled=True
        )
        for t in zip(*terms)
    ]
    rms = jnp.sqrt(tiny[2:8, 0].reshape(2, 3) / (tiny[2, 128] * D))
    gq, gk, gv, go, gg, gu, gd = grads
    return out, gin, tiny[0], gq, gk, gv, go, tiny[1], gg, gu, gd, rms


def solution(mesh):
    blocks = P("dp", "fsdp")
    slots = P(("dp", "fsdp"), None, None)
    in_specs = (slots, P(("dp", "fsdp")), P(), blocks, blocks, blocks, blocks, P(), blocks, blocks, blocks, slots)
    out_specs = (slots, slots, P(), blocks, blocks, blocks, blocks, P(), blocks, blocks, blocks, P())

    def on_device(*args):
        fits = mesh.shape["dp"] == 4 and mesh.shape["fsdp"] == 8 and args[0].shape[0] == 1
        return (whole if fits else by_collectives)(*args)

    return jax.shard_map(on_device, mesh=mesh, in_specs=in_specs, out_specs=out_specs, check_vma=False)
```

```python
import functools
import jax
import jax.numpy as jnp
import numpy as np
from jax import lax
from jax.experimental import pallas as pl
from jax.experimental.pallas import tpu as pltpu
from jax.sharding import PartitionSpec as P

D = 576
NQ = 9
NK = 3
GROUP = NQ // NK
H = 64
HALF = H // 2
FF = 1536
T = 512
NF = 8
QB = D // NF
KB = NK * H // NF
FB = FF // NF
EPS = 1e-05
ROPE_BASE = 10000.0
SCALE = H ** (-0.5)
NEG = -1e30
BLK = 256
VMEM_LIMIT = 63 * 2**20
ROWS = D // 4
LANES = FF // 4
OW = QB - 8
BF = jnp.bfloat16
F32 = jnp.float32


def dot(a, b, ca, cb):
    return lax.dot_general(a, b, (((ca,), (cb,)), ((), ())), preferred_element_type=F32)


def rope_tables():
    inverse = ROPE_BASE ** (-(2.0 * np.arange(HALF, dtype=np.float64)) / H)
    angles = inverse[:, None] * np.arange(T, dtype=np.float64)[None, :]
    return np.cos(angles).astype(np.float32), np.sin(angles).astype(np.float32)


def parts_of(row):
    hi = row.astype(BF).astype(F32)
    rest = row - hi
    mid = rest.astype(BF).astype(F32)
    return [hi, mid, rest - mid]


def lane_tiles():
    return [slice(128 * i, 128 * i + 128) for i in range(T // 128)]


class Work:
    def __init__(self, order, refs):
        self.order = order
        self.__dict__.update(refs)

    def start(self):
        count = self.length[0]
        place = lax.broadcasted_iota(jnp.int32, (8, T), 1)
        valid = (place < count).astype(F32)
        self.valid[...] = valid
        for ts in lane_tiles():
            self.S[0, :, ts] = self.x[:, ts].astype(F32)
            self.G[:, ts] = jnp.where(valid[0:1, ts] > 0.0, self.ct[:, ts].astype(F32), 0.0)
        self.gainA[...] = jnp.broadcast_to(self.ga[...], (128, D)).T
        self.gainM[...] = jnp.broadcast_to(self.gm[...], (128, D)).T
        row = lax.broadcasted_iota(jnp.int32, (H, 1024), 0)
        lane = lax.broadcasted_iota(jnp.int32, (H, 1024), 1)
        self.pick[...] = jnp.where(lane == 128 * (row // 8) + 120 + lax.rem(row, 8), 1.0, 0.0).astype(BF)
        self.gacc[...] = jnp.zeros_like(self.gacc)
        self.QA[:, :, H:, :] = jnp.zeros((2, NQ, H, T), BF)
        self.DOA[:, H:, :] = jnp.zeros((NQ, H, T), BF)

    def norm(self, src, r, gain, dst, rho_ref, row):
        for ts in lane_tiles():
            v = src[r, :, ts]
            total = jnp.sum(v * v, axis=0, keepdims=True)
            if row is not None:
                self.stat[row : row + 1, ts] = total
            rho = lax.rsqrt(total * (1.0 / D) + EPS)
            rho_ref[r, 0:1, ts] = rho
            dst[r, :, ts] = (v * rho * gain[...]).astype(BF)

    def natural_rows(self, ref, base, width, first, count):
        pieces = []
        row = first
        while row < first + count:
            f, i = row // width, row % width
            n = min(width - i, first + count - row)
            at = 128 * self.order.index(f) + base + i
            pieces.append(ref[at : at + n, :])
            row += n
        return pieces[0] if len(pieces) == 1 else jnp.concatenate(pieces, axis=0)

    def prepare(self, r):
        self.norm(self.S, r, self.gainA, self.XA, self.rhoA, 3 * r)

    def project(self, r):
        for c in range(2):
            cs = slice(512 * c, 512 * c + 512)
            self.Y[cs, :] = dot(self.WA[:, cs], self.XA[r], 0, 0)
        cos, sin = self.cos[...], self.sin[...]
        one = jnp.ones((1, T), F32)
        place = lax.broadcasted_iota(jnp.int32, (1, T), 1)
        bias = jnp.where(place < self.length[0], 0.0, NEG)
        for h in range(NQ + NK):
            base, width, at = (0, QB, h) if h < NQ else (QB, KB, h - NQ)
            a = self.natural_rows(self.Y, base, width, H * at, HALF)
            b = self.natural_rows(self.Y, base, width, H * at + HALF, HALF)
            first, second = a * cos - b * sin, b * cos + a * sin
            if h < NQ:
                self.QA[r, h, 0:HALF, :] = (first * SCALE).astype(BF)
                self.QA[r, h, HALF:H, :] = (second * SCALE).astype(BF)
                self.QA[r, h, H : H + 16, :] = jnp.concatenate([one, jnp.zeros((15, T), F32)], axis=0).astype(BF)
            else:
                g = h - NQ
                key = jnp.concatenate([first, second], axis=0)
                self.KT[r, g] = key.astype(BF)
                v = jnp.concatenate(
                    [
                        self.natural_rows(self.Y, QB + KB, KB, H * g, HALF),
                        self.natural_rows(self.Y, QB + KB, KB, H * g + HALF, HALF),
                    ],
                    axis=0,
                )
                self.VT[g] = v.astype(BF)
                ones3 = jnp.ones((3, T), F32)
                tail = jnp.zeros((H - 4, T), F32)
                ktall = jnp.concatenate([key, bias, ones3, tail], axis=0)
                vtall = jnp.concatenate([v, jnp.zeros((1, T), F32), ones3, tail], axis=0)
                for ts in lane_tiles():
                    self.KTOK[r, g, ts, :] = ktall[:, ts].T.astype(BF)
                    self.VTOK[r, g, ts, :] = vtall[:, ts].T.astype(BF)

    def diagonal(self):
        key = lax.broadcasted_iota(jnp.int32, (BLK, BLK), 0)
        query = lax.broadcasted_iota(jnp.int32, (BLK, BLK), 1)
        return key <= query

    def attend(self, r, links=None):
        low, high = slice(0, BLK), slice(BLK, T)

        def head(h, carry):
            g = h // GROUP
            allowed = self.diagonal()
            at = pl.ds(pl.multiple_of(h * H, H), H)
            s = dot(self.KTOK[r, g, low, :], self.QA[r, h, :, low], 1, 0)
            s = jnp.where(allowed, s, NEG)
            top = jnp.max(s, axis=0, keepdims=True)
            p = jnp.exp(s - top)
            total = jnp.sum(p, axis=0, keepdims=True)
            o = dot(self.VT[g, :, low], p.astype(BF), 1, 0)
            self.AT[r, at, low] = (o * (1.0 / total)).astype(BF)
            lse0 = top + jnp.log(total)
            s0 = dot(self.KTOK[r, g, low, :], self.QA[r, h, :, high], 1, 0)
            s1 = dot(self.KTOK[r, g, high, :], self.QA[r, h, :, high], 1, 0)
            s1 = jnp.where(allowed, s1, NEG)
            top = jnp.maximum(jnp.max(s0, axis=0, keepdims=True), jnp.max(s1, axis=0, keepdims=True))
            p0 = jnp.exp(s0 - top)
            p1 = jnp.exp(s1 - top)
            total = jnp.sum(p0, axis=0, keepdims=True) + jnp.sum(p1, axis=0, keepdims=True)
            o = dot(self.VT[g, :, low], p0.astype(BF), 1, 0) + dot(self.VT[g, :, high], p1.astype(BF), 1, 0)
            self.AT[r, at, high] = (o * (1.0 / total)).astype(BF)
            lse1 = top + jnp.log(total)
            lse = jnp.concatenate([lse0, lse1], axis=1)
            rows = [jnp.ones((1, T), F32)] + parts_of(-lse) + [jnp.zeros((12, T), F32)]
            self.QA[r, h, H : H + 16, :] = jnp.concatenate(rows, axis=0).astype(BF)
            return carry

        for g in range(NK):
            lax.fori_loop(GROUP * g, GROUP * g + GROUP, head, 0)
            if links:
                links.run(*HEADS[g])

    def rest_of_output(self):
        self.WO[:, NF * OW :] = dot(self.WA[...], self.pick[...], 1, 1).astype(BF)

    def after(self, value, src, r, dst, row, squares):
        n = value.shape[0]
        now = src[r, row : row + n, :] + value
        if dst is self.E:
            dst[row : row + n, :] = now
        else:
            dst[r if dst is self.M else 1, row : row + n, :] = now
        for i in range(n // 8):
            part = value[8 * i : 8 * i + 8]
            squares = squares + part * part
        return squares

    def out_project(self, r):
        self.Y[0:D, :] = dot(self.WO[...], self.AT[r], 0, 0)
        squares = jnp.zeros((8, T), F32)
        for b in range(NF):
            f = self.order[b]
            squares = self.after(self.Y[OW * b : OW * b + OW, :], self.S, r, self.M, QB * f, squares)
            at = NF * OW + 8 * b
            squares = self.after(self.Y[at : at + 8, :], self.S, r, self.M, QB * f + OW, squares)
        self.stat[3 * r + 1 : 3 * r + 2, :] = jnp.sum(squares, axis=0, keepdims=True)

    def mlp(self, r, links=None):
        self.norm(self.M, r, self.gainM, self.XM, self.rhoM, None)
        for y in range(2):
            cs = slice(512 * y, 512 * y + 512)
            for i in range(3):
                self.Y[512 * i : 512 * i + 512, :] = dot(self.WG[i, :, cs], self.XM[r], 0, 0)

            def block(z, carry):
                f = self.natural(y, z)
                for j in range(3):
                    gate_at, up_at = self.places(j)
                    gate = self.Y[pl.ds(pl.multiple_of(gate_at[0] * 512 + 128 * z + gate_at[1], 64), 64), :]
                    up = self.Y[pl.ds(pl.multiple_of(up_at[0] * 512 + 128 * z + up_at[1], 64), 64), :]
                    rows = pl.ds(pl.multiple_of(FB * f + 64 * j, 64), 64)
                    self.GATE[r, rows, :] = gate.astype(BF)
                    self.UP[r, rows, :] = up.astype(BF)
                    self.HID[r, rows, :] = (gate * jax.nn.sigmoid(gate) * up).astype(BF)
                return carry

            lax.fori_loop(0, 4, block, 0)
            if links:
                links.run(*MLP[y])
        self.Y[0:D, :] = dot(self.WDT[...], self.HID[r], 1, 0)
        squares = jnp.zeros((8, T), F32)
        for b in range(NF):
            dst = self.S if r == 0 else self.E
            squares = self.after(self.Y[QB * b : QB * b + QB, :], self.M, r, dst, QB * self.order[b], squares)
        self.stat[3 * r + 2 : 3 * r + 3, :] = jnp.sum(squares, axis=0, keepdims=True)

    def natural(self, y, z):
        return 2 * z + y if self.order[1] == 2 else 4 * y + z

    def places(self, j):
        return ((0, 0), (0, 64), (1, 0))[j], ((1, 64), (2, 0), (2, 64))[j]

    def write_output(self):
        valid = self.valid[0:1, :]
        for ts in lane_tiles():
            v = jnp.where(valid[:, ts] > 0.0, self.E[:, ts], 0.0)
            self.out[:, ts] = v.astype(BF)

    def pack_down(self):
        for k in range(NF // 2):
            rows = [self.G[QB * self.order[b] : QB * self.order[b] + QB, :] for b in (2 * k, 2 * k + 1)]
            self.GLD[2 * QB * k : 2 * QB * k + 2 * QB, :] = jnp.concatenate(rows, axis=0).astype(BF)

    def pack_out(self):
        tails = []
        for b in range(NF):
            at = QB * self.order[b]
            self.GLO[OW * b : OW * b + OW, :] = self.G[at : at + OW, :].astype(BF)
            tails.append(self.G[at + OW : at + QB, :])
        self.GLO[NF * OW : D, :] = jnp.concatenate(tails, axis=0).astype(BF)

    def add_term(self, dst, index, value, r):
        if r == 0:
            value = value + dst[index].astype(F32)
        dst[index] = value.astype(dst.dtype)

    def norm_back(self, src, r, rho_ref, gain, slot):
        for ts in lane_tiles():
            e, v, rho = self.E[:, ts], src[r, :, ts], rho_ref[r, 0:1, ts]
            u = e * gain[...]
            mean = jnp.sum(u * v, axis=0, keepdims=True) * (1.0 / D)
            self.gacc[slot] += e * (v * rho)
            self.G[:, ts] = self.G[:, ts] + rho * (u - v * (rho * rho * mean))

    def mlp_back(self, r, links=None):
        self.pack_down()
        for c in range(2):
            cs = slice(768 * c, 768 * c + 768)
            self.add_term(self.DD, (slice(None), cs), dot(self.GLD[...], self.HID[r, cs, :], 1, 1), r)
        if links:
            links.run(*AFTER_DOWN)

        for k in range(4):
            rows = slice(2 * FB * k, 2 * FB * k + 2 * FB)
            self.Y[0 : 2 * FB, :] = dot(self.WDT[:, rows], self.GLD[...], 0, 0)
            for m in range(2):
                f = 2 * k + m
                b = self.order.index(f)
                for j in range(3):
                    at = FB * f + 64 * j
                    grad = self.Y[FB * m + 64 * j : FB * m + 64 * j + 64, :]
                    gate = self.GATE[r, at : at + 64, :].astype(F32)
                    up = self.UP[r, at : at + 64, :].astype(F32)
                    sig = jax.nn.sigmoid(gate)
                    silu = gate * sig
                    gate_at, up_at = self.places(j)
                    to = 1024 * gate_at[0] + 128 * b + gate_at[1]
                    self.DGU[to : to + 64, :] = (grad * up * (sig + silu * (1.0 - sig))).astype(BF)
                    to = 1024 * up_at[0] + 128 * b + up_at[1]
                    self.DGU[to : to + 64, :] = (grad * silu).astype(BF)
            if links:
                links.run(*HIDDEN[k])
        for i in range(3):
            cs = slice(1024 * i, 1024 * i + 1024)
            self.add_term(self.DG, (i,), dot(self.XM[r], self.DGU[cs, :], 1, 1), r)
            if links:
                links.run(*AFTER_GATE[i])
        for i in range(3):
            term = dot(self.WG[i], self.DGU[1024 * i : 1024 * i + 1024, :], 1, 0)
            self.E[...] = term if i == 0 else self.E[...] + term
        if links:
            links.run(*BEFORE_NORM)
        self.norm_back(self.M, r, self.rhoM, self.gainM, 1)

    def attend_back(self, r, links=None):
        self.pack_out()
        self.add_term(self.DO, (slice(None), slice(None)), dot(self.AT[r], self.GLO[0:D, :], 1, 1), r)
        if links:
            links.run(*AFTER_OUT)
        self.E[...] = dot(self.WO[...], self.GLO[0:D, :], 1, 0)
        if links:
            links.run(*BEFORE_HEADS)
        for h in range(NQ):
            rows = slice(H * h, H * h + H)
            do = self.E[rows, :].astype(BF)
            self.DOA[h, 0:H, :] = do
            delta = jnp.sum(do.astype(F32) * self.AT[r, rows, :].astype(F32), axis=0, keepdims=True)
            rows = [jnp.zeros((1, T), F32)] + parts_of(-delta) + [jnp.zeros((12, T), F32)]
            self.DOA[h, H : H + 16, :] = jnp.concatenate(rows, axis=0).astype(BF)
        low, high = slice(0, BLK), slice(BLK, T)
        self.Y[D : D + 2 * NK * H, :] = jnp.zeros((2 * NK * H, T), F32)

        def head(h, carry):
            g = h // GROUP
            allowed = self.diagonal()
            at = pl.ds(pl.multiple_of(h * H, H), H)
            kat = pl.ds(pl.multiple_of(D + g * H, H), H)
            vat = pl.ds(pl.multiple_of(D + NK * H + g * H, H), H)
            q, do = self.QA[r, h], self.DOA[h]
            k0, k1 = self.KTOK[r, g, low, :], self.KTOK[r, g, high, :]
            v0, v1 = self.VTOK[r, g, low, :], self.VTOK[r, g, high, :]
            t0, t1 = self.KT[r, g, :, low], self.KT[r, g, :, high]

            p = jnp.where(allowed, jnp.exp(dot(k0, q[:, low], 1, 0)), 0.0)
            ds = (p * dot(v0, do[:, low], 1, 0)).astype(BF)
            p = p.astype(BF)
            self.Y[at, low] = dot(t0, ds, 1, 0) * SCALE
            dk0 = dot(q[0:H, low], ds, 1, 1)
            dv0 = dot(do[0:H, low], p, 1, 1)

            p = jnp.exp(dot(k0, q[:, high], 1, 0))
            ds = (p * dot(v0, do[:, high], 1, 0)).astype(BF)
            p = p.astype(BF)
            dq = dot(t0, ds, 1, 0)
            dk0 += dot(q[0:H, high], ds, 1, 1)
            dv0 += dot(do[0:H, high], p, 1, 1)

            p = jnp.where(allowed, jnp.exp(dot(k1, q[:, high], 1, 0)), 0.0)
            ds = (p * dot(v1, do[:, high], 1, 0)).astype(BF)
            p = p.astype(BF)
            self.Y[at, high] = (dq + dot(t1, ds, 1, 0)) * SCALE
            self.Y[kat, low] += dk0
            self.Y[vat, low] += dv0
            self.Y[kat, high] += dot(q[0:H, high], ds, 1, 1)
            self.Y[vat, high] += dot(do[0:H, high], p, 1, 1)
            return carry

        for g in range(NK):
            lax.fori_loop(GROUP * g, GROUP * g + GROUP, head, 0)
            if links:
                links.run(*BACK_HEADS[g])

    def project_back(self, r, links=None):
        cos, sin = self.cos[...], self.sin[...]
        for h in range(NQ + NK):
            first, second = slice(H * h, H * h + HALF), slice(H * h + HALF, H * h + H)
            a, b = self.Y[first, :], self.Y[second, :]
            self.Y[first, :] = a * cos + b * sin
            self.Y[second, :] = b * cos - a * sin
        for b in range(NF):
            f = self.order[b]
            rows = jnp.concatenate(
                [
                    self.Y[QB * f : QB * f + QB, :],
                    self.Y[D + KB * f : D + KB * f + KB, :],
                    self.Y[D + NK * H + KB * f : D + NK * H + KB * f + KB, :],
                    jnp.zeros((128 - QB - 2 * KB, T), F32),
                ],
                axis=0,
            )
            self.GLO[128 * b : 128 * b + 128, :] = rows.astype(BF)
        for c in range(2):
            cs = slice(512 * c, 512 * c + 512)
            term = dot(self.XA[r], self.GLO[cs, :], 1, 1)
            if r == 0:
                term = term + dot(self.DO[:, NF * OW :], self.pick[:, cs], 1, 0)
            self.add_term(self.DA, (slice(None), cs), term, r)
        if links:
            links.run(*AFTER_QKV)
        self.E[...] = dot(self.WA[...], self.GLO[...], 1, 0)
        self.norm_back(self.S, r, self.rhoA, self.gainA, 0)

    def write_grad(self):
        for ts in lane_tiles():
            self.gin[:, ts] = self.G[:, ts]

    def small(self):
        valid = self.valid[0:1, :]
        rows = [jnp.sum(self.gacc[i].T, axis=0, keepdims=True) for i in range(2)]
        sums = jnp.sum(jnp.where(valid > 0.0, self.stat[0:6, :], 0.0), axis=1, keepdims=True)
        count = jnp.sum(valid, axis=1, keepdims=True)
        lane = lax.broadcasted_iota(jnp.int32, (6, D), 1)
        return jnp.concatenate(rows + [jnp.where(lane < 128, sums, count)], axis=0)


SCRATCH = dict(
    S=((2, D, T), F32), G=((D, T), F32), E=((D, T), F32), Y=((1536, T), F32),
    XA=((2, D, T), BF), XM=((2, D, T), BF), rhoA=((2, 8, T), F32), rhoM=((2, 8, T), F32),
    QA=((2, NQ, 128, T), BF), KT=((2, NK, H, T), BF), VT=((NK, H, T), BF),
    KTOK=((2, NK, T, 128), BF), VTOK=((2, NK, T, 128), BF), AT=((2, D, T), BF), M=((2, D, T), F32),
    GATE=((2, FF, T), BF), UP=((2, FF, T), BF), HID=((2, FF, T), BF),
    GLD=((D, T), BF), GLO=((1024, T), BF), DGU=((2 * FF, T), BF), DOA=((NQ, 128, T), BF),
    stat=((8, T), F32), valid=((8, T), F32), gacc=((2, D, 128), F32), gainA=((D, 128), F32), gainM=((D, 128), F32), pick=((H, 1024), BF),
)
WEIGHTS = dict(WA=((D, 1024), BF), WO=((D, D), BF), WG=((3, D, 1024), BF), WDT=((D, FF), BF))
GRADS = dict(DA=((D, 1024), BF), DO=((D, D), BF), DG=((3, D, 1024), BF), DD=((D, FF), BF))

def compute_kernel(order, names, *refs):
    w = Work(order, dict(zip(names, refs)))
    w.start()
    w.rest_of_output()
    for r in range(2):
        w.prepare(r)
        w.project(r)
        w.attend(r)
        w.out_project(r)
        w.mlp(r)
    w.write_output()
    for r in (1, 0):
        w.mlp_back(r)
        w.attend_back(r)
        w.project_back(r)
    w.write_grad()
    w.tiny[...] = w.small()


def local_compute(order, x, length, ga, gm, ct, packed):
    cos, sin = rope_tables()
    ins = dict(length=length, x=x, ct=ct, ga=ga[None, :], gm=gm[None, :], cos=jnp.asarray(cos), sin=jnp.asarray(sin), **packed)
    outs = dict(out=((D, T), BF), gin=((D, T), F32), tiny=((8, D), F32), **GRADS)
    names = list(ins) + list(outs) + list(SCRATCH)
    vmem = pl.BlockSpec(memory_space=pltpu.VMEM)
    results = pl.pallas_call(
        functools.partial(compute_kernel, order, names),
        out_shape=[jax.ShapeDtypeStruct(*s) for s in outs.values()],
        in_specs=[pl.BlockSpec(memory_space=pltpu.SMEM)] + [vmem] * (len(ins) - 1),
        out_specs=[vmem] * len(outs),
        scratch_shapes=[pltpu.VMEM(*s) for s in SCRATCH.values()],
        compiler_params=pltpu.CompilerParams(vmem_limit_bytes=VMEM_LIMIT),
    )(*ins.values())
    return dict(zip(outs, results))


def pack(order, q, k, v, o, g, u, d):
    def cols(w, width):
        return w.reshape(w.shape[0], NF, width)[:, np.array(order)]
    ob = cols(o, QB)
    wa = jnp.concatenate([cols(q, QB), cols(k, KB), cols(v, KB), ob[:, :, OW:]], axis=2).reshape(D, 1024)
    wo = jnp.concatenate([ob[:, :, :OW].reshape(D, NF * OW), ob[:, :, OW:].reshape(D, D - NF * OW)], axis=1)
    wg = jnp.concatenate([cols(g, FB), cols(u, FB)], axis=2).reshape(D, NF, 3, 128)
    wg = wg.transpose(2, 0, 1, 3).reshape(3, D, 1024)
    wd = d.T.reshape(NF, QB, FF)[np.array(order)].reshape(D, FF)
    return dict(WA=wa, WO=wo, WG=wg, WDT=wd)


def unpack(order, r):
    back = np.argsort(np.array(order))
    a = r["DA"].astype(F32).reshape(D, NF, 128)[:, back]
    o = r["DO"][:, : NF * OW].astype(F32).reshape(D, NF, OW)[:, back]
    o = jnp.concatenate([o, a[:, :, 120:]], axis=2).reshape(D, D)
    g = r["DG"].astype(F32).reshape(3, D, NF, 128).transpose(1, 2, 0, 3).reshape(D, NF, 2 * FB)[:, back]
    d = r["DD"].astype(F32).reshape(NF, QB, FF)[back].reshape(D, FF).T
    return (
        a[:, :, :QB].reshape(D, D), a[:, :, QB : QB + KB].reshape(D, NK * H), a[:, :, QB + KB : 120].reshape(D, NK * H),
        o, g[:, :, :FB].reshape(D, FF), g[:, :, FB:].reshape(D, FF), d,
    )


PIECES = ("A", "O", "G0", "G1", "G2", "D0", "D1")
DCUT = dict(D0=(0, 256), D1=(256, 128))
MESH = pl.DeviceIdType.MESH


def region(refs, piece, dp, y, z=0, count=4):
    ref, line = refs[piece[0]], 4 * y + z
    if piece[0] == "D":
        first, size = DCUT[piece]
        rows = pl.ds(pl.multiple_of(QB * line, 16), QB * count)
        return ref.at[rows, pl.ds(pl.multiple_of(LANES * dp + first, 128), size)]
    width = OW if piece == "O" else 128
    rows = pl.ds(pl.multiple_of(ROWS * dp, 16), ROWS)
    lanes = pl.ds(pl.multiple_of(width * line, 128), width * count)
    return ref.at[int(piece[1]), rows, lanes] if piece[0] == "G" else ref.at[rows, lanes]


def shape_of(piece, count):
    if piece[0] == "D":
        return (QB * count, DCUT[piece][1])
    return (ROWS, (OW if piece == "O" else 128) * count)


def slip_shape(piece):
    return (QB + 8, DCUT[piece][1]) if piece[0] == "D" else (ROWS, 128)


def cut(piece, line, z):
    if piece == "O":
        return jnp.concatenate([line[:, OW * z : OW * z + OW]] * 2, axis=1)
    return jnp.concatenate([line[QB * z : QB * z + QB], jnp.zeros((8, line.shape[1]), F32)], axis=0)


class Links:
    def __init__(self, refs):
        self.__dict__.update(refs)
        self.weights = dict(A=refs["WA"], O=refs["WO"], G=refs["WG"], D=refs["WDT"])
        self.grads = dict(A=refs["DA"], O=refs["DO"], G=refs["DG"], D=refs["DD"])
        self.dp, f = lax.axis_index("dp"), lax.axis_index("fsdp")
        self.x, self.c = self.dp // 2, lax.rem(self.dp, 2)
        self.z, self.y = f // 2, lax.rem(f, 2)
        self.far = 2 * (1 - self.x) + self.c
        self.other = 2 * self.x + 1 - self.c
        self.sib = (self.other, f)
        self.xn = (self.far, f)
        self.yn = (self.dp, 2 * self.z + 1 - self.y)
        self.peer = [None] + [lax.rem(self.z + k, 4) for k in (1, 2, 3)]
        self.zn = [None] + [(self.dp, 2 * self.peer[k] + self.y) for k in (1, 2, 3)]
        self.copies = {}
        self.used = 0

    def barrier(self):
        sem = pltpu.get_barrier_semaphore()
        partners = [self.sib, self.xn, self.yn] + self.zn[1:]
        for device in partners:
            pl.semaphore_signal(sem, inc=1, device_id=device, device_id_type=MESH)
        pl.semaphore_wait(sem, len(partners))

    def send(self, name, src, dst, device):
        copy = pltpu.make_async_remote_copy(
            src_ref=src,
            dst_ref=dst,
            send_sem=self.sent.at[self.used],
            recv_sem=self.came.at[self.used],
            device_id=device,
            device_id_type=MESH,
        )
        self.used += 1
        copy.start()
        self.copies[name] = copy

    def arrived(self, *names):
        for name in names:
            self.copies[name].wait_recv()

    def finish(self):
        for copy in self.copies.values():
            copy.wait_send()

    def run(self, *steps):
        for step in steps:
            kind, piece = step.split()
            getattr(self, kind)(piece)


    def spread(self, tag, p, device, dp=None, y=None, z=0, count=4):
        block = region(self.weights, p, self.dp if dp is None else dp, self.y if y is None else y, z, count)
        self.send(("w", p, tag), block, block, device)

    def share(self, p):
        for k in (1, 3, 2):
            if p[0] in "OD":
                block = getattr(self, "slip" + p).at[self.z]
                self.send(("w", p, f"z{k}"), block, block, self.zn[k])
            else:
                self.spread(f"z{k}", p, self.zn[k], z=self.z, count=1)

    def line(self, p):
        self.arrived(*[("w", p, f"z{k}") for k in (1, 2, 3)])
        if p[0] in "OD":
            slips = [getattr(self, "slip" + p)[z].astype(F32) for z in range(4)]
            if p == "O":
                whole = jnp.concatenate([slip[:, :OW] for slip in slips], axis=1)
            else:
                whole = jnp.concatenate([slip[:QB] for slip in slips], axis=0)
            region(self.weights, p, self.dp, self.y)[...] = whole.astype(BF)
        self.spread("x", p, self.xn)
        self.spread("y", p, self.yn)
        self.spread("s", p, self.sib)

    def cross(self, p):
        self.arrived(("w", p, "x"))
        self.spread("xy", p, self.yn, dp=self.far, count=2)
        self.spread("sx", p, self.sib, dp=self.far)
        self.arrived(("w", p, "y"))
        self.spread("yx", p, self.xn, y=1 - self.y, z=2, count=2)
        self.spread("sy", p, self.sib, y=1 - self.y)

    def rest(self, p):
        self.arrived(("w", p, "xy"))
        self.spread("sxy", p, self.sib, dp=self.far, y=1 - self.y, count=2)
        self.arrived(("w", p, "yx"))
        self.spread("syx", p, self.sib, dp=self.far, y=1 - self.y, z=2, count=2)

    def end(self, p):
        self.arrived(*[("w", p, tag) for tag in ("s", "sx", "sy", "sxy", "syx")])


    def term(self, p, dp, y, z=0, count=4):
        return region(self.grads, p, dp, y, z, count)

    def add(self, p, dp, y, z, count, came):
        at = self.term(p, dp, y, z, count)
        at[...] = at[...] + came[...]

    def sibs(self, p):
        room = getattr(self, "one" + p)
        for i in range(2):
            for y in range(2):
                dp = 2 * i + 1 - self.c
                self.send(("g", p, "s", i, y), self.term(p, dp, y), room.at[i, y], self.sib)

    def pair(self, p):
        room = getattr(self, "one" + p)
        for i in range(2):
            for y in range(2):
                self.arrived(("g", p, "s", i, y))
                self.add(p, 2 * i + self.c, y, 0, 4, room.at[i, y])
        ups, across = getattr(self, "twoy" + p), getattr(self, "twox" + p)
        for i, dp in enumerate((self.dp, self.far)):
            self.send(("g", p, "y", i), self.term(p, dp, 1 - self.y, 0, 2), ups.at[i], self.yn)
        for j, y in enumerate((self.y, 1 - self.y)):
            self.send(("g", p, "x", j), self.term(p, self.far, y, 2, 2), across.at[j], self.xn)

    def twos(self, p):
        ups, across = getattr(self, "twoy" + p), getattr(self, "twox" + p)
        for i in (1, 0):
            self.arrived(("g", p, "y", i))
            self.add(p, (self.dp, self.far)[i], self.y, 0, 2, ups.at[i])
            if i == 1:
                self.send(("g", p, "yx"), self.term(p, self.far, self.y, 0, 2), getattr(self, "threex" + p), self.xn)
        for j in (1, 0):
            self.arrived(("g", p, "x", j))
            self.add(p, self.dp, (self.y, 1 - self.y)[j], 2, 2, across.at[j])
            if j == 1:
                self.send(("g", p, "xy"), self.term(p, self.dp, 1 - self.y, 2, 2), getattr(self, "threey" + p), self.yn)

    def fours(self, p):
        self.arrived(("g", p, "yx"))
        self.add(p, self.dp, self.y, 0, 2, getattr(self, "threex" + p))
        self.arrived(("g", p, "xy"))
        self.add(p, self.dp, self.y, 2, 2, getattr(self, "threey" + p))
        if p[0] in "OD":
            line = self.term(p, self.dp, self.y)[...].astype(F32)
            for z in range(4):
                getattr(self, "part" + p)[z] = cut(p, line, z).astype(BF)
        for k in (1, 3, 2):
            src = getattr(self, "part" + p).at[self.peer[k]] if p[0] in "OD" else self.term(p, self.dp, self.y, self.peer[k], 1)
            self.send(("g", p, "z", k), src, getattr(self, "four" + p).at[k - 1], self.zn[k])

    def total(self, p):
        own = getattr(self, "part" + p)[self.z] if p[0] in "OD" else self.term(p, self.dp, self.y, self.z, 1)[...]
        total = own.astype(F32)
        for k in (1, 2, 3):
            self.arrived(("g", p, "z", k))
            total = total + getattr(self, "four" + p)[k - 1].astype(F32)
        if p[0] == "D":
            first, size = DCUT[p]
            self.sumD[:, first : first + size] = total[:QB, :]
        else:
            at = 128 * ("A", "O", "G0", "G1", "G2").index(p)
            self.sumN[:, at : at + 128] = total


    def tiny(self, step):
        step = int(step)
        if step > 0:
            self.arrived(("t", step - 1))
            self.tinies[step] = self.tinies[step - 1] + self.tinyin[step - 1]
        if step < 3:
            self.send(("t", step), self.tinies.at[step], self.tinyin.at[step], (self.sib, self.xn, self.yn)[step])
        else:
            for k in (1, 2, 3):
                self.send(("t", step, k), self.tinies.at[3], self.tinyz.at[k], self.zn[k])

    def tiny_end(self):
        self.tinyz[0] = self.tinies[3]
        for k in (1, 2, 3):
            self.arrived(("t", 3, k))
        total = None
        for z in range(4):
            term = self.tinyz[lax.rem(self.z - z + 4, 4)]
            total = term if total is None else total + term
        self.sumT[...] = total


def rooms():
    shapes = {}
    for p in PIECES:
        shapes["one" + p] = ((2, 2) + shape_of(p, 4), BF)
        for room in ("twoy", "twox"):
            shapes[room + p] = ((2,) + shape_of(p, 2), BF)
        for room in ("threex", "threey"):
            shapes[room + p] = (shape_of(p, 2), BF)
        shapes["four" + p] = ((3,) + slip_shape(p), BF)
        if p[0] in "OD":
            shapes["slip" + p] = ((4,) + slip_shape(p), BF)
            shapes["part" + p] = ((4,) + slip_shape(p), BF)
    shapes["tinies"] = ((4, 8, D), F32)
    shapes["tinyin"] = ((3, 8, D), F32)
    shapes["tinyz"] = ((4, 8, D), F32)
    return shapes


COPIES = len(PIECES) * (12 + 13) + 6


def pack_own(links, refs):
    rows = lambda *names: [refs[n][...].astype(F32) for n in names]
    q, k, v, o, g, u, d = rows("q", "k", "v", "o", "g", "u", "d")
    gu = jnp.concatenate([g, u], axis=1)
    whole = dict(A=jnp.concatenate([q, k.T, v.T, o[:, OW:]], axis=1), G0=gu[:, :128], G1=gu[:, 128:256], G2=gu[:, 256:])
    for p in PIECES:
        if p == "O":
            links.slipO[links.z] = cut(p, o, 0).astype(BF)
        elif p[0] == "D":
            first, size = DCUT[p]
            getattr(links, "slip" + p)[links.z] = cut(p, d[:, first : first + size], 0).astype(BF)
        else:
            region(links.weights, p, links.dp, links.y, links.z, 1)[...] = whole[p].astype(BF)


BEGIN = ("share A", "share O", "share G0", "share G1", "share G2", "share D0", "share D1")
BEFORE_PROJECT = ("line A", "line O", "cross A", "line G0", "cross O", "rest A", "line G1", "end A")
AFTER_PROJECT = ("cross G0", "rest O", "line G2")
HEADS = (("cross G1", "rest G0"), ("line D0",), ("cross G2", "rest G1"))
BEFORE_OUT = ("end O", "line D1")
BEFORE_MLP = ("cross D0", "rest G2", "end G0", "end G1", "end G2")
MLP = (("cross D1", "rest D0"), ("rest D1", "end D0", "end D1"))
AFTER_DOWN = ("sibs D0", "sibs D1")
HIDDEN = (("pair D0",), ("pair D1",), (), ("twos D0",))
AFTER_GATE = (("sibs G0", "twos D1"), ("sibs G1", "pair G0", "fours D0"), ("sibs G2", "pair G1", "fours D1"))
BEFORE_NORM = ("pair G2",)
AFTER_OUT = ("sibs O", "twos G0")
BEFORE_HEADS = ("pair O",)
BACK_HEADS = (("twos G1", "fours G0"), ("twos G2", "fours G1"), ("twos O", "fours G2"))
AFTER_QKV = ("sibs A", "fours O")
LAST = ("tiny 0", "pair A", "tiny 1", "twos A", "tiny 2")
VERY_LAST = ("total D0", "total D1", "total G0", "total G1", "total G2", "fours A", "tiny 3", "total O", "total A")


def whole_kernel(order, names, *args):
    refs = dict(zip(names, args))
    w, links = Work(order, refs), Links(refs)
    links.barrier()
    pack_own(links, refs)
    links.run(*BEGIN)
    w.start()
    w.prepare(0)
    links.run(*BEFORE_PROJECT)
    w.project(0)
    links.run(*AFTER_PROJECT)
    w.attend(0, links)
    w.rest_of_output()
    links.run(*BEFORE_OUT)
    w.out_project(0)
    links.run(*BEFORE_MLP)
    w.mlp(0, links)
    w.prepare(1)
    w.project(1)
    w.attend(1)
    w.out_project(1)
    w.mlp(1)
    w.write_output()
    w.mlp_back(1)
    w.attend_back(1)
    w.project_back(1)
    w.mlp_back(0, links)
    w.attend_back(0, links)
    w.project_back(0, links)
    links.tinies[0] = w.small()
    links.run(*LAST)
    w.write_grad()
    links.run(*VERY_LAST)
    links.tiny_end()
    links.finish()


def finish_kernel(*refs):
    out, gin, sums, sumd, tiny, oout, ogin, ga, q, k, v, o, gm, g, u, d, rms = refs
    oout[...] = out[...]
    ogin[...] = gin[...]
    q[...] = sums[:, :QB]
    k[...] = sums[:, QB : QB + KB].T
    v[...] = sums[:, QB + KB : 120].T
    o[...] = jnp.concatenate([sums[:, 128 : 128 + OW], sums[:, 120:128]], axis=1)
    g[...] = sums[:, 256 : 256 + FB]
    u[...] = sums[:, 256 + FB : 256 + 2 * FB]
    d[...] = sumd[...]
    ga[...] = tiny[0:1, :]
    gm[...] = tiny[1:2, :]
    lane = lax.broadcasted_iota(jnp.int32, (1, 3), 1)
    for r in range(2):
        first, second, third = [tiny[2 + 3 * r + i : 3 + 3 * r + i, 0:3] for i in range(3)]
        squares = jnp.where(lane == 0, first, jnp.where(lane == 1, second, third))
        rms[r : r + 1, :] = jnp.sqrt(squares / (tiny[2:3, 128:131] * D))


def whole(x, length, ga, q, k, v, o, gm, g, u, d, ct):
    order = [2 * (b % 4) + b // 4 for b in range(NF)]
    cos, sin = rope_tables()
    ins = dict(
        length=length, x=x[0].T, ct=ct[0].T, ga=ga[None, :], gm=gm[None, :], cos=jnp.asarray(cos), sin=jnp.asarray(sin),
        q=q, k=k.T, v=v.T, o=o, g=g, u=u, d=d.T,
    )
    outs = dict(
        out=((D, T), BF), gin=((D, T), F32), sumN=((ROWS, 256 + 2 * FB), F32), sumD=((QB, LANES), F32), sumT=((8, D), F32)
    )
    scratch = dict(SCRATCH, **WEIGHTS, **GRADS, **rooms())
    names = list(ins) + list(outs) + list(scratch) + ["sent", "came"]
    vmem = pl.BlockSpec(memory_space=pltpu.VMEM)
    r = pl.pallas_call(
        functools.partial(whole_kernel, order, names),
        out_shape=[jax.ShapeDtypeStruct(*s) for s in outs.values()],
        in_specs=[pl.BlockSpec(memory_space=pltpu.SMEM)] + [vmem] * (len(ins) - 1),
        out_specs=[vmem] * len(outs),
        scratch_shapes=[pltpu.VMEM(*s) for s in scratch.values()]
        + [pltpu.SemaphoreType.DMA((COPIES,)), pltpu.SemaphoreType.DMA((COPIES,))],
        compiler_params=pltpu.CompilerParams(
            vmem_limit_bytes=VMEM_LIMIT, collective_id=0, has_side_effects=True
        ),
    )(*ins.values())
    rows = [
        ((D, T), BF), ((D, T), F32), ((1, D), F32), (q.shape, F32), (k.shape[::-1], F32), (v.shape[::-1], F32),
        (o.shape, F32), ((1, D), F32), (g.shape, F32), (u.shape, F32), (d.shape[::-1], F32), ((2, 3), F32),
    ]
    out, gin, ga, q, k, v, o, gm, g, u, d, rms = pl.pallas_call(
        finish_kernel,
        out_shape=[jax.ShapeDtypeStruct(*s) for s in rows],
        in_specs=[vmem] * len(outs),
        out_specs=[vmem] * len(rows),
    )(*r)
    return out.T[None], gin.T[None], ga[0], q, k.T, v.T, o, gm[0], g, u, d.T, rms


def by_collectives(x, length, ga, q, k, v, o, gm, g, u, d, ct):
    order = list(range(NF))
    full = [lax.all_gather(lax.all_gather(w, "fsdp", axis=1, tiled=True), "dp", axis=0, tiled=True) for w in (q, k, v, o, g, u, d)]
    packed = pack(order, *full)
    results = [local_compute(order, x[i].T, length[i : i + 1], ga, gm, ct[i].T, packed) for i in range(x.shape[0])]
    out = jnp.stack([r["out"].T for r in results])
    gin = jnp.stack([r["gin"].T for r in results])
    tiny = lax.psum(sum(r["tiny"] for r in results), ("dp", "fsdp"))
    terms = [unpack(order, r) for r in results]
    grads = [
        lax.psum_scatter(
            lax.psum_scatter(sum(t), "dp", scatter_dimension=0, tiled=True), "fsdp", scatter_dimension=1, tiled=True
        )
        for t in zip(*terms)
    ]
    rms = jnp.sqrt(tiny[2:8, 0].reshape(2, 3) / (tiny[2, 128] * D))
    gq, gk, gv, go, gg, gu, gd = grads
    return out, gin, tiny[0], gq, gk, gv, go, tiny[1], gg, gu, gd, rms


def solution(mesh):
    blocks = P("dp", "fsdp")
    slots = P(("dp", "fsdp"), None, None)
    in_specs = (slots, P(("dp", "fsdp")), P(), blocks, blocks, blocks, blocks, P(), blocks, blocks, blocks, slots)
    out_specs = (slots, slots, P(), blocks, blocks, blocks, blocks, P(), blocks, blocks, blocks, P())

    def on_device(*args):
        fits = mesh.shape["dp"] == 4 and mesh.shape["fsdp"] == 8 and args[0].shape[0] == 1
        return (whole if fits else by_collectives)(*args)

    return jax.shard_map(on_device, mesh=mesh, in_specs=in_specs, out_specs=out_specs, check_vma=False)
```

```python
import functools
import jax
import jax.numpy as jnp
import numpy as np
from jax import lax
from jax.experimental import pallas as pl
from jax.experimental.pallas import tpu as pltpu
from jax.sharding import PartitionSpec as P

D = 576
NQ = 9
NK = 3
GROUP = NQ // NK
H = 64
HALF = H // 2
FF = 1536
T = 512
NF = 8
QB = D // NF
KB = NK * H // NF
FB = FF // NF
EPS = 1e-05
ROPE_BASE = 10000.0
SCALE = H ** (-0.5)
NEG = -1e30
BLK = 256
VMEM_LIMIT = 63 * 2**20
ROWS = D // 4
LANES = FF // 4
OW = QB - 8
BF = jnp.bfloat16
F32 = jnp.float32


def dot(a, b, ca, cb):
    return lax.dot_general(a, b, (((ca,), (cb,)), ((), ())), preferred_element_type=F32)


def rope_tables():
    inverse = ROPE_BASE ** (-(2.0 * np.arange(HALF, dtype=np.float64)) / H)
    angles = inverse[:, None] * np.arange(T, dtype=np.float64)[None, :]
    return np.cos(angles).astype(np.float32), np.sin(angles).astype(np.float32)


def parts_of(row):
    hi = row.astype(BF).astype(F32)
    rest = row - hi
    mid = rest.astype(BF).astype(F32)
    return [hi, mid, rest - mid]


def lane_tiles():
    return [slice(128 * i, 128 * i + 128) for i in range(T // 128)]


class Work:
    def __init__(self, order, refs):
        self.order = order
        self.__dict__.update(refs)

    def start(self):
        count = self.length[0]
        place = lax.broadcasted_iota(jnp.int32, (8, T), 1)
        valid = (place < count).astype(F32)
        self.valid[...] = valid
        for ts in lane_tiles():
            self.S[0, :, ts] = self.x[:, ts].astype(F32)
            self.G[:, ts] = jnp.where(valid[0:1, ts] > 0.0, self.ct[:, ts].astype(F32), 0.0)
        self.gainA[...] = jnp.broadcast_to(self.ga[...].reshape(1, D), (128, D)).T
        self.gainM[...] = jnp.broadcast_to(self.gm[...].reshape(1, D), (128, D)).T
        row = lax.broadcasted_iota(jnp.int32, (H, 1024), 0)
        lane = lax.broadcasted_iota(jnp.int32, (H, 1024), 1)
        self.pick[...] = jnp.where(lane == 128 * (row // 8) + 120 + lax.rem(row, 8), 1.0, 0.0).astype(BF)
        self.gacc[...] = jnp.zeros_like(self.gacc)
        def blank(h, carry):
            self.QA[0, h, H:, :] = jnp.zeros((H, T), BF)
            self.QA[1, h, H:, :] = jnp.zeros((H, T), BF)
            self.DOA[h, H:, :] = jnp.zeros((H, T), BF)
            return carry

        lax.fori_loop(0, NQ, blank, 0)

        def clear(i, carry):
            rows = pl.ds(pl.multiple_of(i * 64, 64), 64)
            self.DA[rows, :] = jnp.zeros((64, 1024), BF)
            self.DO[rows, :] = jnp.zeros((64, D), BF)
            self.DD[rows, :] = jnp.zeros((64, FF), BF)
            for k in range(3):
                self.DG[k, rows, :] = jnp.zeros((64, 1024), BF)
            return carry

        lax.fori_loop(0, D // 64, clear, 0)

    def norm(self, src, r, gain, dst, rho_ref, row):
        for ts in lane_tiles():
            v = src[r, :, ts]
            total = jnp.sum(v * v, axis=0, keepdims=True)
            if row is not None:
                self.stat[r, row : row + 1, ts] = total
            rho = lax.rsqrt(total * (1.0 / D) + EPS)
            rho_ref[r, 0:1, ts] = rho
            dst[r, :, ts] = (v * rho * gain[...]).astype(BF)

    def natural_rows(self, ref, base, width, first, count):
        pieces = []
        row = first
        while row < first + count:
            f, i = row // width, row % width
            n = min(width - i, first + count - row)
            at = 128 * self.order.index(f) + base + i
            pieces.append(ref[at : at + n, :])
            row += n
        return pieces[0] if len(pieces) == 1 else jnp.concatenate(pieces, axis=0)

    def prepare(self, r):
        self.norm(self.S, r, self.gainA, self.XA, self.rhoA, 0)

    def project(self, r):
        def part(c, carry):
            cs = pl.ds(pl.multiple_of(512 * c, 512), 512)
            self.Y[cs, :] = dot(self.WA[:, cs], self.XA[r], 0, 0)
            return carry

        for c in range(2):
            part(c, 0)
        cos, sin = self.cos[...], self.sin[...]
        one = jnp.ones((1, T), F32)
        place = lax.broadcasted_iota(jnp.int32, (1, T), 1)
        bias = jnp.where(place < self.length[0], 0.0, NEG)
        for h in range(NQ + NK):
            base, width, at = (0, QB, h) if h < NQ else (QB, KB, h - NQ)
            a = self.natural_rows(self.Y, base, width, H * at, HALF)
            b = self.natural_rows(self.Y, base, width, H * at + HALF, HALF)
            first, second = a * cos - b * sin, b * cos + a * sin
            if h < NQ:
                self.QA[r, h, 0:HALF, :] = (first * SCALE).astype(BF)
                self.QA[r, h, HALF:H, :] = (second * SCALE).astype(BF)
                self.QA[r, h, H : H + 16, :] = jnp.concatenate([one, jnp.zeros((15, T), F32)], axis=0).astype(BF)
            else:
                g = h - NQ
                key = jnp.concatenate([first, second], axis=0)
                self.KT[r, g] = key.astype(BF)
                v = jnp.concatenate(
                    [
                        self.natural_rows(self.Y, QB + KB, KB, H * g, HALF),
                        self.natural_rows(self.Y, QB + KB, KB, H * g + HALF, HALF),
                    ],
                    axis=0,
                )
                self.VT[g] = v.astype(BF)
                ones3 = jnp.ones((3, T), F32)
                tail = jnp.zeros((H - 4, T), F32)
                ktall = jnp.concatenate([key, bias, ones3, tail], axis=0)
                vtall = jnp.concatenate([v, jnp.zeros((1, T), F32), ones3, tail], axis=0)
                for ts in lane_tiles():
                    self.KTOK[r, g, ts, :] = ktall[:, ts].T.astype(BF)
                    self.VTOK[r, g, ts, :] = vtall[:, ts].T.astype(BF)

    def diagonal(self):
        key = lax.broadcasted_iota(jnp.int32, (BLK, BLK), 0)
        query = lax.broadcasted_iota(jnp.int32, (BLK, BLK), 1)
        return key <= query

    def attend(self, r, links):
        low, high = slice(0, BLK), slice(BLK, T)

        def head(h, carry):
            g = h // GROUP
            allowed = self.diagonal()
            at = pl.ds(pl.multiple_of(h * H, H), H)
            s = dot(self.KTOK[r, g, low, :], self.QA[r, h, :, low], 1, 0)
            s = jnp.where(allowed, s, NEG)
            top = jnp.max(s, axis=0, keepdims=True)
            p = jnp.exp(s - top)
            total = jnp.sum(p, axis=0, keepdims=True)
            o = dot(self.VT[g, :, low], p.astype(BF), 1, 0)
            self.AT[r, at, low] = (o * (1.0 / total)).astype(BF)
            lse0 = top + jnp.log(total)
            s0 = dot(self.KTOK[r, g, low, :], self.QA[r, h, :, high], 1, 0)
            s1 = dot(self.KTOK[r, g, high, :], self.QA[r, h, :, high], 1, 0)
            s1 = jnp.where(allowed, s1, NEG)
            top = jnp.maximum(jnp.max(s0, axis=0, keepdims=True), jnp.max(s1, axis=0, keepdims=True))
            p0 = jnp.exp(s0 - top)
            p1 = jnp.exp(s1 - top)
            total = jnp.sum(p0, axis=0, keepdims=True) + jnp.sum(p1, axis=0, keepdims=True)
            o = dot(self.VT[g, :, low], p0.astype(BF), 1, 0) + dot(self.VT[g, :, high], p1.astype(BF), 1, 0)
            self.AT[r, at, high] = (o * (1.0 / total)).astype(BF)
            lse1 = top + jnp.log(total)
            lse = jnp.concatenate([lse0, lse1], axis=1)
            rows = [jnp.ones((1, T), F32)] + parts_of(-lse) + [jnp.zeros((12, T), F32)]
            self.QA[r, h, H : H + 16, :] = jnp.concatenate(rows, axis=0).astype(BF)
            return carry

        def group(g, carry):
            lax.fori_loop(0, GROUP, lambda k, c: head(GROUP * g + k, c), 0, unroll=True)
            for k in range(NK):
                links.run_if((r == 0) & (g == k), HEADS[k])
            return carry

        lax.fori_loop(0, NK, group, 0)

    def rest_of_output(self):
        self.WO[:, NF * OW :] = dot(self.WA[...], self.pick[...], 1, 1).astype(BF)

    def after(self, value, src, r, dst, to, row, squares):
        n = value.shape[0]
        dst[to, row : row + n, :] = src[r, row : row + n, :] + value
        for i in range(n // 8):
            part = value[8 * i : 8 * i + 8]
            squares = squares + part * part
        return squares

    def out_project(self, r):
        self.Y[0:D, :] = dot(self.WO[...], self.AT[r], 0, 0)
        squares = jnp.zeros((8, T), F32)
        for b in range(NF):
            f = self.order[b]
            squares = self.after(self.Y[OW * b : OW * b + OW, :], self.S, r, self.M, r, QB * f, squares)
            at = NF * OW + 8 * b
            squares = self.after(self.Y[at : at + 8, :], self.S, r, self.M, r, QB * f + OW, squares)
        self.stat[r, 1:2, :] = jnp.sum(squares, axis=0, keepdims=True)

    def mlp(self, r, links):
        self.norm(self.M, r, self.gainM, self.XM, self.rhoM, None)

        def half(y, carry):
            cs = pl.ds(pl.multiple_of(512 * y, 512), 512)

            def part(i, carry):
                to = pl.ds(pl.multiple_of(512 * i, 512), 512)
                self.Y[to, :] = dot(self.WG[i, :, cs], self.XM[r], 0, 0)
                return carry

            for i in range(3):
                part(i, 0)

            def block(z, carry):
                f = self.natural(y, z)
                for j in range(3):
                    gate_at, up_at = self.places(j)
                    gate = self.Y[pl.ds(pl.multiple_of(gate_at[0] * 512 + 128 * z + gate_at[1], 64), 64), :]
                    up = self.Y[pl.ds(pl.multiple_of(up_at[0] * 512 + 128 * z + up_at[1], 64), 64), :]
                    rows = pl.ds(pl.multiple_of(FB * f + 64 * j, 64), 64)
                    self.GATE[r, rows, :] = gate.astype(BF)
                    self.UP[r, rows, :] = up.astype(BF)
                    self.HID[r, rows, :] = (gate * jax.nn.sigmoid(gate) * up).astype(BF)
                return carry

            for z in range(4):
                block(z, 0)
            links.run_if(r == 0, MLP[y])
            return carry

        for y in range(2):
            half(y, 0)
        self.Y[0:D, :] = dot(self.WDT[...], self.HID[r], 1, 0)
        squares = jnp.zeros((8, T), F32)
        for b in range(NF):
            squares = self.after(self.Y[QB * b : QB * b + QB, :], self.M, r, self.S, r + 1, QB * self.order[b], squares)
        self.stat[r, 2:3, :] = jnp.sum(squares, axis=0, keepdims=True)

    def natural(self, y, z):
        return 2 * z + y if self.order[1] == 2 else 4 * y + z

    def places(self, j):
        return ((0, 0), (0, 64), (1, 0))[j], ((1, 64), (2, 0), (2, 64))[j]

    def write_output(self):
        valid = self.valid[0:1, :]
        for ts in lane_tiles():
            v = jnp.where(valid[:, ts] > 0.0, self.S[2, :, ts], 0.0)
            self.out[:, ts] = v.astype(BF)

    def pack_down(self):
        for k in range(NF // 2):
            rows = [self.G[QB * self.order[b] : QB * self.order[b] + QB, :] for b in (2 * k, 2 * k + 1)]
            self.GLD[2 * QB * k : 2 * QB * k + 2 * QB, :] = jnp.concatenate(rows, axis=0).astype(BF)

    def pack_out(self):
        tails = []
        for b in range(NF):
            at = QB * self.order[b]
            self.GLO[OW * b : OW * b + OW, :] = self.G[at : at + OW, :].astype(BF)
            tails.append(self.G[at + OW : at + QB, :])
        self.GLO[NF * OW : D, :] = jnp.concatenate(tails, axis=0).astype(BF)

    def add_term(self, dst, index, value):
        dst[index] = (value + dst[index].astype(F32)).astype(dst.dtype)

    def norm_back(self, src, r, rho_ref, gain, slot):
        for ts in lane_tiles():
            e, v, rho = self.E[:, ts], src[r, :, ts], rho_ref[r, 0:1, ts]
            u = e * gain[...]
            mean = jnp.sum(u * v, axis=0, keepdims=True) * (1.0 / D)
            self.gacc[slot] += e * (v * rho)
            self.G[:, ts] = self.G[:, ts] + rho * (u - v * (rho * rho * mean))

    def mlp_back(self, r, links):
        self.pack_down()
        for c in range(2):
            cs = slice(768 * c, 768 * c + 768)
            self.add_term(self.DD, (slice(None), cs), dot(self.GLD[...], self.HID[r, cs, :], 1, 1))
        links.run_if(r == 0, AFTER_DOWN)

        def hidden(k, carry):
            rows = pl.ds(pl.multiple_of(2 * FB * k, 128), 2 * FB)
            self.Y[0 : 2 * FB, :] = dot(self.WDT[:, rows], self.GLD[...], 0, 0)
            for m in range(2):
                f = 2 * k + m
                b = k + 4 * m if self.order[1] == 2 else f
                for j in range(3):
                    at = pl.ds(pl.multiple_of(FB * f + 64 * j, 64), 64)
                    grad = self.Y[FB * m + 64 * j : FB * m + 64 * j + 64, :]
                    gate = self.GATE[r, at, :].astype(F32)
                    up = self.UP[r, at, :].astype(F32)
                    sig = jax.nn.sigmoid(gate)
                    silu = gate * sig
                    gate_at, up_at = self.places(j)
                    to = pl.ds(pl.multiple_of(1024 * gate_at[0] + 128 * b + gate_at[1], 64), 64)
                    self.DGU[to, :] = (grad * up * (sig + silu * (1.0 - sig))).astype(BF)
                    to = pl.ds(pl.multiple_of(1024 * up_at[0] + 128 * b + up_at[1], 64), 64)
                    self.DGU[to, :] = (grad * silu).astype(BF)
            links.run_if(r == 0, HIDDEN[k])
            return carry

        for k in range(4):
            hidden(k, 0)

        def matrix(i, carry):
            grad = self.DGU[pl.ds(pl.multiple_of(1024 * i, 1024), 1024), :]
            self.add_term(self.DG, (i,), dot(self.XM[r], grad, 1, 1))
            links.run_if(r == 0, AFTER_GATE[i])
            return carry

        for i in range(3):
            matrix(i, 0)
        self.E[...] = dot(self.WG[0], self.DGU[0:1024, :], 1, 0)

        def back(i, carry):
            grad = self.DGU[pl.ds(pl.multiple_of(1024 * i, 1024), 1024), :]
            self.E[...] = self.E[...] + dot(self.WG[i], grad, 1, 0)
            return carry

        for i in (1, 2):
            back(i, 0)
        links.run_if(r == 0, BEFORE_NORM)
        self.norm_back(self.M, r, self.rhoM, self.gainM, 1)

    def attend_back(self, r, links):
        self.pack_out()
        term = dot(self.AT[r], self.GLO[0:D, :], 1, 1)
        self.add_term(self.DO, (slice(None), slice(0, NF * OW)), term[:, : NF * OW])
        self.DO[:, NF * OW :] = term[:, NF * OW :].astype(BF)
        links.run_if(r == 0, AFTER_OUT)
        self.E[...] = dot(self.WO[...], self.GLO[0:D, :], 1, 0)
        links.run_if(r == 0, BEFORE_HEADS)
        for h in range(NQ):
            rows = slice(H * h, H * h + H)
            do = self.E[rows, :].astype(BF)
            self.DOA[h, 0:H, :] = do
            delta = jnp.sum(do.astype(F32) * self.AT[r, rows, :].astype(F32), axis=0, keepdims=True)
            rows = [jnp.zeros((1, T), F32)] + parts_of(-delta) + [jnp.zeros((12, T), F32)]
            self.DOA[h, H : H + 16, :] = jnp.concatenate(rows, axis=0).astype(BF)
        low, high = slice(0, BLK), slice(BLK, T)
        self.Y[D : D + 2 * NK * H, :] = jnp.zeros((2 * NK * H, T), F32)

        def head(h, carry):
            g = h // GROUP
            allowed = self.diagonal()
            at = pl.ds(pl.multiple_of(h * H, H), H)
            kat = pl.ds(pl.multiple_of(D + g * H, H), H)
            vat = pl.ds(pl.multiple_of(D + NK * H + g * H, H), H)
            q, do = self.QA[r, h], self.DOA[h]
            k0, k1 = self.KTOK[r, g, low, :], self.KTOK[r, g, high, :]
            v0, v1 = self.VTOK[r, g, low, :], self.VTOK[r, g, high, :]
            t0, t1 = self.KT[r, g, :, low], self.KT[r, g, :, high]

            p = jnp.where(allowed, jnp.exp(dot(k0, q[:, low], 1, 0)), 0.0)
            ds = (p * dot(v0, do[:, low], 1, 0)).astype(BF)
            p = p.astype(BF)
            self.Y[at, low] = dot(t0, ds, 1, 0) * SCALE
            dk0 = dot(q[0:H, low], ds, 1, 1)
            dv0 = dot(do[0:H, low], p, 1, 1)

            p = jnp.exp(dot(k0, q[:, high], 1, 0))
            ds = (p * dot(v0, do[:, high], 1, 0)).astype(BF)
            p = p.astype(BF)
            dq = dot(t0, ds, 1, 0)
            dk0 += dot(q[0:H, high], ds, 1, 1)
            dv0 += dot(do[0:H, high], p, 1, 1)

            p = jnp.where(allowed, jnp.exp(dot(k1, q[:, high], 1, 0)), 0.0)
            ds = (p * dot(v1, do[:, high], 1, 0)).astype(BF)
            p = p.astype(BF)
            self.Y[at, high] = (dq + dot(t1, ds, 1, 0)) * SCALE
            self.Y[kat, low] += dk0
            self.Y[vat, low] += dv0
            self.Y[kat, high] += dot(q[0:H, high], ds, 1, 1)
            self.Y[vat, high] += dot(do[0:H, high], p, 1, 1)
            return carry

        def group(g, carry):
            lax.fori_loop(0, GROUP, lambda k, c: head(GROUP * g + k, c), 0, unroll=True)
            for k in range(NK):
                links.run_if((r == 0) & (g == k), BACK_HEADS[k])
            return carry

        lax.fori_loop(0, NK, group, 0)

    def project_back(self, r, links):
        cos, sin = self.cos[...], self.sin[...]
        for h in range(NQ + NK):
            first, second = slice(H * h, H * h + HALF), slice(H * h + HALF, H * h + H)
            a, b = self.Y[first, :], self.Y[second, :]
            self.Y[first, :] = a * cos + b * sin
            self.Y[second, :] = b * cos - a * sin
        for b in range(NF):
            f = self.order[b]
            rows = jnp.concatenate(
                [
                    self.Y[QB * f : QB * f + QB, :],
                    self.Y[D + KB * f : D + KB * f + KB, :],
                    self.Y[D + NK * H + KB * f : D + NK * H + KB * f + KB, :],
                    jnp.zeros((128 - QB - 2 * KB, T), F32),
                ],
                axis=0,
            )
            self.GLO[128 * b : 128 * b + 128, :] = rows.astype(BF)
        def part(c, carry):
            cs = pl.ds(pl.multiple_of(512 * c, 512), 512)
            term = dot(self.XA[r], self.GLO[cs, :], 1, 1) + dot(self.DO[:, NF * OW :], self.pick[:, cs], 1, 0)
            self.add_term(self.DA, (slice(None), cs), term)
            return carry

        for c in range(2):
            part(c, 0)
        links.run_if(r == 0, AFTER_QKV)
        self.E[...] = dot(self.WA[...], self.GLO[...], 1, 0)
        self.norm_back(self.S, r, self.rhoA, self.gainA, 0)

    def write_grad(self):
        for ts in lane_tiles():
            self.gin[:, ts] = self.G[:, ts]

    def small(self):
        valid = self.valid[0:1, :]
        rows = [jnp.sum(self.gacc[i].T, axis=0, keepdims=True) for i in range(2)]
        sums = jnp.sum(jnp.where(valid > 0.0, jnp.concatenate([self.stat[0, 0:3], self.stat[1, 0:3]], axis=0), 0.0), axis=1, keepdims=True)
        count = jnp.sum(valid, axis=1, keepdims=True)
        lane = lax.broadcasted_iota(jnp.int32, (6, D), 1)
        return jnp.concatenate(rows + [jnp.where(lane < 128, sums, count)], axis=0)


SCRATCH = dict(
    S=((3, D, T), F32), G=((D, T), F32), E=((D, T), F32), Y=((1536, T), F32),
    XA=((2, D, T), BF), XM=((2, D, T), BF), rhoA=((2, 8, T), F32), rhoM=((2, 8, T), F32),
    QA=((2, NQ, 128, T), BF), KT=((2, NK, H, T), BF), VT=((NK, H, T), BF),
    KTOK=((2, NK, T, 128), BF), VTOK=((2, NK, T, 128), BF), AT=((2, D, T), BF), M=((2, D, T), F32),
    GATE=((2, FF, T), BF), UP=((2, FF, T), BF), HID=((2, FF, T), BF),
    GLD=((D, T), BF), GLO=((1024, T), BF), DGU=((2 * FF, T), BF), DOA=((NQ, 128, T), BF),
    stat=((2, 8, T), F32), valid=((8, T), F32), gacc=((2, D, 128), F32), gainA=((D, 128), F32), gainM=((D, 128), F32), pick=((H, 1024), BF),
)
WEIGHTS = dict(WA=((D, 1024), BF), WO=((D, D), BF), WG=((3, D, 1024), BF), WDT=((D, FF), BF))
GRADS = dict(DA=((D, 1024), BF), DO=((D, D), BF), DG=((3, D, 1024), BF), DD=((D, FF), BF))

class Alone:
    def run_if(self, condition, steps):
        pass


def applications(w, links):
    def forward(r, carry):
        w.prepare(r)
        links.run_if(r == 0, BEFORE_PROJECT)
        w.project(r)
        links.run_if(r == 0, AFTER_PROJECT)
        w.attend(r, links)
        pl.when(r == 0)(w.rest_of_output)
        links.run_if(r == 0, BEFORE_OUT)
        w.out_project(r)
        links.run_if(r == 0, BEFORE_MLP)
        w.mlp(r, links)
        return carry

    def backward(i, carry):
        w.mlp_back(1 - i, links)
        w.attend_back(1 - i, links)
        w.project_back(1 - i, links)
        return carry

    lax.fori_loop(0, 2, forward, 0)
    w.write_output()
    lax.fori_loop(0, 2, backward, 0)


def compute_kernel(order, names, *refs):
    w = Work(order, dict(zip(names, refs)))
    w.start()
    applications(w, Alone())
    w.write_grad()
    w.tiny[...] = w.small()


def local_compute(order, x, length, ga, gm, ct, packed):
    cos, sin = rope_tables()
    ins = dict(length=length, x=x, ct=ct, ga=ga, gm=gm, cos=jnp.asarray(cos), sin=jnp.asarray(sin), **packed)
    outs = dict(out=((D, T), BF), gin=((D, T), F32), tiny=((8, D), F32), **GRADS)
    names = list(ins) + list(outs) + list(SCRATCH)
    vmem = pl.BlockSpec(memory_space=pltpu.VMEM)
    results = pl.pallas_call(
        functools.partial(compute_kernel, order, names),
        out_shape=[jax.ShapeDtypeStruct(*s) for s in outs.values()],
        in_specs=[pl.BlockSpec(memory_space=pltpu.SMEM)] + [vmem] * (len(ins) - 1),
        out_specs=[vmem] * len(outs),
        scratch_shapes=[pltpu.VMEM(*s) for s in SCRATCH.values()],
        compiler_params=pltpu.CompilerParams(vmem_limit_bytes=VMEM_LIMIT),
    )(*ins.values())
    return dict(zip(outs, results))


def pack(order, q, k, v, o, g, u, d):
    def cols(w, width):
        return w.reshape(w.shape[0], NF, width)[:, np.array(order)]
    ob = cols(o, QB)
    wa = jnp.concatenate([cols(q, QB), cols(k, KB), cols(v, KB), ob[:, :, OW:]], axis=2).reshape(D, 1024)
    wo = jnp.concatenate([ob[:, :, :OW].reshape(D, NF * OW), ob[:, :, OW:].reshape(D, D - NF * OW)], axis=1)
    wg = jnp.concatenate([cols(g, FB), cols(u, FB)], axis=2).reshape(D, NF, 3, 128)
    wg = wg.transpose(2, 0, 1, 3).reshape(3, D, 1024)
    wd = d.T.reshape(NF, QB, FF)[np.array(order)].reshape(D, FF)
    return dict(WA=wa, WO=wo, WG=wg, WDT=wd)


def unpack(order, r):
    back = np.argsort(np.array(order))
    a = r["DA"].astype(F32).reshape(D, NF, 128)[:, back]
    o = r["DO"][:, : NF * OW].astype(F32).reshape(D, NF, OW)[:, back]
    o = jnp.concatenate([o, a[:, :, 120:]], axis=2).reshape(D, D)
    g = r["DG"].astype(F32).reshape(3, D, NF, 128).transpose(1, 2, 0, 3).reshape(D, NF, 2 * FB)[:, back]
    d = r["DD"].astype(F32).reshape(NF, QB, FF)[back].reshape(D, FF).T
    return (
        a[:, :, :QB].reshape(D, D), a[:, :, QB : QB + KB].reshape(D, NK * H), a[:, :, QB + KB : 120].reshape(D, NK * H),
        o, g[:, :, :FB].reshape(D, FF), g[:, :, FB:].reshape(D, FF), d,
    )


PIECES = ("A", "O", "G0", "G1", "G2", "D0", "D1")
DCUT = dict(D0=(0, 256), D1=(256, 128))
MESH = pl.DeviceIdType.MESH


def region(refs, piece, dp, y, z=0, count=4):
    ref, line = refs[piece[0]], 4 * y + z
    if piece[0] == "D":
        first, size = DCUT[piece]
        rows = pl.ds(pl.multiple_of(QB * line, 16), QB * count)
        return ref.at[rows, pl.ds(pl.multiple_of(LANES * dp + first, 128), size)]
    width = OW if piece == "O" else 128
    rows = pl.ds(pl.multiple_of(ROWS * dp, 16), ROWS)
    lanes = pl.ds(pl.multiple_of(width * line, 128), width * count)
    return ref.at[int(piece[1]), rows, lanes] if piece[0] == "G" else ref.at[rows, lanes]


def shape_of(piece, count):
    if piece[0] == "D":
        return (QB * count, DCUT[piece][1])
    return (ROWS, (OW if piece == "O" else 128) * count)


def slip_shape(piece):
    return (QB + 8, DCUT[piece][1]) if piece[0] == "D" else (ROWS, 128)


def cut(piece, line, z):
    if piece == "O":
        return jnp.concatenate([line[:, OW * z : OW * z + OW]] * 2, axis=1)
    return jnp.concatenate([line[QB * z : QB * z + QB], jnp.zeros((8, line.shape[1]), F32)], axis=0)


class Links:
    def __init__(self, refs):
        self.__dict__.update(refs)
        self.weights = dict(A=refs["WA"], O=refs["WO"], G=refs["WG"], D=refs["WDT"])
        self.grads = dict(A=refs["DA"], O=refs["DO"], G=refs["DG"], D=refs["DD"])
        self.dp, f = lax.axis_index("dp"), lax.axis_index("fsdp")
        self.x, self.c = self.dp // 2, lax.rem(self.dp, 2)
        self.z, self.y = f // 2, lax.rem(f, 2)
        self.ny = 1 - self.y
        self.theirs = [2 * i + 1 - self.c for i in range(2)]
        self.far = 2 * (1 - self.x) + self.c
        self.other = 2 * self.x + 1 - self.c
        self.sib = (self.other, f)
        self.xn = (self.far, f)
        self.yn = (self.dp, 2 * self.z + 1 - self.y)
        self.peer = [None] + [lax.rem(self.z + k, 4) for k in (1, 2, 3)]
        self.zn = [None] + [(self.dp, 2 * self.peer[k] + self.y) for k in (1, 2, 3)]
        self.copies = {}
        self.used = 0

    def greet(self):
        for device in [self.sib, self.xn, self.yn] + self.zn[1:]:
            pl.semaphore_signal(pltpu.get_barrier_semaphore(), inc=1, device_id=device, device_id_type=MESH)

    def met(self):
        pl.semaphore_wait(pltpu.get_barrier_semaphore(), 6)

    def send(self, name, src, dst, device):
        index = self.used
        self.used += 1

        def copy():
            return pltpu.make_async_remote_copy(
                src_ref=src(),
                dst_ref=dst(),
                send_sem=self.sent.at[index],
                recv_sem=self.came.at[index],
                device_id=device,
                device_id_type=MESH,
            )

        copy().start()
        self.copies[name] = copy

    def arrived(self, *names):
        for name in names:
            self.copies[name]().wait_recv()

    def finish(self):
        for copy in self.copies.values():
            copy().wait_send()

    def run_if(self, condition, steps):
        if steps:
            pl.when(condition)(functools.partial(self.run, *steps))

    def run(self, *steps):
        for step in steps:
            kind, piece = step.split()
            getattr(self, kind)(piece)


    def spread(self, tag, p, device, dp=None, y=None, z=0, count=4):
        block = lambda: region(self.weights, p, self.dp if dp is None else dp, self.y if y is None else y, z, count)
        self.send(("w", p, tag), block, block, device)

    def share(self, p):
        for k in (1, 3, 2):
            if p[0] in "OD":
                block = lambda: getattr(self, "slip" + p).at[self.z]
                self.send(("w", p, f"z{k}"), block, block, self.zn[k])
            else:
                self.spread(f"z{k}", p, self.zn[k], z=self.z, count=1)

    def line(self, p):
        self.arrived(*[("w", p, f"z{k}") for k in (1, 2, 3)])
        if p[0] in "OD":
            slips = [getattr(self, "slip" + p)[z].astype(F32) for z in range(4)]
            if p == "O":
                whole = jnp.concatenate([slip[:, :OW] for slip in slips], axis=1)
            else:
                whole = jnp.concatenate([slip[:QB] for slip in slips], axis=0)
            region(self.weights, p, self.dp, self.y)[...] = whole.astype(BF)
        self.spread("x", p, self.xn)
        self.spread("y", p, self.yn)
        self.spread("s", p, self.sib)

    def cross(self, p):
        self.arrived(("w", p, "x"))
        self.spread("xy", p, self.yn, dp=self.far, count=2)
        self.spread("sx", p, self.sib, dp=self.far)
        self.arrived(("w", p, "y"))
        self.spread("yx", p, self.xn, y=self.ny, z=2, count=2)
        self.spread("sy", p, self.sib, y=self.ny)

    def rest(self, p):
        self.arrived(("w", p, "xy"))
        self.spread("sxy", p, self.sib, dp=self.far, y=self.ny, count=2)
        self.arrived(("w", p, "yx"))
        self.spread("syx", p, self.sib, dp=self.far, y=self.ny, z=2, count=2)

    def end(self, p):
        self.arrived(*[("w", p, tag) for tag in ("s", "sx", "sy", "sxy", "syx")])


    def term(self, p, dp, y, z=0, count=4):
        return region(self.grads, p, dp, y, z, count)

    def add(self, p, dp, y, z, count, came):
        at = self.term(p, dp, y, z, count)
        at[...] = at[...] + came[...]

    def sibs(self, p):
        room = getattr(self, "one" + p)
        for i in range(2):
            for y in range(2):
                dp = self.theirs[i]
                self.send(
                    ("g", p, "s", i, y),
                    lambda dp=dp, y=y: self.term(p, dp, y),
                    lambda i=i, y=y: room.at[i, y],
                    self.sib,
                )

    def pair(self, p):
        room = getattr(self, "one" + p)
        for i in range(2):
            for y in range(2):
                self.arrived(("g", p, "s", i, y))
                self.add(p, 2 * i + self.c, y, 0, 4, room.at[i, y])
        ups, across = getattr(self, "twoy" + p), getattr(self, "twox" + p)
        for i, dp in enumerate((self.dp, self.far)):
            self.send(
                ("g", p, "y", i), lambda dp=dp: self.term(p, dp, self.ny, 0, 2), lambda i=i: ups.at[i], self.yn
            )
        for j, y in enumerate((self.y, self.ny)):
            self.send(
                ("g", p, "x", j), lambda y=y: self.term(p, self.far, y, 2, 2), lambda j=j: across.at[j], self.xn
            )

    def twos(self, p):
        ups, across = getattr(self, "twoy" + p), getattr(self, "twox" + p)
        for i in (1, 0):
            self.arrived(("g", p, "y", i))
            self.add(p, (self.dp, self.far)[i], self.y, 0, 2, ups.at[i])
            if i == 1:
                self.send(
                    ("g", p, "yx"), lambda: self.term(p, self.far, self.y, 0, 2), lambda: getattr(self, "threex" + p), self.xn
                )
        for j in (1, 0):
            self.arrived(("g", p, "x", j))
            self.add(p, self.dp, (self.y, self.ny)[j], 2, 2, across.at[j])
            if j == 1:
                self.send(
                    ("g", p, "xy"), lambda: self.term(p, self.dp, self.ny, 2, 2), lambda: getattr(self, "threey" + p), self.yn
                )

    def fours(self, p):
        self.arrived(("g", p, "yx"))
        self.add(p, self.dp, self.y, 0, 2, getattr(self, "threex" + p))
        self.arrived(("g", p, "xy"))
        self.add(p, self.dp, self.y, 2, 2, getattr(self, "threey" + p))
        if p[0] in "OD":
            line = self.term(p, self.dp, self.y)[...].astype(F32)
            for z in range(4):
                getattr(self, "part" + p)[z] = cut(p, line, z).astype(BF)
        for k in (1, 3, 2):
            if p[0] in "OD":
                src = lambda k=k: getattr(self, "part" + p).at[self.peer[k]]
            else:
                src = lambda k=k: self.term(p, self.dp, self.y, self.peer[k], 1)
            self.send(("g", p, "z", k), src, lambda k=k: getattr(self, "four" + p).at[k - 1], self.zn[k])

    def total(self, p):
        own = getattr(self, "part" + p)[self.z] if p[0] in "OD" else self.term(p, self.dp, self.y, self.z, 1)[...]
        total = own.astype(F32)
        for k in (1, 2, 3):
            self.arrived(("g", p, "z", k))
            total = total + getattr(self, "four" + p)[k - 1].astype(F32)
        if p[0] == "D":
            first, size = DCUT[p]
            self.sumD[:, first : first + size] = total[:QB, :]
        else:
            at = 128 * ("A", "O", "G0", "G1", "G2").index(p)
            self.sumN[:, at : at + 128] = total


    def tiny(self, step):
        step = int(step)
        if step > 0:
            self.arrived(("t", step - 1))
            self.tinies[step] = self.tinies[step - 1] + self.tinyin[step - 1]
        if step < 3:
            device = (self.sib, self.xn, self.yn)[step]
            self.send(("t", step), lambda: self.tinies.at[step], lambda: self.tinyin.at[step], device)
        else:
            for k in (1, 2, 3):
                self.send(("t", step, k), lambda: self.tinies.at[3], lambda k=k: self.tinyz.at[k], self.zn[k])

    def tiny_end(self):
        self.tinyz[0] = self.tinies[3]
        for k in (1, 2, 3):
            self.arrived(("t", 3, k))
        total = None
        for z in range(4):
            term = self.tinyz[lax.rem(self.z - z + 4, 4)]
            total = term if total is None else total + term
        self.sumT[...] = total


def rooms():
    shapes = {}
    for p in PIECES:
        shapes["one" + p] = ((2, 2) + shape_of(p, 4), BF)
        for room in ("twoy", "twox"):
            shapes[room + p] = ((2,) + shape_of(p, 2), BF)
        for room in ("threex", "threey"):
            shapes[room + p] = (shape_of(p, 2), BF)
        shapes["four" + p] = ((3,) + slip_shape(p), BF)
        if p[0] in "OD":
            shapes["slip" + p] = ((4,) + slip_shape(p), BF)
            shapes["part" + p] = ((4,) + slip_shape(p), BF)
    shapes["tinies"] = ((4, 8, D), F32)
    shapes["tinyin"] = ((3, 8, D), F32)
    shapes["tinyz"] = ((4, 8, D), F32)
    return shapes


COPIES = len(PIECES) * (12 + 13) + 6


def pack_own(links, refs):
    rows = lambda *names: [refs[n][...].astype(F32) for n in names]
    q, k, v, o, g, u, d = rows("q", "k", "v", "o", "g", "u", "d")
    gu = jnp.concatenate([g, u], axis=1)
    whole = dict(A=jnp.concatenate([q, k.T, v.T, o[:, OW:]], axis=1), G0=gu[:, :128], G1=gu[:, 128:256], G2=gu[:, 256:])
    for p in PIECES:
        if p == "O":
            links.slipO[links.z] = cut(p, o, 0).astype(BF)
        elif p[0] == "D":
            first, size = DCUT[p]
            getattr(links, "slip" + p)[links.z] = cut(p, d[:, first : first + size], 0).astype(BF)
        else:
            region(links.weights, p, links.dp, links.y, links.z, 1)[...] = whole[p].astype(BF)


BEGIN = ("share A", "share O", "share G0", "share G1", "share G2", "share D0", "share D1")
BEFORE_PROJECT = ("line A", "line O", "cross A", "line G0", "cross O", "rest A", "line G1", "end A")
AFTER_PROJECT = ("cross G0", "rest O", "line G2")
HEADS = (("cross G1", "rest G0"), ("line D0",), ("cross G2", "rest G1"))
BEFORE_OUT = ("end O", "line D1")
BEFORE_MLP = ("cross D0", "rest G2", "end G0", "end G1", "end G2")
MLP = (("cross D1", "rest D0"), ("rest D1", "end D0", "end D1"))
AFTER_DOWN = ("sibs D0", "sibs D1")
HIDDEN = (("pair D0",), ("pair D1",), (), ("twos D0",))
AFTER_GATE = (("sibs G0", "twos D1"), ("sibs G1", "pair G0", "fours D0"), ("sibs G2", "pair G1", "fours D1"))
BEFORE_NORM = ("pair G2",)
AFTER_OUT = ("sibs O", "twos G0")
BEFORE_HEADS = ("pair O",)
BACK_HEADS = (("twos G1", "fours G0"), ("twos G2", "fours G1"), ("twos O", "fours G2"))
AFTER_QKV = ("sibs A", "fours O")
LAST = ("tiny 0", "pair A", "tiny 1", "twos A", "tiny 2")
VERY_LAST = ("total D0", "total D1", "total G0", "total G1", "total G2", "fours A", "tiny 3", "total O", "total A")


def whole_kernel(order, names, *args):
    refs = dict(zip(names, args))
    w, links = Work(order, refs), Links(refs)
    links.greet()
    pack_own(links, refs)
    links.met()
    links.run(*BEGIN)
    w.start()
    applications(w, links)
    links.tinies[0] = w.small()
    links.run(*LAST)
    w.write_grad()
    links.run(*VERY_LAST)
    links.tiny_end()
    links.finish()


def finish_kernel(*refs):
    out, gin, sums, sumd, tiny, oout, ogin, ga, q, k, v, o, gm, g, u, d, rms = refs
    oout[...] = out[...]
    ogin[...] = gin[...]
    q[...] = sums[:, :QB]
    k[...] = sums[:, QB : QB + KB].T
    v[...] = sums[:, QB + KB : 120].T
    o[...] = jnp.concatenate([sums[:, 128 : 128 + OW], sums[:, 120:128]], axis=1)
    g[...] = sums[:, 256 : 256 + FB]
    u[...] = sums[:, 256 + FB : 256 + 2 * FB]
    d[...] = sumd[...]
    ga[...] = tiny[0:1, :].reshape(D)
    gm[...] = tiny[1:2, :].reshape(D)
    lane = lax.broadcasted_iota(jnp.int32, (1, 3), 1)
    for r in range(2):
        first, second, third = [tiny[2 + 3 * r + i : 3 + 3 * r + i, 0:3] for i in range(3)]
        squares = jnp.where(lane == 0, first, jnp.where(lane == 1, second, third))
        rms[r : r + 1, :] = jnp.sqrt(squares / (tiny[2:3, 128:131] * D))


def whole(x, length, ga, q, k, v, o, gm, g, u, d, ct):
    order = [2 * (b % 4) + b // 4 for b in range(NF)]
    cos, sin = rope_tables()
    ins = dict(
        length=length, x=x[0].T, ct=ct[0].T, ga=ga, gm=gm, cos=jnp.asarray(cos), sin=jnp.asarray(sin),
        q=q, k=k.T, v=v.T, o=o, g=g, u=u, d=d.T,
    )
    outs = dict(
        out=((D, T), BF), gin=((D, T), F32), sumN=((ROWS, 256 + 2 * FB), F32), sumD=((QB, LANES), F32), sumT=((8, D), F32)
    )
    scratch = dict(SCRATCH, **WEIGHTS, **GRADS, **rooms())
    names = list(ins) + list(outs) + list(scratch) + ["sent", "came"]
    vmem = pl.BlockSpec(memory_space=pltpu.VMEM)
    r = pl.pallas_call(
        functools.partial(whole_kernel, order, names),
        out_shape=[jax.ShapeDtypeStruct(*s) for s in outs.values()],
        in_specs=[pl.BlockSpec(memory_space=pltpu.SMEM)] + [vmem] * (len(ins) - 1),
        out_specs=[vmem] * len(outs),
        scratch_shapes=[pltpu.VMEM(*s) for s in scratch.values()]
        + [pltpu.SemaphoreType.DMA((COPIES,)), pltpu.SemaphoreType.DMA((COPIES,))],
        compiler_params=pltpu.CompilerParams(
            vmem_limit_bytes=VMEM_LIMIT, collective_id=0, has_side_effects=True
        ),
    )(*ins.values())
    rows = [
        ((D, T), BF), ((D, T), F32), ((D,), F32), (q.shape, F32), (k.shape[::-1], F32), (v.shape[::-1], F32),
        (o.shape, F32), ((D,), F32), (g.shape, F32), (u.shape, F32), (d.shape[::-1], F32), ((2, 3), F32),
    ]
    out, gin, ga, q, k, v, o, gm, g, u, d, rms = pl.pallas_call(
        finish_kernel,
        out_shape=[jax.ShapeDtypeStruct(*s) for s in rows],
        in_specs=[vmem] * len(outs),
        out_specs=[vmem] * len(rows),
    )(*r)
    return out.T[None], gin.T[None], ga, q, k.T, v.T, o, gm, g, u, d.T, rms


def by_collectives(x, length, ga, q, k, v, o, gm, g, u, d, ct):
    order = list(range(NF))
    full = [lax.all_gather(lax.all_gather(w, "fsdp", axis=1, tiled=True), "dp", axis=0, tiled=True) for w in (q, k, v, o, g, u, d)]
    packed = pack(order, *full)
    results = [local_compute(order, x[i].T, length[i : i + 1], ga, gm, ct[i].T, packed) for i in range(x.shape[0])]
    out = jnp.stack([r["out"].T for r in results])
    gin = jnp.stack([r["gin"].T for r in results])
    tiny = lax.psum(sum(r["tiny"] for r in results), ("dp", "fsdp"))
    terms = [unpack(order, r) for r in results]
    grads = [
        lax.psum_scatter(
            lax.psum_scatter(sum(t), "dp", scatter_dimension=0, tiled=True), "fsdp", scatter_dimension=1, tiled=True
        )
        for t in zip(*terms)
    ]
    rms = jnp.sqrt(tiny[2:8, 0].reshape(2, 3) / (tiny[2, 128] * D))
    gq, gk, gv, go, gg, gu, gd = grads
    return out, gin, tiny[0], gq, gk, gv, go, tiny[1], gg, gu, gd, rms


def solution(mesh):
    blocks = P("dp", "fsdp")
    slots = P(("dp", "fsdp"), None, None)
    in_specs = (slots, P(("dp", "fsdp")), P(), blocks, blocks, blocks, blocks, P(), blocks, blocks, blocks, slots)
    out_specs = (slots, slots, P(), blocks, blocks, blocks, blocks, P(), blocks, blocks, blocks, P())

    def on_device(*args):
        fits = mesh.shape["dp"] == 4 and mesh.shape["fsdp"] == 8 and args[0].shape[0] == 1
        return (whole if fits else by_collectives)(*args)

    return jax.shard_map(on_device, mesh=mesh, in_specs=in_specs, out_specs=out_specs, check_vma=False)
```

```python
import functools
import jax
import jax.numpy as jnp
import numpy as np
from jax import lax
from jax.experimental import pallas as pl
from jax.experimental.pallas import tpu as pltpu
from jax.sharding import PartitionSpec as P

D = 576
NQ = 9
NK = 3
GROUP = NQ // NK
H = 64
HALF = H // 2
FF = 1536
T = 512
NF = 8
QB = D // NF
KB = NK * H // NF
FB = FF // NF
EPS = 1e-05
ROPE_BASE = 10000.0
SCALE = H ** (-0.5)
NEG = -1e30
BLK = 256
VMEM_LIMIT = 63 * 2**20
ROWS = D // 4
LANES = FF // 4
OW = QB - 8
BF = jnp.bfloat16
F32 = jnp.float32


def dot(a, b, ca, cb):
    return lax.dot_general(a, b, (((ca,), (cb,)), ((), ())), preferred_element_type=F32)


def rope_tables():
    inverse = ROPE_BASE ** (-(2.0 * np.arange(HALF, dtype=np.float64)) / H)
    angles = inverse[:, None] * np.arange(T, dtype=np.float64)[None, :]
    return np.cos(angles).astype(np.float32), np.sin(angles).astype(np.float32)


def parts_of(row):
    hi = row.astype(BF).astype(F32)
    rest = row - hi
    mid = rest.astype(BF).astype(F32)
    return [hi, mid, rest - mid]


def lane_tiles():
    return [slice(128 * i, 128 * i + 128) for i in range(T // 128)]


class Work:
    def __init__(self, order, refs):
        self.order = order
        self.__dict__.update(refs)

    def start(self):
        count = self.length[0]
        place = lax.broadcasted_iota(jnp.int32, (8, T), 1)
        valid = (place < count).astype(F32)
        self.valid[...] = valid
        for ts in lane_tiles():
            self.S[0, :, ts] = self.x[:, ts].astype(F32)
            self.G[:, ts] = jnp.where(valid[0:1, ts] > 0.0, self.ct[:, ts].astype(F32), 0.0)
        self.gainA[...] = jnp.broadcast_to(self.ga[...].reshape(1, D), (128, D)).T
        self.gainM[...] = jnp.broadcast_to(self.gm[...].reshape(1, D), (128, D)).T
        row = lax.broadcasted_iota(jnp.int32, (H, 1024), 0)
        lane = lax.broadcasted_iota(jnp.int32, (H, 1024), 1)
        self.pick[...] = jnp.where(lane == 128 * (row // 8) + 120 + lax.rem(row, 8), 1.0, 0.0).astype(BF)
        self.gacc[...] = jnp.zeros_like(self.gacc)
        def blank(h, carry):
            self.QA[0, h, H:, :] = jnp.zeros((H, T), BF)
            self.QA[1, h, H:, :] = jnp.zeros((H, T), BF)
            self.DOA[h, H:, :] = jnp.zeros((H, T), BF)
            return carry

        lax.fori_loop(0, NQ, blank, 0)

        def clear(i, carry):
            rows = pl.ds(pl.multiple_of(i * 64, 64), 64)
            self.DA[rows, :] = jnp.zeros((64, 1024), BF)
            self.DO[rows, :] = jnp.zeros((64, D), BF)
            self.DD[rows, :] = jnp.zeros((64, FF), BF)
            for k in range(3):
                self.DG[k, rows, :] = jnp.zeros((64, 1024), BF)
            return carry

        lax.fori_loop(0, D // 64, clear, 0)

    def norm(self, src, r, gain, dst, rho_ref, row):
        for ts in lane_tiles():
            v = src[r, :, ts]
            total = jnp.sum(v * v, axis=0, keepdims=True)
            if row is not None:
                self.stat[r, row : row + 1, ts] = total
            rho = lax.rsqrt(total * (1.0 / D) + EPS)
            rho_ref[r, 0:1, ts] = rho
            dst[r, :, ts] = (v * rho * gain[...]).astype(BF)

    def natural_rows(self, ref, base, width, first, count):
        pieces = []
        row = first
        while row < first + count:
            f, i = row // width, row % width
            n = min(width - i, first + count - row)
            at = 128 * self.order.index(f) + base + i
            pieces.append(ref[at : at + n, :])
            row += n
        return pieces[0] if len(pieces) == 1 else jnp.concatenate(pieces, axis=0)

    def prepare(self, r):
        self.norm(self.S, r, self.gainA, self.XA, self.rhoA, 0)

    def project(self, r):
        def part(c, carry):
            cs = pl.ds(pl.multiple_of(512 * c, 512), 512)
            self.Y[cs, :] = dot(self.WA[:, cs], self.XA[r], 0, 0)
            return carry

        for c in range(2):
            part(c, 0)
        cos, sin = self.cos[...], self.sin[...]
        one = jnp.ones((1, T), F32)
        place = lax.broadcasted_iota(jnp.int32, (1, T), 1)
        bias = jnp.where(place < self.length[0], 0.0, NEG)
        for h in range(NQ + NK):
            base, width, at = (0, QB, h) if h < NQ else (QB, KB, h - NQ)
            a = self.natural_rows(self.Y, base, width, H * at, HALF)
            b = self.natural_rows(self.Y, base, width, H * at + HALF, HALF)
            first, second = a * cos - b * sin, b * cos + a * sin
            if h < NQ:
                self.QA[r, h, 0:HALF, :] = (first * SCALE).astype(BF)
                self.QA[r, h, HALF:H, :] = (second * SCALE).astype(BF)
                self.QA[r, h, H : H + 16, :] = jnp.concatenate([one, jnp.zeros((15, T), F32)], axis=0).astype(BF)
            else:
                g = h - NQ
                key = jnp.concatenate([first, second], axis=0)
                self.KT[r, g] = key.astype(BF)
                v = jnp.concatenate(
                    [
                        self.natural_rows(self.Y, QB + KB, KB, H * g, HALF),
                        self.natural_rows(self.Y, QB + KB, KB, H * g + HALF, HALF),
                    ],
                    axis=0,
                )
                self.VT[g] = v.astype(BF)
                ones3 = jnp.ones((3, T), F32)
                tail = jnp.zeros((H - 4, T), F32)
                ktall = jnp.concatenate([key, bias, ones3, tail], axis=0)
                vtall = jnp.concatenate([v, jnp.zeros((1, T), F32), ones3, tail], axis=0)
                for ts in lane_tiles():
                    self.KTOK[r, g, ts, :] = ktall[:, ts].T.astype(BF)
                    self.VTOK[r, g, ts, :] = vtall[:, ts].T.astype(BF)

    def diagonal(self):
        key = lax.broadcasted_iota(jnp.int32, (BLK, BLK), 0)
        query = lax.broadcasted_iota(jnp.int32, (BLK, BLK), 1)
        return key <= query

    def attend(self, r, links):
        low, high = slice(0, BLK), slice(BLK, T)

        def head(h, carry):
            g = h // GROUP
            allowed = self.diagonal()
            at = pl.ds(pl.multiple_of(h * H, H), H)
            s = dot(self.KTOK[r, g, low, :], self.QA[r, h, :, low], 1, 0)
            s = jnp.where(allowed, s, NEG)
            top = jnp.max(s, axis=0, keepdims=True)
            p = jnp.exp(s - top)
            total = jnp.sum(p, axis=0, keepdims=True)
            o = dot(self.VT[g, :, low], p.astype(BF), 1, 0)
            self.AT[r, at, low] = (o * (1.0 / total)).astype(BF)
            lse0 = top + jnp.log(total)
            s0 = dot(self.KTOK[r, g, low, :], self.QA[r, h, :, high], 1, 0)
            s1 = dot(self.KTOK[r, g, high, :], self.QA[r, h, :, high], 1, 0)
            s1 = jnp.where(allowed, s1, NEG)
            top = jnp.maximum(jnp.max(s0, axis=0, keepdims=True), jnp.max(s1, axis=0, keepdims=True))
            p0 = jnp.exp(s0 - top)
            p1 = jnp.exp(s1 - top)
            total = jnp.sum(p0, axis=0, keepdims=True) + jnp.sum(p1, axis=0, keepdims=True)
            o = dot(self.VT[g, :, low], p0.astype(BF), 1, 0) + dot(self.VT[g, :, high], p1.astype(BF), 1, 0)
            self.AT[r, at, high] = (o * (1.0 / total)).astype(BF)
            lse1 = top + jnp.log(total)
            lse = jnp.concatenate([lse0, lse1], axis=1)
            rows = [jnp.ones((1, T), F32)] + parts_of(-lse) + [jnp.zeros((12, T), F32)]
            self.QA[r, h, H : H + 16, :] = jnp.concatenate(rows, axis=0).astype(BF)
            return carry

        def group(g, carry):
            [head(GROUP * g + k, 0) for k in range(GROUP)]
            links.run_if(r == 0, HEADS[g])
            return carry

        for g in range(NK):
            group(g, 0)

    def rest_of_output(self):
        self.WO[:, NF * OW :] = dot(self.WA[...], self.pick[...], 1, 1).astype(BF)

    def after(self, value, src, r, dst, to, row, squares):
        n = value.shape[0]
        dst[to, row : row + n, :] = src[r, row : row + n, :] + value
        for i in range(n // 8):
            part = value[8 * i : 8 * i + 8]
            squares = squares + part * part
        return squares

    def out_project(self, r):
        self.Y[0:D, :] = dot(self.WO[...], self.AT[r], 0, 0)
        squares = jnp.zeros((8, T), F32)
        for b in range(NF):
            f = self.order[b]
            squares = self.after(self.Y[OW * b : OW * b + OW, :], self.S, r, self.M, r, QB * f, squares)
            at = NF * OW + 8 * b
            squares = self.after(self.Y[at : at + 8, :], self.S, r, self.M, r, QB * f + OW, squares)
        self.stat[r, 1:2, :] = jnp.sum(squares, axis=0, keepdims=True)

    def mlp(self, r, links):
        self.norm(self.M, r, self.gainM, self.XM, self.rhoM, None)

        def half(y, carry):
            cs = pl.ds(pl.multiple_of(512 * y, 512), 512)

            def part(i, carry):
                to = pl.ds(pl.multiple_of(512 * i, 512), 512)
                self.Y[to, :] = dot(self.WG[i, :, cs], self.XM[r], 0, 0)
                return carry

            for i in range(3):
                part(i, 0)

            def block(z, carry):
                f = self.natural(y, z)
                for j in range(3):
                    gate_at, up_at = self.places(j)
                    gate = self.Y[pl.ds(pl.multiple_of(gate_at[0] * 512 + 128 * z + gate_at[1], 64), 64), :]
                    up = self.Y[pl.ds(pl.multiple_of(up_at[0] * 512 + 128 * z + up_at[1], 64), 64), :]
                    rows = pl.ds(pl.multiple_of(FB * f + 64 * j, 64), 64)
                    self.GATE[r, rows, :] = gate.astype(BF)
                    self.UP[r, rows, :] = up.astype(BF)
                    self.HID[r, rows, :] = (gate * jax.nn.sigmoid(gate) * up).astype(BF)
                return carry

            for z in range(4):
                block(z, 0)
            links.run_if(r == 0, MLP[y])
            return carry

        for y in range(2):
            half(y, 0)
        self.Y[0:D, :] = dot(self.WDT[...], self.HID[r], 1, 0)
        squares = jnp.zeros((8, T), F32)
        for b in range(NF):
            squares = self.after(self.Y[QB * b : QB * b + QB, :], self.M, r, self.S, r + 1, QB * self.order[b], squares)
        self.stat[r, 2:3, :] = jnp.sum(squares, axis=0, keepdims=True)

    def natural(self, y, z):
        return 2 * z + y if self.order[1] == 2 else 4 * y + z

    def places(self, j):
        return ((0, 0), (0, 64), (1, 0))[j], ((1, 64), (2, 0), (2, 64))[j]

    def write_output(self):
        valid = self.valid[0:1, :]
        for ts in lane_tiles():
            v = jnp.where(valid[:, ts] > 0.0, self.S[2, :, ts], 0.0)
            self.out[:, ts] = v.astype(BF)

    def pack_down(self):
        for k in range(NF // 2):
            rows = [self.G[QB * self.order[b] : QB * self.order[b] + QB, :] for b in (2 * k, 2 * k + 1)]
            self.GLD[2 * QB * k : 2 * QB * k + 2 * QB, :] = jnp.concatenate(rows, axis=0).astype(BF)

    def pack_out(self):
        tails = []
        for b in range(NF):
            at = QB * self.order[b]
            self.GLO[OW * b : OW * b + OW, :] = self.G[at : at + OW, :].astype(BF)
            tails.append(self.G[at + OW : at + QB, :])
        self.GLO[NF * OW : D, :] = jnp.concatenate(tails, axis=0).astype(BF)

    def add_term(self, dst, index, value):
        dst[index] = (value + dst[index].astype(F32)).astype(dst.dtype)

    def norm_back(self, src, r, rho_ref, gain, slot):
        for ts in lane_tiles():
            e, v, rho = self.E[:, ts], src[r, :, ts], rho_ref[r, 0:1, ts]
            u = e * gain[...]
            mean = jnp.sum(u * v, axis=0, keepdims=True) * (1.0 / D)
            self.gacc[slot] += e * (v * rho)
            self.G[:, ts] = self.G[:, ts] + rho * (u - v * (rho * rho * mean))

    def mlp_back(self, r, links):
        self.pack_down()
        for c in range(2):
            cs = slice(768 * c, 768 * c + 768)
            self.add_term(self.DD, (slice(None), cs), dot(self.GLD[...], self.HID[r, cs, :], 1, 1))
        links.run_if(r == 0, AFTER_DOWN)

        def hidden(k, carry):
            rows = pl.ds(pl.multiple_of(2 * FB * k, 128), 2 * FB)
            self.Y[0 : 2 * FB, :] = dot(self.WDT[:, rows], self.GLD[...], 0, 0)
            for m in range(2):
                f = 2 * k + m
                b = k + 4 * m if self.order[1] == 2 else f
                for j in range(3):
                    at = pl.ds(pl.multiple_of(FB * f + 64 * j, 64), 64)
                    grad = self.Y[FB * m + 64 * j : FB * m + 64 * j + 64, :]
                    gate = self.GATE[r, at, :].astype(F32)
                    up = self.UP[r, at, :].astype(F32)
                    sig = jax.nn.sigmoid(gate)
                    silu = gate * sig
                    gate_at, up_at = self.places(j)
                    to = pl.ds(pl.multiple_of(1024 * gate_at[0] + 128 * b + gate_at[1], 64), 64)
                    self.DGU[to, :] = (grad * up * (sig + silu * (1.0 - sig))).astype(BF)
                    to = pl.ds(pl.multiple_of(1024 * up_at[0] + 128 * b + up_at[1], 64), 64)
                    self.DGU[to, :] = (grad * silu).astype(BF)
            links.run_if(r == 0, HIDDEN[k])
            return carry

        for k in range(4):
            hidden(k, 0)

        def matrix(i, carry):
            grad = self.DGU[pl.ds(pl.multiple_of(1024 * i, 1024), 1024), :]
            self.add_term(self.DG, (i,), dot(self.XM[r], grad, 1, 1))
            links.run_if(r == 0, AFTER_GATE[i])
            return carry

        for i in range(3):
            matrix(i, 0)
        self.E[...] = dot(self.WG[0], self.DGU[0:1024, :], 1, 0)

        def back(i, carry):
            grad = self.DGU[pl.ds(pl.multiple_of(1024 * i, 1024), 1024), :]
            self.E[...] = self.E[...] + dot(self.WG[i], grad, 1, 0)
            return carry

        for i in (1, 2):
            back(i, 0)
        links.run_if(r == 0, BEFORE_NORM)
        self.norm_back(self.M, r, self.rhoM, self.gainM, 1)

    def attend_back(self, r, links):
        self.pack_out()
        term = dot(self.AT[r], self.GLO[0:D, :], 1, 1)
        self.add_term(self.DO, (slice(None), slice(0, NF * OW)), term[:, : NF * OW])
        self.DO[:, NF * OW :] = term[:, NF * OW :].astype(BF)
        links.run_if(r == 0, AFTER_OUT)
        self.E[...] = dot(self.WO[...], self.GLO[0:D, :], 1, 0)
        links.run_if(r == 0, BEFORE_HEADS)
        for h in range(NQ):
            rows = slice(H * h, H * h + H)
            do = self.E[rows, :].astype(BF)
            self.DOA[h, 0:H, :] = do
            delta = jnp.sum(do.astype(F32) * self.AT[r, rows, :].astype(F32), axis=0, keepdims=True)
            rows = [jnp.zeros((1, T), F32)] + parts_of(-delta) + [jnp.zeros((12, T), F32)]
            self.DOA[h, H : H + 16, :] = jnp.concatenate(rows, axis=0).astype(BF)
        low, high = slice(0, BLK), slice(BLK, T)
        self.Y[D : D + 2 * NK * H, :] = jnp.zeros((2 * NK * H, T), F32)

        def head(h, carry):
            g = h // GROUP
            allowed = self.diagonal()
            at = pl.ds(pl.multiple_of(h * H, H), H)
            kat = pl.ds(pl.multiple_of(D + g * H, H), H)
            vat = pl.ds(pl.multiple_of(D + NK * H + g * H, H), H)
            q, do = self.QA[r, h], self.DOA[h]
            k0, k1 = self.KTOK[r, g, low, :], self.KTOK[r, g, high, :]
            v0, v1 = self.VTOK[r, g, low, :], self.VTOK[r, g, high, :]
            t0, t1 = self.KT[r, g, :, low], self.KT[r, g, :, high]

            p = jnp.where(allowed, jnp.exp(dot(k0, q[:, low], 1, 0)), 0.0)
            ds = (p * dot(v0, do[:, low], 1, 0)).astype(BF)
            p = p.astype(BF)
            self.Y[at, low] = dot(t0, ds, 1, 0) * SCALE
            dk0 = dot(q[0:H, low], ds, 1, 1)
            dv0 = dot(do[0:H, low], p, 1, 1)

            p = jnp.exp(dot(k0, q[:, high], 1, 0))
            ds = (p * dot(v0, do[:, high], 1, 0)).astype(BF)
            p = p.astype(BF)
            dq = dot(t0, ds, 1, 0)
            dk0 += dot(q[0:H, high], ds, 1, 1)
            dv0 += dot(do[0:H, high], p, 1, 1)

            p = jnp.where(allowed, jnp.exp(dot(k1, q[:, high], 1, 0)), 0.0)
            ds = (p * dot(v1, do[:, high], 1, 0)).astype(BF)
            p = p.astype(BF)
            self.Y[at, high] = (dq + dot(t1, ds, 1, 0)) * SCALE
            self.Y[kat, low] += dk0
            self.Y[vat, low] += dv0
            self.Y[kat, high] += dot(q[0:H, high], ds, 1, 1)
            self.Y[vat, high] += dot(do[0:H, high], p, 1, 1)
            return carry

        def group(g, carry):
            [head(GROUP * g + k, 0) for k in range(GROUP)]
            links.run_if(r == 0, BACK_HEADS[g])
            return carry

        for g in range(NK):
            group(g, 0)

    def project_back(self, r, links):
        cos, sin = self.cos[...], self.sin[...]
        for h in range(NQ + NK):
            first, second = slice(H * h, H * h + HALF), slice(H * h + HALF, H * h + H)
            a, b = self.Y[first, :], self.Y[second, :]
            self.Y[first, :] = a * cos + b * sin
            self.Y[second, :] = b * cos - a * sin
        for b in range(NF):
            f = self.order[b]
            rows = jnp.concatenate(
                [
                    self.Y[QB * f : QB * f + QB, :],
                    self.Y[D + KB * f : D + KB * f + KB, :],
                    self.Y[D + NK * H + KB * f : D + NK * H + KB * f + KB, :],
                    jnp.zeros((128 - QB - 2 * KB, T), F32),
                ],
                axis=0,
            )
            self.GLO[128 * b : 128 * b + 128, :] = rows.astype(BF)
        def part(c, carry):
            cs = pl.ds(pl.multiple_of(512 * c, 512), 512)
            term = dot(self.XA[r], self.GLO[cs, :], 1, 1) + dot(self.DO[:, NF * OW :], self.pick[:, cs], 1, 0)
            self.add_term(self.DA, (slice(None), cs), term)
            return carry

        for c in range(2):
            part(c, 0)
        links.run_if(r == 0, AFTER_QKV)
        self.E[...] = dot(self.WA[...], self.GLO[...], 1, 0)
        self.norm_back(self.S, r, self.rhoA, self.gainA, 0)

    def write_grad(self):
        for ts in lane_tiles():
            self.gin[:, ts] = self.G[:, ts]

    def small(self):
        valid = self.valid[0:1, :]
        rows = [jnp.sum(self.gacc[i].T, axis=0, keepdims=True) for i in range(2)]
        sums = jnp.sum(jnp.where(valid > 0.0, jnp.concatenate([self.stat[0, 0:3], self.stat[1, 0:3]], axis=0), 0.0), axis=1, keepdims=True)
        count = jnp.sum(valid, axis=1, keepdims=True)
        lane = lax.broadcasted_iota(jnp.int32, (6, D), 1)
        return jnp.concatenate(rows + [jnp.where(lane < 128, sums, count)], axis=0)


SCRATCH = dict(
    S=((3, D, T), F32), G=((D, T), F32), E=((D, T), F32), Y=((1536, T), F32),
    XA=((2, D, T), BF), XM=((2, D, T), BF), rhoA=((2, 8, T), F32), rhoM=((2, 8, T), F32),
    QA=((2, NQ, 128, T), BF), KT=((2, NK, H, T), BF), VT=((NK, H, T), BF),
    KTOK=((2, NK, T, 128), BF), VTOK=((2, NK, T, 128), BF), AT=((2, D, T), BF), M=((2, D, T), F32),
    GATE=((2, FF, T), BF), UP=((2, FF, T), BF), HID=((2, FF, T), BF),
    GLD=((D, T), BF), GLO=((1024, T), BF), DGU=((2 * FF, T), BF), DOA=((NQ, 128, T), BF),
    stat=((2, 8, T), F32), valid=((8, T), F32), gacc=((2, D, 128), F32), gainA=((D, 128), F32), gainM=((D, 128), F32), pick=((H, 1024), BF),
)
WEIGHTS = dict(WA=((D, 1024), BF), WO=((D, D), BF), WG=((3, D, 1024), BF), WDT=((D, FF), BF))
GRADS = dict(DA=((D, 1024), BF), DO=((D, D), BF), DG=((3, D, 1024), BF), DD=((D, FF), BF))

class Alone:
    def run_if(self, condition, steps):
        pass


def applications(w, links):
    def forward(r, carry):
        w.prepare(r)
        links.run_if(r == 0, BEFORE_PROJECT)
        w.project(r)
        links.run_if(r == 0, AFTER_PROJECT)
        w.attend(r, links)
        pl.when(r == 0)(w.rest_of_output)
        links.run_if(r == 0, BEFORE_OUT)
        w.out_project(r)
        links.run_if(r == 0, BEFORE_MLP)
        w.mlp(r, links)
        return carry

    def backward(i, carry):
        w.mlp_back(1 - i, links)
        w.attend_back(1 - i, links)
        w.project_back(1 - i, links)
        return carry

    lax.fori_loop(0, 2, forward, 0)
    w.write_output()
    lax.fori_loop(0, 2, backward, 0)


def compute_kernel(order, names, *refs):
    w = Work(order, dict(zip(names, refs)))
    w.start()
    applications(w, Alone())
    w.write_grad()
    w.tiny[...] = w.small()


def local_compute(order, x, length, ga, gm, ct, packed):
    cos, sin = rope_tables()
    ins = dict(length=length, x=x, ct=ct, ga=ga, gm=gm, cos=jnp.asarray(cos), sin=jnp.asarray(sin), **packed)
    outs = dict(out=((D, T), BF), gin=((D, T), F32), tiny=((8, D), F32), **GRADS)
    names = list(ins) + list(outs) + list(SCRATCH)
    vmem = pl.BlockSpec(memory_space=pltpu.VMEM)
    results = pl.pallas_call(
        functools.partial(compute_kernel, order, names),
        out_shape=[jax.ShapeDtypeStruct(*s) for s in outs.values()],
        in_specs=[pl.BlockSpec(memory_space=pltpu.SMEM)] + [vmem] * (len(ins) - 1),
        out_specs=[vmem] * len(outs),
        scratch_shapes=[pltpu.VMEM(*s) for s in SCRATCH.values()],
        compiler_params=pltpu.CompilerParams(vmem_limit_bytes=VMEM_LIMIT),
    )(*ins.values())
    return dict(zip(outs, results))


def pack(order, q, k, v, o, g, u, d):
    def cols(w, width):
        return w.reshape(w.shape[0], NF, width)[:, np.array(order)]
    ob = cols(o, QB)
    wa = jnp.concatenate([cols(q, QB), cols(k, KB), cols(v, KB), ob[:, :, OW:]], axis=2).reshape(D, 1024)
    wo = jnp.concatenate([ob[:, :, :OW].reshape(D, NF * OW), ob[:, :, OW:].reshape(D, D - NF * OW)], axis=1)
    wg = jnp.concatenate([cols(g, FB), cols(u, FB)], axis=2).reshape(D, NF, 3, 128)
    wg = wg.transpose(2, 0, 1, 3).reshape(3, D, 1024)
    wd = d.T.reshape(NF, QB, FF)[np.array(order)].reshape(D, FF)
    return dict(WA=wa, WO=wo, WG=wg, WDT=wd)


def unpack(order, r):
    back = np.argsort(np.array(order))
    a = r["DA"].astype(F32).reshape(D, NF, 128)[:, back]
    o = r["DO"][:, : NF * OW].astype(F32).reshape(D, NF, OW)[:, back]
    o = jnp.concatenate([o, a[:, :, 120:]], axis=2).reshape(D, D)
    g = r["DG"].astype(F32).reshape(3, D, NF, 128).transpose(1, 2, 0, 3).reshape(D, NF, 2 * FB)[:, back]
    d = r["DD"].astype(F32).reshape(NF, QB, FF)[back].reshape(D, FF).T
    return (
        a[:, :, :QB].reshape(D, D), a[:, :, QB : QB + KB].reshape(D, NK * H), a[:, :, QB + KB : 120].reshape(D, NK * H),
        o, g[:, :, :FB].reshape(D, FF), g[:, :, FB:].reshape(D, FF), d,
    )


PIECES = ("A0", "A1", "O", "G0", "G1", "G2", "D0", "D1")
CUT = dict(A0=(0, 80), A1=(80, ROWS - 80), D0=(0, 256), D1=(256, 128))
MESH = pl.DeviceIdType.MESH


def region(refs, piece, dp, y, z=0, count=4):
    ref, line = refs[piece[0]], 4 * y + z
    if piece[0] == "D":
        first, size = CUT[piece]
        rows = pl.ds(pl.multiple_of(QB * line, 16), QB * count)
        return ref.at[rows, pl.ds(pl.multiple_of(LANES * dp + first, 128), size)]
    width = OW if piece == "O" else 128
    first, size = CUT.get(piece, (0, ROWS))
    rows = pl.ds(pl.multiple_of(ROWS * dp + first, 16), size)
    lanes = pl.ds(pl.multiple_of(width * line, 128), width * count)
    return ref.at[int(piece[1]), rows, lanes] if piece[0] == "G" else ref.at[rows, lanes]


def shape_of(piece, count):
    if piece[0] == "D":
        return (QB * count, CUT[piece][1])
    return (CUT.get(piece, (0, ROWS))[1], (OW if piece == "O" else 128) * count)


def slip_shape(piece):
    return (QB + 8, CUT[piece][1]) if piece[0] == "D" else (CUT.get(piece, (0, ROWS))[1], 128)


def cut(piece, line, z):
    if piece == "O":
        return jnp.concatenate([line[:, OW * z : OW * z + OW]] * 2, axis=1)
    return jnp.concatenate([line[QB * z : QB * z + QB], jnp.zeros((8, line.shape[1]), F32)], axis=0)


class Links:
    def __init__(self, refs):
        self.__dict__.update(refs)
        self.weights = dict(A=refs["WA"], O=refs["WO"], G=refs["WG"], D=refs["WDT"])
        self.grads = dict(A=refs["DA"], O=refs["DO"], G=refs["DG"], D=refs["DD"])
        self.dp, f = lax.axis_index("dp"), lax.axis_index("fsdp")
        self.x, self.c = self.dp // 2, lax.rem(self.dp, 2)
        self.z, self.y = f // 2, lax.rem(f, 2)
        self.ny = 1 - self.y
        places = [(1 - self.x, self.ny), (self.x, self.ny), (1 - self.x, self.y), (self.x, self.y)]
        self.mine = [(2 * x + self.c, y) for x, y in places]
        self.theirs = [(2 * x + 1 - self.c, y) for x, y in places]
        self.far = 2 * (1 - self.x) + self.c
        self.other = 2 * self.x + 1 - self.c
        self.sib = (self.other, f)
        self.xn = (self.far, f)
        self.yn = (self.dp, 2 * self.z + 1 - self.y)
        self.peer = [None] + [lax.rem(self.z + k, 4) for k in (1, 2, 3)]
        self.zn = [None] + [(self.dp, 2 * self.peer[k] + self.y) for k in (1, 2, 3)]
        self.copies = {}
        self.used = 0

    def greet(self):
        for device in [self.sib, self.xn, self.yn] + self.zn[1:]:
            pl.semaphore_signal(pltpu.get_barrier_semaphore(), inc=1, device_id=device, device_id_type=MESH)

    def met(self):
        pl.semaphore_wait(pltpu.get_barrier_semaphore(), 6)

    def send(self, name, src, dst, device):
        index = self.used
        self.used += 1

        def copy():
            return pltpu.make_async_remote_copy(
                src_ref=src(),
                dst_ref=dst(),
                send_sem=self.sent.at[index],
                recv_sem=self.came.at[index],
                device_id=device,
                device_id_type=MESH,
            )

        copy().start()
        self.copies[name] = copy

    def arrived(self, *names):
        for name in names:
            self.copies[name]().wait_recv()

    def finish(self):
        for copy in self.copies.values():
            copy().wait_send()

    def run_if(self, condition, steps):
        if steps:
            pl.when(condition)(functools.partial(self.run, *steps))

    def run(self, *steps):
        for step in steps:
            kind, piece = step.split()
            getattr(self, kind)(piece)


    def spread(self, tag, p, device, dp=None, y=None, z=0, count=4):
        block = lambda: region(self.weights, p, self.dp if dp is None else dp, self.y if y is None else y, z, count)
        self.send(("w", p, tag), block, block, device)

    def share(self, p):
        for k in (1, 3, 2):
            if p[0] in "OD":
                block = lambda: getattr(self, "slip" + p).at[self.z]
                self.send(("w", p, f"z{k}"), block, block, self.zn[k])
            else:
                self.spread(f"z{k}", p, self.zn[k], z=self.z, count=1)

    def line(self, p):
        self.arrived(*[("w", p, f"z{k}") for k in (1, 2, 3)])
        if p[0] in "OD":
            slips = [getattr(self, "slip" + p)[z].astype(F32) for z in range(4)]
            if p == "O":
                whole = jnp.concatenate([slip[:, :OW] for slip in slips], axis=1)
            else:
                whole = jnp.concatenate([slip[:QB] for slip in slips], axis=0)
            region(self.weights, p, self.dp, self.y)[...] = whole.astype(BF)
        self.spread("x", p, self.xn)
        self.spread("y", p, self.yn)
        self.spread("s", p, self.sib)

    def cross(self, p):
        self.arrived(("w", p, "x"))
        self.spread("xy", p, self.yn, dp=self.far, count=2)
        self.spread("sx", p, self.sib, dp=self.far)
        self.arrived(("w", p, "y"))
        self.spread("yx", p, self.xn, y=self.ny, z=2, count=2)
        self.spread("sy", p, self.sib, y=self.ny)

    def rest(self, p):
        self.arrived(("w", p, "xy"))
        self.spread("sxy", p, self.sib, dp=self.far, y=self.ny, count=2)
        self.arrived(("w", p, "yx"))
        self.spread("syx", p, self.sib, dp=self.far, y=self.ny, z=2, count=2)

    def end(self, p):
        self.arrived(*[("w", p, tag) for tag in ("s", "sx", "sy", "sxy", "syx")])


    def term(self, p, dp, y, z=0, count=4):
        return region(self.grads, p, dp, y, z, count)

    def add(self, p, dp, y, z, count, came):
        at = self.term(p, dp, y, z, count)
        at[...] = at[...] + came[...]

    def sibs(self, p):
        for i in range(4):
            src = lambda i=i: self.term(p, *self.theirs[i])
            self.send(("g", p, "s", i), src, lambda i=i: getattr(self, "one" + p).at[i], self.sib)

    def pair(self, p):
        for i in range(4):
            self.arrived(("g", p, "s", i))
            self.add(p, *self.mine[i], 0, 4, getattr(self, "one" + p).at[i])
            if i < 2:
                src = lambda i=i: self.term(p, *self.mine[i], 0, 2)
                self.send(("g", p, "y", i), src, lambda i=i: getattr(self, "twoy" + p).at[i], self.yn)
            if i in (0, 2):
                src = lambda i=i: self.term(p, *self.mine[i], 2, 2)
                self.send(("g", p, "x", i // 2), src, lambda i=i: getattr(self, "twox" + p).at[i // 2], self.xn)

    def twos(self, p):
        self.arrived(("g", p, "y", 0))
        self.add(p, self.far, self.y, 0, 2, getattr(self, "twoy" + p).at[0])
        src = lambda: self.term(p, self.far, self.y, 0, 2)
        self.send(("g", p, "yx"), src, lambda: getattr(self, "threex" + p), self.xn)
        self.arrived(("g", p, "x", 0))
        self.add(p, self.dp, self.ny, 2, 2, getattr(self, "twox" + p).at[0])
        src = lambda: self.term(p, self.dp, self.ny, 2, 2)
        self.send(("g", p, "xy"), src, lambda: getattr(self, "threey" + p), self.yn)

    def fours(self, p):
        self.arrived(("g", p, "y", 1), ("g", p, "x", 1), ("g", p, "yx"), ("g", p, "xy"))
        for z, two, three in ((0, "twoy", "threex"), (2, "twox", "threey")):
            at = self.term(p, self.dp, self.y, z, 2)
            at[...] = at[...] + getattr(self, two + p)[1] + getattr(self, three + p)[...]
        if p[0] in "OD":
            line = self.term(p, self.dp, self.y)[...].astype(F32)
            for z in range(4):
                getattr(self, "part" + p)[z] = cut(p, line, z).astype(BF)
        for k in (1, 3, 2):
            if p[0] in "OD":
                src = lambda k=k: getattr(self, "part" + p).at[self.peer[k]]
            else:
                src = lambda k=k: self.term(p, self.dp, self.y, self.peer[k], 1)
            self.send(("g", p, "z", k), src, lambda k=k: getattr(self, "four" + p).at[k - 1], self.zn[k])

    def total(self, p):
        own = getattr(self, "part" + p)[self.z] if p[0] in "OD" else self.term(p, self.dp, self.y, self.z, 1)[...]
        total = own.astype(F32)
        for k in (1, 2, 3):
            self.arrived(("g", p, "z", k))
            total = total + getattr(self, "four" + p)[k - 1].astype(F32)
        if p[0] == "D":
            first, size = CUT[p]
            self.sumD[:, first : first + size] = total[:QB, :]
        else:
            at = 128 * ("A", "O", "G0", "G1", "G2").index("A" if p[0] == "A" else p)
            first, size = CUT.get(p, (0, ROWS))
            self.sumN[first : first + size, at : at + 128] = total


    def tiny(self, step):
        step = int(step)
        if step > 0:
            self.arrived(("t", step - 1))
            self.tinies[step] = self.tinies[step - 1] + self.tinyin[step - 1]
        if step < 3:
            device = (self.sib, self.xn, self.yn)[step]
            self.send(("t", step), lambda: self.tinies.at[step], lambda: self.tinyin.at[step], device)
        else:
            for k in (1, 2, 3):
                self.send(("t", step, k), lambda: self.tinies.at[3], lambda k=k: self.tinyz.at[k], self.zn[k])

    def tiny_end(self):
        self.tinyz[0] = self.tinies[3]
        for k in (1, 2, 3):
            self.arrived(("t", 3, k))
        total = None
        for z in range(4):
            term = self.tinyz[lax.rem(self.z - z + 4, 4)]
            total = term if total is None else total + term
        self.sumT[...] = total


def rooms():
    shapes = {}
    for p in PIECES:
        shapes["one" + p] = ((4,) + shape_of(p, 4), BF)
        for room in ("twoy", "twox"):
            shapes[room + p] = ((2,) + shape_of(p, 2), BF)
        for room in ("threex", "threey"):
            shapes[room + p] = (shape_of(p, 2), BF)
        shapes["four" + p] = ((3,) + slip_shape(p), BF)
        if p[0] in "OD":
            shapes["slip" + p] = ((4,) + slip_shape(p), BF)
            shapes["part" + p] = ((4,) + slip_shape(p), BF)
    shapes["tinies"] = ((4, 8, D), F32)
    shapes["tinyin"] = ((3, 8, D), F32)
    shapes["tinyz"] = ((4, 8, D), F32)
    return shapes


COPIES = len(PIECES) * (12 + 13) + 6


def pack_own(links, refs):
    rows = lambda *names: [refs[n][...].astype(F32) for n in names]
    q, k, v, o, g, u, d = rows("q", "k", "v", "o", "g", "u", "d")
    gu = jnp.concatenate([g, u], axis=1)
    a = jnp.concatenate([q, k.T, v.T, o[:, OW:]], axis=1)
    whole = dict(A0=a[:80], A1=a[80:], G0=gu[:, :128], G1=gu[:, 128:256], G2=gu[:, 256:])
    for p in PIECES:
        if p == "O":
            links.slipO[links.z] = cut(p, o, 0).astype(BF)
        elif p[0] == "D":
            first, size = CUT[p]
            getattr(links, "slip" + p)[links.z] = cut(p, d[:, first : first + size], 0).astype(BF)
        else:
            region(links.weights, p, links.dp, links.y, links.z, 1)[...] = whole[p].astype(BF)


BEGIN = ("share A0", "share A1", "share O", "share G0", "share G1", "share G2", "share D0", "share D1")
BEFORE_PROJECT = (
    "line A0", "line A1", "cross A0", "line O", "cross A1", "line G0", "rest A0", "cross O", "line G1", "rest A1", "line G2",
    "end A0", "end A1",
)
AFTER_PROJECT = ("cross G0", "rest O")
HEADS = (("line D0", "cross G1"), ("rest G0", "line D1"), ("end O", "cross G2"))
BEFORE_OUT = ()
BEFORE_MLP = ("rest G1", "cross D0", "rest G2", "end G0", "end G1", "end G2")
MLP = (("cross D1", "rest D0"), ("rest D1", "end D0", "end D1"))
AFTER_DOWN = ("sibs D1", "sibs D0")
HIDDEN = (("pair D1",), ("pair D0",), (), ())
AFTER_GATE = (("sibs G0", "twos D1"), ("sibs G1",), ("pair G0", "sibs G2", "twos D0"))
BEFORE_NORM = ("pair G1", "twos G0")
AFTER_OUT = ("sibs O", "pair G2")
BEFORE_HEADS = ("fours D1",)
BACK_HEADS = (("twos G1", "pair O"), ("fours D0", "twos G2"), ("fours G0", "twos O"))
AFTER_QKV = ("sibs A0", "sibs A1", "fours G1", "pair A0", "pair A1")
LAST = (
    "tiny 0", "fours G2", "fours O", "tiny 1", "total D1", "total D0", "twos A0", "tiny 2", "twos A1", "total G0",
)
VERY_LAST = ("fours A0", "total G1", "tiny 3", "total G2", "total O", "fours A1", "total A0", "total A1")


def whole_kernel(order, names, *args):
    refs = dict(zip(names, args))
    w, links = Work(order, refs), Links(refs)
    links.greet()
    pack_own(links, refs)
    links.met()
    links.run(*BEGIN)
    w.start()
    applications(w, links)
    links.tinies[0] = w.small()
    links.run(*LAST)
    w.write_grad()
    links.run(*VERY_LAST)
    links.tiny_end()
    links.finish()


def finish_kernel(*refs):
    out, gin, sums, sumd, tiny, oout, ogin, ga, q, k, v, o, gm, g, u, d, rms = refs
    oout[...] = out[...]
    ogin[...] = gin[...]
    q[...] = sums[:, :QB]
    k[...] = sums[:, QB : QB + KB].T
    v[...] = sums[:, QB + KB : 120].T
    o[...] = jnp.concatenate([sums[:, 128 : 128 + OW], sums[:, 120:128]], axis=1)
    g[...] = sums[:, 256 : 256 + FB]
    u[...] = sums[:, 256 + FB : 256 + 2 * FB]
    d[...] = sumd[...]
    ga[...] = tiny[0:1, :].reshape(D)
    gm[...] = tiny[1:2, :].reshape(D)
    lane = lax.broadcasted_iota(jnp.int32, (1, 3), 1)
    for r in range(2):
        first, second, third = [tiny[2 + 3 * r + i : 3 + 3 * r + i, 0:3] for i in range(3)]
        squares = jnp.where(lane == 0, first, jnp.where(lane == 1, second, third))
        rms[r : r + 1, :] = jnp.sqrt(squares / (tiny[2:3, 128:131] * D))


def whole(x, length, ga, q, k, v, o, gm, g, u, d, ct):
    order = [2 * (b % 4) + b // 4 for b in range(NF)]
    cos, sin = rope_tables()
    ins = dict(
        length=length, x=x[0].T, ct=ct[0].T, ga=ga, gm=gm, cos=jnp.asarray(cos), sin=jnp.asarray(sin),
        q=q, k=k.T, v=v.T, o=o, g=g, u=u, d=d.T,
    )
    outs = dict(
        out=((D, T), BF), gin=((D, T), F32), sumN=((ROWS, 256 + 2 * FB), F32), sumD=((QB, LANES), F32), sumT=((8, D), F32)
    )
    scratch = dict(SCRATCH, **WEIGHTS, **GRADS, **rooms())
    names = list(ins) + list(outs) + list(scratch) + ["sent", "came"]
    vmem = pl.BlockSpec(memory_space=pltpu.VMEM)
    r = pl.pallas_call(
        functools.partial(whole_kernel, order, names),
        out_shape=[jax.ShapeDtypeStruct(*s) for s in outs.values()],
        in_specs=[pl.BlockSpec(memory_space=pltpu.SMEM)] + [vmem] * (len(ins) - 1),
        out_specs=[vmem] * len(outs),
        scratch_shapes=[pltpu.VMEM(*s) for s in scratch.values()]
        + [pltpu.SemaphoreType.DMA((COPIES,)), pltpu.SemaphoreType.DMA((COPIES,))],
        compiler_params=pltpu.CompilerParams(
            vmem_limit_bytes=VMEM_LIMIT, collective_id=0, has_side_effects=True
        ),
    )(*ins.values())
    rows = [
        ((D, T), BF), ((D, T), F32), ((D,), F32), (q.shape, F32), (k.shape[::-1], F32), (v.shape[::-1], F32),
        (o.shape, F32), ((D,), F32), (g.shape, F32), (u.shape, F32), (d.shape[::-1], F32), ((2, 3), F32),
    ]
    out, gin, ga, q, k, v, o, gm, g, u, d, rms = pl.pallas_call(
        finish_kernel,
        out_shape=[jax.ShapeDtypeStruct(*s) for s in rows],
        in_specs=[vmem] * len(outs),
        out_specs=[vmem] * len(rows),
    )(*r)
    return out.T[None], gin.T[None], ga, q, k.T, v.T, o, gm, g, u, d.T, rms


def by_collectives(x, length, ga, q, k, v, o, gm, g, u, d, ct):
    order = list(range(NF))
    full = [lax.all_gather(lax.all_gather(w, "fsdp", axis=1, tiled=True), "dp", axis=0, tiled=True) for w in (q, k, v, o, g, u, d)]
    packed = pack(order, *full)
    results = [local_compute(order, x[i].T, length[i : i + 1], ga, gm, ct[i].T, packed) for i in range(x.shape[0])]
    out = jnp.stack([r["out"].T for r in results])
    gin = jnp.stack([r["gin"].T for r in results])
    tiny = lax.psum(sum(r["tiny"] for r in results), ("dp", "fsdp"))
    terms = [unpack(order, r) for r in results]
    grads = [
        lax.psum_scatter(
            lax.psum_scatter(sum(t), "dp", scatter_dimension=0, tiled=True), "fsdp", scatter_dimension=1, tiled=True
        )
        for t in zip(*terms)
    ]
    rms = jnp.sqrt(tiny[2:8, 0].reshape(2, 3) / (tiny[2, 128] * D))
    gq, gk, gv, go, gg, gu, gd = grads
    return out, gin, tiny[0], gq, gk, gv, go, tiny[1], gg, gu, gd, rms


def solution(mesh):
    blocks = P("dp", "fsdp")
    slots = P(("dp", "fsdp"), None, None)
    in_specs = (slots, P(("dp", "fsdp")), P(), blocks, blocks, blocks, blocks, P(), blocks, blocks, blocks, slots)
    out_specs = (slots, slots, P(), blocks, blocks, blocks, blocks, P(), blocks, blocks, blocks, P())

    def on_device(*args):
        fits = mesh.shape["dp"] == 4 and mesh.shape["fsdp"] == 8 and args[0].shape[0] == 1
        return (whole if fits else by_collectives)(*args)

    return jax.shard_map(on_device, mesh=mesh, in_specs=in_specs, out_specs=out_specs, check_vma=False)
```

```python
import functools
import jax
import jax.numpy as jnp
import numpy as np
from jax import lax
from jax.experimental import pallas as pl
from jax.experimental.pallas import tpu as pltpu
from jax.sharding import PartitionSpec as P

D = 576
NQ = 9
NK = 3
GROUP = NQ // NK
H = 64
HALF = H // 2
FF = 1536
T = 512
NF = 8
QB = D // NF
KB = NK * H // NF
FB = FF // NF
EPS = 1e-05
ROPE_BASE = 10000.0
SCALE = H ** (-0.5)
NEG = -1e30
BLK = 256
VMEM_LIMIT = 63 * 2**20
ROWS = D // 4
LANES = FF // 4
OW = QB - 8
BF = jnp.bfloat16
F32 = jnp.float32


def dot(a, b, ca, cb):
    return lax.dot_general(a, b, (((ca,), (cb,)), ((), ())), preferred_element_type=F32)


def rope_tables():
    inverse = ROPE_BASE ** (-(2.0 * np.arange(HALF, dtype=np.float64)) / H)
    angles = inverse[:, None] * np.arange(T, dtype=np.float64)[None, :]
    return np.cos(angles).astype(np.float32), np.sin(angles).astype(np.float32)


def parts_of(row):
    hi = row.astype(BF).astype(F32)
    rest = row - hi
    mid = rest.astype(BF).astype(F32)
    return [hi, mid, rest - mid]


def lane_tiles():
    return [slice(128 * i, 128 * i + 128) for i in range(T // 128)]


class Work:
    def __init__(self, order, refs):
        self.order = order
        self.__dict__.update(refs)

    def start(self):
        count = self.length[0]
        place = lax.broadcasted_iota(jnp.int32, (8, T), 1)
        valid = (place < count).astype(F32)
        self.valid[...] = valid
        for ts in lane_tiles():
            self.S[0, :, ts] = self.x[:, ts].astype(F32)
            self.G[:, ts] = jnp.where(valid[0:1, ts] > 0.0, self.ct[:, ts].astype(F32), 0.0)
        self.gainA[...] = jnp.broadcast_to(self.ga[...].reshape(1, D), (128, D)).T
        self.gainM[...] = jnp.broadcast_to(self.gm[...].reshape(1, D), (128, D)).T
        row = lax.broadcasted_iota(jnp.int32, (H, 1024), 0)
        lane = lax.broadcasted_iota(jnp.int32, (H, 1024), 1)
        self.pick[...] = jnp.where(lane == 128 * (row // 8) + 120 + lax.rem(row, 8), 1.0, 0.0).astype(BF)
        self.gacc[...] = jnp.zeros_like(self.gacc)
        def blank(h, carry):
            self.QA[0, h, H:, :] = jnp.zeros((H, T), BF)
            self.QA[1, h, H:, :] = jnp.zeros((H, T), BF)
            self.DOA[h, H:, :] = jnp.zeros((H, T), BF)
            return carry

        lax.fori_loop(0, NQ, blank, 0)

        def clear(i, carry):
            rows = pl.ds(pl.multiple_of(i * 64, 64), 64)
            self.DA[rows, :] = jnp.zeros((64, 1024), BF)
            self.DO[rows, :] = jnp.zeros((64, D), BF)
            self.DD[rows, :] = jnp.zeros((64, FF), BF)
            for k in range(3):
                self.DG[k, rows, :] = jnp.zeros((64, 1024), BF)
            return carry

        lax.fori_loop(0, D // 64, clear, 0)

    def norm(self, src, r, gain, dst, rho_ref, row):
        for ts in lane_tiles():
            v = src[r, :, ts]
            total = jnp.sum(v * v, axis=0, keepdims=True)
            if row is not None:
                self.stat[r, row : row + 1, ts] = total
            rho = lax.rsqrt(total * (1.0 / D) + EPS)
            rho_ref[r, 0:1, ts] = rho
            dst[r, :, ts] = (v * rho * gain[...]).astype(BF)

    def natural_rows(self, ref, base, width, first, count):
        pieces = []
        row = first
        while row < first + count:
            f, i = row // width, row % width
            n = min(width - i, first + count - row)
            at = 128 * self.order.index(f) + base + i
            pieces.append(ref[at : at + n, :])
            row += n
        return pieces[0] if len(pieces) == 1 else jnp.concatenate(pieces, axis=0)

    def prepare(self, r):
        self.norm(self.S, r, self.gainA, self.XA, self.rhoA, 0)

    def project(self, r):
        def part(c, carry):
            cs = pl.ds(pl.multiple_of(512 * c, 512), 512)
            self.Y[cs, :] = dot(self.WA[:, cs], self.XA[r], 0, 0)
            return carry

        for c in range(2):
            part(c, 0)
        cos, sin = self.cos[...], self.sin[...]
        one = jnp.ones((1, T), F32)
        place = lax.broadcasted_iota(jnp.int32, (1, T), 1)
        bias = jnp.where(place < self.length[0], 0.0, NEG)
        for h in range(NQ + NK):
            base, width, at = (0, QB, h) if h < NQ else (QB, KB, h - NQ)
            a = self.natural_rows(self.Y, base, width, H * at, HALF)
            b = self.natural_rows(self.Y, base, width, H * at + HALF, HALF)
            first, second = a * cos - b * sin, b * cos + a * sin
            if h < NQ:
                self.QA[r, h, 0:HALF, :] = (first * SCALE).astype(BF)
                self.QA[r, h, HALF:H, :] = (second * SCALE).astype(BF)
                self.QA[r, h, H : H + 16, :] = jnp.concatenate([one, jnp.zeros((15, T), F32)], axis=0).astype(BF)
            else:
                g = h - NQ
                key = jnp.concatenate([first, second], axis=0)
                self.KT[r, g] = key.astype(BF)
                v = jnp.concatenate(
                    [
                        self.natural_rows(self.Y, QB + KB, KB, H * g, HALF),
                        self.natural_rows(self.Y, QB + KB, KB, H * g + HALF, HALF),
                    ],
                    axis=0,
                )
                self.VT[g] = v.astype(BF)
                ones3 = jnp.ones((3, T), F32)
                tail = jnp.zeros((H - 4, T), F32)
                ktall = jnp.concatenate([key, bias, ones3, tail], axis=0)
                vtall = jnp.concatenate([v, jnp.zeros((1, T), F32), ones3, tail], axis=0)
                for ts in lane_tiles():
                    self.KTOK[r, g, ts, :] = ktall[:, ts].T.astype(BF)
                    self.VTOK[r, g, ts, :] = vtall[:, ts].T.astype(BF)

    def diagonal(self):
        key = lax.broadcasted_iota(jnp.int32, (BLK, BLK), 0)
        query = lax.broadcasted_iota(jnp.int32, (BLK, BLK), 1)
        return key <= query

    def attend(self, r, links):
        low, high = slice(0, BLK), slice(BLK, T)

        def head(h, carry):
            g = h // GROUP
            allowed = self.diagonal()
            at = pl.ds(pl.multiple_of(h * H, H), H)
            s = dot(self.KTOK[r, g, low, :], self.QA[r, h, :, low], 1, 0)
            s = jnp.where(allowed, s, NEG)
            top = jnp.max(s, axis=0, keepdims=True)
            p = jnp.exp(s - top)
            total = jnp.sum(p, axis=0, keepdims=True)
            o = dot(self.VT[g, :, low], p.astype(BF), 1, 0)
            self.AT[r, at, low] = (o * (1.0 / total)).astype(BF)
            lse0 = top + jnp.log(total)
            s0 = dot(self.KTOK[r, g, low, :], self.QA[r, h, :, high], 1, 0)
            s1 = dot(self.KTOK[r, g, high, :], self.QA[r, h, :, high], 1, 0)
            s1 = jnp.where(allowed, s1, NEG)
            top = jnp.maximum(jnp.max(s0, axis=0, keepdims=True), jnp.max(s1, axis=0, keepdims=True))
            p0 = jnp.exp(s0 - top)
            p1 = jnp.exp(s1 - top)
            total = jnp.sum(p0, axis=0, keepdims=True) + jnp.sum(p1, axis=0, keepdims=True)
            o = dot(self.VT[g, :, low], p0.astype(BF), 1, 0) + dot(self.VT[g, :, high], p1.astype(BF), 1, 0)
            self.AT[r, at, high] = (o * (1.0 / total)).astype(BF)
            lse1 = top + jnp.log(total)
            lse = jnp.concatenate([lse0, lse1], axis=1)
            rows = [jnp.ones((1, T), F32)] + parts_of(-lse) + [jnp.zeros((12, T), F32)]
            self.QA[r, h, H : H + 16, :] = jnp.concatenate(rows, axis=0).astype(BF)
            return carry

        def group(g, carry):
            [head(GROUP * g + k, 0) for k in range(GROUP)]
            links.run_if(r == 0, HEADS[g])
            return carry

        for g in range(NK):
            group(g, 0)

    def rest_of_output(self):
        self.WO[:, NF * OW :] = dot(self.WA[...], self.pick[...], 1, 1).astype(BF)

    def after(self, value, src, r, dst, to, row, squares):
        n = value.shape[0]
        dst[to, row : row + n, :] = src[r, row : row + n, :] + value
        for i in range(n // 8):
            part = value[8 * i : 8 * i + 8]
            squares = squares + part * part
        return squares

    def out_project(self, r):
        self.Y[0:D, :] = dot(self.WO[...], self.AT[r], 0, 0)
        squares = jnp.zeros((8, T), F32)
        for b in range(NF):
            f = self.order[b]
            squares = self.after(self.Y[OW * b : OW * b + OW, :], self.S, r, self.M, r, QB * f, squares)
            at = NF * OW + 8 * b
            squares = self.after(self.Y[at : at + 8, :], self.S, r, self.M, r, QB * f + OW, squares)
        self.stat[r, 1:2, :] = jnp.sum(squares, axis=0, keepdims=True)

    def mlp(self, r, links):
        self.norm(self.M, r, self.gainM, self.XM, self.rhoM, None)

        def half(y, carry):
            cs = pl.ds(pl.multiple_of(512 * y, 512), 512)

            def part(i, carry):
                to = pl.ds(pl.multiple_of(512 * i, 512), 512)
                self.Y[to, :] = dot(self.WG[i, :, cs], self.XM[r], 0, 0)
                return carry

            for i in range(3):
                part(i, 0)

            def block(z, carry):
                f = self.natural(y, z)
                for j in range(3):
                    gate_at, up_at = self.places(j)
                    gate = self.Y[pl.ds(pl.multiple_of(gate_at[0] * 512 + 128 * z + gate_at[1], 64), 64), :]
                    up = self.Y[pl.ds(pl.multiple_of(up_at[0] * 512 + 128 * z + up_at[1], 64), 64), :]
                    rows = pl.ds(pl.multiple_of(FB * f + 64 * j, 64), 64)
                    self.GATE[r, rows, :] = gate.astype(BF)
                    self.UP[r, rows, :] = up.astype(BF)
                    self.HID[r, rows, :] = (gate * jax.nn.sigmoid(gate) * up).astype(BF)
                return carry

            for z in range(4):
                block(z, 0)
            links.run_if(r == 0, MLP[y])
            return carry

        for y in range(2):
            half(y, 0)
        self.Y[0:D, :] = dot(self.WDT[...], self.HID[r], 1, 0)
        squares = jnp.zeros((8, T), F32)
        for b in range(NF):
            squares = self.after(self.Y[QB * b : QB * b + QB, :], self.M, r, self.S, r + 1, QB * self.order[b], squares)
        self.stat[r, 2:3, :] = jnp.sum(squares, axis=0, keepdims=True)

    def natural(self, y, z):
        return 2 * z + y if self.order[1] == 2 else 4 * y + z

    def places(self, j):
        return ((0, 0), (0, 64), (1, 0))[j], ((1, 64), (2, 0), (2, 64))[j]

    def write_output(self):
        valid = self.valid[0:1, :]
        for ts in lane_tiles():
            v = jnp.where(valid[:, ts] > 0.0, self.S[2, :, ts], 0.0)
            self.out[:, ts] = v.astype(BF)

    def pack_down(self):
        for k in range(NF // 2):
            rows = [self.G[QB * self.order[b] : QB * self.order[b] + QB, :] for b in (2 * k, 2 * k + 1)]
            self.GLD[2 * QB * k : 2 * QB * k + 2 * QB, :] = jnp.concatenate(rows, axis=0).astype(BF)

    def pack_out(self):
        tails = []
        for b in range(NF):
            at = QB * self.order[b]
            self.GLO[OW * b : OW * b + OW, :] = self.G[at : at + OW, :].astype(BF)
            tails.append(self.G[at + OW : at + QB, :])
        self.GLO[NF * OW : D, :] = jnp.concatenate(tails, axis=0).astype(BF)

    def add_term(self, dst, index, value):
        dst[index] = (value + dst[index].astype(F32)).astype(dst.dtype)

    def norm_back(self, src, r, rho_ref, gain, slot):
        for ts in lane_tiles():
            e, v, rho = self.E[:, ts], src[r, :, ts], rho_ref[r, 0:1, ts]
            u = e * gain[...]
            mean = jnp.sum(u * v, axis=0, keepdims=True) * (1.0 / D)
            self.gacc[slot] += e * (v * rho)
            self.G[:, ts] = self.G[:, ts] + rho * (u - v * (rho * rho * mean))

    def mlp_back(self, r, links):
        self.pack_down()
        for c in range(2):
            cs = slice(768 * c, 768 * c + 768)
            self.add_term(self.DD, (slice(None), cs), dot(self.GLD[...], self.HID[r, cs, :], 1, 1))
        links.run_if(r == 0, AFTER_DOWN)

        def hidden(k, carry):
            rows = pl.ds(pl.multiple_of(2 * FB * k, 128), 2 * FB)
            self.Y[0 : 2 * FB, :] = dot(self.WDT[:, rows], self.GLD[...], 0, 0)
            for m in range(2):
                f = 2 * k + m
                b = k + 4 * m if self.order[1] == 2 else f
                for j in range(3):
                    at = pl.ds(pl.multiple_of(FB * f + 64 * j, 64), 64)
                    grad = self.Y[FB * m + 64 * j : FB * m + 64 * j + 64, :]
                    gate = self.GATE[r, at, :].astype(F32)
                    up = self.UP[r, at, :].astype(F32)
                    sig = jax.nn.sigmoid(gate)
                    silu = gate * sig
                    gate_at, up_at = self.places(j)
                    to = pl.ds(pl.multiple_of(1024 * gate_at[0] + 128 * b + gate_at[1], 64), 64)
                    self.DGU[to, :] = (grad * up * (sig + silu * (1.0 - sig))).astype(BF)
                    to = pl.ds(pl.multiple_of(1024 * up_at[0] + 128 * b + up_at[1], 64), 64)
                    self.DGU[to, :] = (grad * silu).astype(BF)
            links.run_if(r == 0, HIDDEN[k])
            return carry

        for k in range(4):
            hidden(k, 0)

        def matrix(i, carry):
            grad = self.DGU[pl.ds(pl.multiple_of(1024 * i, 1024), 1024), :]
            self.add_term(self.DG, (i,), dot(self.XM[r], grad, 1, 1))
            links.run_if(r == 0, AFTER_GATE[i])
            return carry

        for i in range(3):
            matrix(i, 0)
        self.E[...] = dot(self.WG[0], self.DGU[0:1024, :], 1, 0)

        def back(i, carry):
            grad = self.DGU[pl.ds(pl.multiple_of(1024 * i, 1024), 1024), :]
            self.E[...] = self.E[...] + dot(self.WG[i], grad, 1, 0)
            return carry

        for i in (1, 2):
            back(i, 0)
        links.run_if(r == 0, BEFORE_NORM)
        self.norm_back(self.M, r, self.rhoM, self.gainM, 1)

    def attend_back(self, r, links):
        self.pack_out()
        term = dot(self.AT[r], self.GLO[0:D, :], 1, 1)
        self.add_term(self.DO, (slice(None), slice(0, NF * OW)), term[:, : NF * OW])
        self.DO[:, NF * OW :] = term[:, NF * OW :].astype(BF)
        links.run_if(r == 0, AFTER_OUT)
        self.E[...] = dot(self.WO[...], self.GLO[0:D, :], 1, 0)
        links.run_if(r == 0, BEFORE_HEADS)
        for h in range(NQ):
            rows = slice(H * h, H * h + H)
            do = self.E[rows, :].astype(BF)
            self.DOA[h, 0:H, :] = do
            delta = jnp.sum(do.astype(F32) * self.AT[r, rows, :].astype(F32), axis=0, keepdims=True)
            rows = [jnp.zeros((1, T), F32)] + parts_of(-delta) + [jnp.zeros((12, T), F32)]
            self.DOA[h, H : H + 16, :] = jnp.concatenate(rows, axis=0).astype(BF)
        low, high = slice(0, BLK), slice(BLK, T)
        self.Y[D : D + 2 * NK * H, :] = jnp.zeros((2 * NK * H, T), F32)

        def head(h, carry):
            g = h // GROUP
            allowed = self.diagonal()
            at = pl.ds(pl.multiple_of(h * H, H), H)
            kat = pl.ds(pl.multiple_of(D + g * H, H), H)
            vat = pl.ds(pl.multiple_of(D + NK * H + g * H, H), H)
            q, do = self.QA[r, h], self.DOA[h]
            k0, k1 = self.KTOK[r, g, low, :], self.KTOK[r, g, high, :]
            v0, v1 = self.VTOK[r, g, low, :], self.VTOK[r, g, high, :]
            t0, t1 = self.KT[r, g, :, low], self.KT[r, g, :, high]

            p = jnp.where(allowed, jnp.exp(dot(k0, q[:, low], 1, 0)), 0.0)
            ds = (p * dot(v0, do[:, low], 1, 0)).astype(BF)
            p = p.astype(BF)
            self.Y[at, low] = dot(t0, ds, 1, 0) * SCALE
            dk0 = dot(q[0:H, low], ds, 1, 1)
            dv0 = dot(do[0:H, low], p, 1, 1)

            p = jnp.exp(dot(k0, q[:, high], 1, 0))
            ds = (p * dot(v0, do[:, high], 1, 0)).astype(BF)
            p = p.astype(BF)
            dq = dot(t0, ds, 1, 0)
            dk0 += dot(q[0:H, high], ds, 1, 1)
            dv0 += dot(do[0:H, high], p, 1, 1)

            p = jnp.where(allowed, jnp.exp(dot(k1, q[:, high], 1, 0)), 0.0)
            ds = (p * dot(v1, do[:, high], 1, 0)).astype(BF)
            p = p.astype(BF)
            self.Y[at, high] = (dq + dot(t1, ds, 1, 0)) * SCALE
            self.Y[kat, low] += dk0
            self.Y[vat, low] += dv0
            self.Y[kat, high] += dot(q[0:H, high], ds, 1, 1)
            self.Y[vat, high] += dot(do[0:H, high], p, 1, 1)
            return carry

        def group(g, carry):
            [head(GROUP * g + k, 0) for k in range(GROUP)]
            links.run_if(r == 0, BACK_HEADS[g])
            return carry

        for g in range(NK):
            group(g, 0)

    def project_back(self, r, links):
        cos, sin = self.cos[...], self.sin[...]
        for h in range(NQ + NK):
            first, second = slice(H * h, H * h + HALF), slice(H * h + HALF, H * h + H)
            a, b = self.Y[first, :], self.Y[second, :]
            self.Y[first, :] = a * cos + b * sin
            self.Y[second, :] = b * cos - a * sin
        for b in range(NF):
            f = self.order[b]
            rows = jnp.concatenate(
                [
                    self.Y[QB * f : QB * f + QB, :],
                    self.Y[D + KB * f : D + KB * f + KB, :],
                    self.Y[D + NK * H + KB * f : D + NK * H + KB * f + KB, :],
                    jnp.zeros((128 - QB - 2 * KB, T), F32),
                ],
                axis=0,
            )
            self.GLO[128 * b : 128 * b + 128, :] = rows.astype(BF)
        def part(c, carry):
            cs = pl.ds(pl.multiple_of(512 * c, 512), 512)
            term = dot(self.XA[r], self.GLO[cs, :], 1, 1) + dot(self.DO[:, NF * OW :], self.pick[:, cs], 1, 0)
            self.add_term(self.DA, (slice(None), cs), term)
            return carry

        for c in range(2):
            part(c, 0)
        links.run_if(r == 0, AFTER_QKV)
        self.E[...] = dot(self.WA[...], self.GLO[...], 1, 0)
        self.norm_back(self.S, r, self.rhoA, self.gainA, 0)

    def write_grad(self):
        for ts in lane_tiles():
            self.gin[:, ts] = self.G[:, ts]

    def small(self):
        valid = self.valid[0:1, :]
        rows = [jnp.sum(self.gacc[i].T, axis=0, keepdims=True) for i in range(2)]
        sums = jnp.sum(jnp.where(valid > 0.0, jnp.concatenate([self.stat[0, 0:3], self.stat[1, 0:3]], axis=0), 0.0), axis=1, keepdims=True)
        count = jnp.sum(valid, axis=1, keepdims=True)
        lane = lax.broadcasted_iota(jnp.int32, (6, D), 1)
        return jnp.concatenate(rows + [jnp.where(lane < 128, sums, count)], axis=0)


SCRATCH = dict(
    S=((3, D, T), F32), G=((D, T), F32), E=((D, T), F32), Y=((1536, T), F32),
    XA=((2, D, T), BF), XM=((2, D, T), BF), rhoA=((2, 8, T), F32), rhoM=((2, 8, T), F32),
    QA=((2, NQ, 128, T), BF), KT=((2, NK, H, T), BF), VT=((NK, H, T), BF),
    KTOK=((2, NK, T, 128), BF), VTOK=((2, NK, T, 128), BF), AT=((2, D, T), BF), M=((2, D, T), F32),
    GATE=((2, FF, T), BF), UP=((2, FF, T), BF), HID=((2, FF, T), BF),
    GLD=((D, T), BF), GLO=((1024, T), BF), DGU=((2 * FF, T), BF), DOA=((NQ, 128, T), BF),
    stat=((2, 8, T), F32), valid=((8, T), F32), gacc=((2, D, 128), F32), gainA=((D, 128), F32), gainM=((D, 128), F32), pick=((H, 1024), BF),
)
WEIGHTS = dict(WA=((D, 1024), BF), WO=((D, D), BF), WG=((3, D, 1024), BF), WDT=((D, FF), BF))
GRADS = dict(DA=((D, 1024), BF), DO=((D, D), BF), DG=((3, D, 1024), BF), DD=((D, FF), BF))

class Alone:
    def run_if(self, condition, steps):
        pass


def applications(w, links):
    def forward(r, carry):
        w.prepare(r)
        links.run_if(r == 0, BEFORE_PROJECT)
        w.project(r)
        links.run_if(r == 0, AFTER_PROJECT)
        w.attend(r, links)
        pl.when(r == 0)(w.rest_of_output)
        links.run_if(r == 0, BEFORE_OUT)
        w.out_project(r)
        links.run_if(r == 0, BEFORE_MLP)
        w.mlp(r, links)
        return carry

    def backward(i, carry):
        w.mlp_back(1 - i, links)
        w.attend_back(1 - i, links)
        w.project_back(1 - i, links)
        return carry

    lax.fori_loop(0, 2, forward, 0)
    w.write_output()
    lax.fori_loop(0, 2, backward, 0)


def compute_kernel(order, names, *refs):
    w = Work(order, dict(zip(names, refs)))
    w.start()
    applications(w, Alone())
    w.write_grad()
    w.tiny[...] = w.small()


def local_compute(order, x, length, ga, gm, ct, packed):
    cos, sin = rope_tables()
    ins = dict(length=length, x=x, ct=ct, ga=ga, gm=gm, cos=jnp.asarray(cos), sin=jnp.asarray(sin), **packed)
    outs = dict(out=((D, T), BF), gin=((D, T), F32), tiny=((8, D), F32), **GRADS)
    names = list(ins) + list(outs) + list(SCRATCH)
    vmem = pl.BlockSpec(memory_space=pltpu.VMEM)
    results = pl.pallas_call(
        functools.partial(compute_kernel, order, names),
        out_shape=[jax.ShapeDtypeStruct(*s) for s in outs.values()],
        in_specs=[pl.BlockSpec(memory_space=pltpu.SMEM)] + [vmem] * (len(ins) - 1),
        out_specs=[vmem] * len(outs),
        scratch_shapes=[pltpu.VMEM(*s) for s in SCRATCH.values()],
        compiler_params=pltpu.CompilerParams(vmem_limit_bytes=VMEM_LIMIT),
    )(*ins.values())
    return dict(zip(outs, results))


def pack(order, q, k, v, o, g, u, d):
    def cols(w, width):
        return w.reshape(w.shape[0], NF, width)[:, np.array(order)]
    ob = cols(o, QB)
    wa = jnp.concatenate([cols(q, QB), cols(k, KB), cols(v, KB), ob[:, :, OW:]], axis=2).reshape(D, 1024)
    wo = jnp.concatenate([ob[:, :, :OW].reshape(D, NF * OW), ob[:, :, OW:].reshape(D, D - NF * OW)], axis=1)
    wg = jnp.concatenate([cols(g, FB), cols(u, FB)], axis=2).reshape(D, NF, 3, 128)
    wg = wg.transpose(2, 0, 1, 3).reshape(3, D, 1024)
    wd = d.T.reshape(NF, QB, FF)[np.array(order)].reshape(D, FF)
    return dict(WA=wa, WO=wo, WG=wg, WDT=wd)


def unpack(order, r):
    back = np.argsort(np.array(order))
    a = r["DA"].astype(F32).reshape(D, NF, 128)[:, back]
    o = r["DO"][:, : NF * OW].astype(F32).reshape(D, NF, OW)[:, back]
    o = jnp.concatenate([o, a[:, :, 120:]], axis=2).reshape(D, D)
    g = r["DG"].astype(F32).reshape(3, D, NF, 128).transpose(1, 2, 0, 3).reshape(D, NF, 2 * FB)[:, back]
    d = r["DD"].astype(F32).reshape(NF, QB, FF)[back].reshape(D, FF).T
    return (
        a[:, :, :QB].reshape(D, D), a[:, :, QB : QB + KB].reshape(D, NK * H), a[:, :, QB + KB : 120].reshape(D, NK * H),
        o, g[:, :, :FB].reshape(D, FF), g[:, :, FB:].reshape(D, FF), d,
    )


PIECES = ("A0", "A1", "O", "G0", "G1", "G2", "D0", "D1")
CUT = dict(A0=(0, 80), A1=(80, ROWS - 80), D0=(0, 256), D1=(256, 128))
MESH = pl.DeviceIdType.MESH


def region(refs, piece, dp, y, z=0, count=4):
    ref, line = refs[piece[0]], 4 * y + z
    if piece[0] == "D":
        first, size = CUT[piece]
        rows = pl.ds(pl.multiple_of(QB * line, 16), QB * count)
        return ref.at[rows, pl.ds(pl.multiple_of(LANES * dp + first, 128), size)]
    width = OW if piece == "O" else 128
    first, size = CUT.get(piece, (0, ROWS))
    rows = pl.ds(pl.multiple_of(ROWS * dp + first, 16), size)
    lanes = pl.ds(pl.multiple_of(width * line, 128), width * count)
    return ref.at[int(piece[1]), rows, lanes] if piece[0] == "G" else ref.at[rows, lanes]


def shape_of(piece, count):
    if piece[0] == "D":
        return (QB * count, CUT[piece][1])
    return (CUT.get(piece, (0, ROWS))[1], (OW if piece == "O" else 128) * count)


def slip_shape(piece):
    return (QB + 8, CUT[piece][1]) if piece[0] == "D" else (CUT.get(piece, (0, ROWS))[1], 128)


def cut(piece, line, z):
    if piece == "O":
        return jnp.concatenate([line[:, OW * z : OW * z + OW]] * 2, axis=1)
    return jnp.concatenate([line[QB * z : QB * z + QB], jnp.zeros((8, line.shape[1]), F32)], axis=0)


def when(condition, action):
    if condition is None:
        action()
    else:
        pl.when(condition)(action)


class Links:
    def __init__(self, refs):
        self.__dict__.update(refs)
        self.weights = dict(A=refs["WA"], O=refs["WO"], G=refs["WG"], D=refs["WDT"])
        self.grads = dict(A=refs["DA"], O=refs["DO"], G=refs["DG"], D=refs["DD"])
        self.dp, f = lax.axis_index("dp"), lax.axis_index("fsdp")
        self.x, self.c = self.dp // 2, lax.rem(self.dp, 2)
        self.z, self.y = f // 2, lax.rem(f, 2)
        self.ny = 1 - self.y
        places = [(1 - self.x, self.ny), (self.x, self.ny), (1 - self.x, self.y), (self.x, self.y)]
        self.mine = [(2 * x + self.c, y) for x, y in places]
        self.theirs = [(2 * x + 1 - self.c, y) for x, y in places]
        self.far = 2 * (1 - self.x) + self.c
        self.other = 2 * self.x + 1 - self.c
        self.sib = (self.other, f)
        self.xn = (self.far, f)
        self.yn = (self.dp, 2 * self.z + 1 - self.y)
        self.peer = [None] + [lax.rem(self.z + k, 4) for k in (1, 2, 3)]
        self.zn = [None] + [(self.dp, 2 * self.peer[k] + self.y) for k in (1, 2, 3)]
        self.side = [None, (self.dp, 2 * (self.z + 1) + self.y), (self.dp, 2 * (self.z - 1) + self.y)]
        self.here = {(sign, t): (self.z + sign * t >= 0) & (self.z + sign * t < 4) for sign in (1, -1) for t in (1, 2, 3)}
        self.on = {(-1, 0): self.z < 3, (1, 0): self.z > 0}
        for sign, t in self.here:
            self.on[sign, t] = self.here[sign, t] & self.on[sign, 0]
        self.copies = {}
        self.used = 0

    def greet(self):
        for device in [self.sib, self.xn, self.yn] + self.zn[1:]:
            pl.semaphore_signal(pltpu.get_barrier_semaphore(), inc=1, device_id=device, device_id_type=MESH)

    def met(self):
        pl.semaphore_wait(pltpu.get_barrier_semaphore(), 6)

    def send(self, name, src, dst, device, condition=None):
        index = self.used
        self.used += 1

        def copy():
            return pltpu.make_async_remote_copy(
                src_ref=src(),
                dst_ref=dst(),
                send_sem=self.sent.at[index],
                recv_sem=self.came.at[index],
                device_id=device,
                device_id_type=MESH,
            )

        when(condition, lambda: copy().start())
        self.copies[name] = (copy, condition)

    def arrived(self, *names, condition=None):
        for name in names:
            when(condition, lambda name=name: self.copies[name][0]().wait_recv())

    def finish(self):
        for copy, condition in self.copies.values():
            when(condition, lambda copy=copy: copy().wait_send())

    def run_if(self, condition, steps):
        if steps:
            pl.when(condition)(functools.partial(self.run, *steps))

    def run(self, *steps):
        for step in steps:
            kind, piece = step.split()
            getattr(self, kind)(piece)


    def spread(self, tag, p, device, dp=None, y=None, z=0, count=4):
        block = lambda: region(self.weights, p, self.dp if dp is None else dp, self.y if y is None else y, z, count)
        self.send(("w", p, tag), block, block, device)

    def block(self, p, z):
        if p[0] in "OD":
            return getattr(self, "slip" + p).at[z]
        return region(self.weights, p, self.dp, self.y, z, 1)

    def hop(self, p, t):
        for tag, sign in (("r", -1), ("l", 1)):
            here = self.here.get((sign, t))
            if t > 0:
                self.arrived(("w", p, tag, t - 1), condition=here)
            block = lambda sign=sign: self.block(p, self.z + sign * t)
            if t < 3:
                self.send(("w", p, tag, t), block, block, self.side[-sign], self.on[sign, t])
            if p[0] in "AG" and t > 0:
                self.send(("w", p, "x", tag, t), block, block, self.xn, here)
                self.send(("w", p, "y", tag, t), block, block, self.yn, here)

    def own(self, p):
        for axis, device in (("x", self.xn), ("y", self.yn)):
            block = lambda: self.block(p, self.z)
            self.send(("w", p, axis, "r", 0), block, block, device)

    def share(self, p):
        self.hop(p, 0)

    def one(self, p):
        self.hop(p, 1)

    def two(self, p):
        self.hop(p, 2)

    def line(self, p):
        self.hop(p, 3)
        if p[0] in "OD":
            slips = [getattr(self, "slip" + p)[z].astype(F32) for z in range(4)]
            if p == "O":
                whole = jnp.concatenate([slip[:, :OW] for slip in slips], axis=1)
            else:
                whole = jnp.concatenate([slip[:QB] for slip in slips], axis=0)
            region(self.weights, p, self.dp, self.y)[...] = whole.astype(BF)
            self.spread("x", p, self.xn)
            self.spread("y", p, self.yn)
        self.spread("s", p, self.sib)

    def across(self, p, axis):
        if p[0] in "OD":
            self.arrived(("w", p, axis))
            return
        for t in range(4):
            for tag, sign in (("r", -1), ("l", 1)):
                if t > 0 or sign < 0:
                    self.arrived(("w", p, axis, tag, t), condition=self.here.get((sign, t)))

    def cross(self, p):
        self.across(p, "x")
        self.spread("xy", p, self.yn, dp=self.far, count=2)
        self.spread("sx", p, self.sib, dp=self.far)
        self.across(p, "y")
        self.spread("yx", p, self.xn, y=self.ny, z=2, count=2)
        self.spread("sy", p, self.sib, y=self.ny)

    def rest(self, p):
        self.arrived(("w", p, "xy"))
        self.spread("sxy", p, self.sib, dp=self.far, y=self.ny, count=2)
        self.arrived(("w", p, "yx"))
        self.spread("syx", p, self.sib, dp=self.far, y=self.ny, z=2, count=2)

    def end(self, p):
        self.arrived(*[("w", p, tag) for tag in ("s", "sx", "sy", "sxy", "syx")])


    def term(self, p, dp, y, z=0, count=4):
        return region(self.grads, p, dp, y, z, count)

    def add(self, p, dp, y, z, count, came):
        at = self.term(p, dp, y, z, count)
        at[...] = at[...] + came[...]

    def sibs(self, p):
        for i in range(4):
            src = lambda i=i: self.term(p, *self.theirs[i])
            self.send(("g", p, "s", i), src, lambda i=i: getattr(self, "one" + p).at[i], self.sib)

    def pair(self, p):
        for i in range(4):
            self.arrived(("g", p, "s", i))
            self.add(p, *self.mine[i], 0, 4, getattr(self, "one" + p).at[i])
            if i < 2:
                src = lambda i=i: self.term(p, *self.mine[i], 0, 2)
                self.send(("g", p, "y", i), src, lambda i=i: getattr(self, "twoy" + p).at[i], self.yn)
            if i in (0, 2):
                src = lambda i=i: self.term(p, *self.mine[i], 2, 2)
                self.send(("g", p, "x", i // 2), src, lambda i=i: getattr(self, "twox" + p).at[i // 2], self.xn)

    def twos(self, p):
        self.arrived(("g", p, "y", 0))
        self.add(p, self.far, self.y, 0, 2, getattr(self, "twoy" + p).at[0])
        src = lambda: self.term(p, self.far, self.y, 0, 2)
        self.send(("g", p, "yx"), src, lambda: getattr(self, "threex" + p), self.xn)
        self.arrived(("g", p, "x", 0))
        self.add(p, self.dp, self.ny, 2, 2, getattr(self, "twox" + p).at[0])
        src = lambda: self.term(p, self.dp, self.ny, 2, 2)
        self.send(("g", p, "xy"), src, lambda: getattr(self, "threey" + p), self.yn)

    def fours(self, p):
        self.arrived(("g", p, "y", 1), ("g", p, "x", 1), ("g", p, "yx"), ("g", p, "xy"))
        for z, two, three in ((0, "twoy", "threex"), (2, "twox", "threey")):
            at = self.term(p, self.dp, self.y, z, 2)
            at[...] = at[...] + getattr(self, two + p)[1] + getattr(self, three + p)[...]
        if p[0] in "OD":
            line = self.term(p, self.dp, self.y)[...].astype(F32)
            for z in range(4):
                getattr(self, "part" + p)[z] = cut(p, line, z).astype(BF)
        for k in (1, 3, 2):
            if p[0] in "OD":
                src = lambda k=k: getattr(self, "part" + p).at[self.peer[k]]
            else:
                src = lambda k=k: self.term(p, self.dp, self.y, self.peer[k], 1)
            self.send(("g", p, "z", k), src, lambda k=k: getattr(self, "four" + p).at[k - 1], self.zn[k])

    def total(self, p):
        own = getattr(self, "part" + p)[self.z] if p[0] in "OD" else self.term(p, self.dp, self.y, self.z, 1)[...]
        total = own.astype(F32)
        for k in (1, 2, 3):
            self.arrived(("g", p, "z", k))
            total = total + getattr(self, "four" + p)[k - 1].astype(F32)
        if p[0] == "D":
            first, size = CUT[p]
            self.sumD[:, first : first + size] = total[:QB, :]
        else:
            at = 128 * ("A", "O", "G0", "G1", "G2").index("A" if p[0] == "A" else p)
            first, size = CUT.get(p, (0, ROWS))
            self.sumN[first : first + size, at : at + 128] = total


    def tiny(self, step):
        step = int(step)
        if step > 0:
            self.arrived(("t", step - 1))
            self.tinies[step] = self.tinies[step - 1] + self.tinyin[step - 1]
        if step < 3:
            device = (self.sib, self.xn, self.yn)[step]
            self.send(("t", step), lambda: self.tinies.at[step], lambda: self.tinyin.at[step], device)
        else:
            for k in (1, 2, 3):
                self.send(("t", step, k), lambda: self.tinies.at[3], lambda k=k: self.tinyz.at[k], self.zn[k])

    def tiny_end(self):
        self.tinyz[0] = self.tinies[3]
        for k in (1, 2, 3):
            self.arrived(("t", 3, k))
        total = None
        for z in range(4):
            term = self.tinyz[lax.rem(self.z - z + 4, 4)]
            total = term if total is None else total + term
        self.sumT[...] = total


def rooms():
    shapes = {}
    for p in PIECES:
        shapes["one" + p] = ((4,) + shape_of(p, 4), BF)
        for room in ("twoy", "twox"):
            shapes[room + p] = ((2,) + shape_of(p, 2), BF)
        for room in ("threex", "threey"):
            shapes[room + p] = (shape_of(p, 2), BF)
        shapes["four" + p] = ((3,) + slip_shape(p), BF)
        if p[0] in "OD":
            shapes["slip" + p] = ((4,) + slip_shape(p), BF)
            shapes["part" + p] = ((4,) + slip_shape(p), BF)
    shapes["tinies"] = ((4, 8, D), F32)
    shapes["tinyin"] = ((3, 8, D), F32)
    shapes["tinyz"] = ((4, 8, D), F32)
    return shapes


COPIES = len(PIECES) * (6 + 14 + 7 + 13) + 6


def pack_own(links, refs):
    rows = lambda *names: [refs[n][...].astype(F32) for n in names]
    q, k, v, o, g, u, d = rows("q", "k", "v", "o", "g", "u", "d")
    gu = jnp.concatenate([g, u], axis=1)
    a = jnp.concatenate([q, k.T, v.T, o[:, OW:]], axis=1)
    whole = dict(A0=a[:80], A1=a[80:], G0=gu[:, :128], G1=gu[:, 128:256], G2=gu[:, 256:])
    for p in PIECES:
        if p == "O":
            links.slipO[links.z] = cut(p, o, 0).astype(BF)
        elif p[0] == "D":
            first, size = CUT[p]
            getattr(links, "slip" + p)[links.z] = cut(p, d[:, first : first + size], 0).astype(BF)
        else:
            region(links.weights, p, links.dp, links.y, links.z, 1)[...] = whole[p].astype(BF)


BEGIN = ("own A1", "share A1", "own A0", "share A0", "own G1", "own G2", "own G0", "share G0")
BEFORE_PROJECT = ("share G2", "one A1", "one A0", "share G1", "one G0", "one G2", "two A1", "two A0", "share O", "two G0", "two G2", "line A1", "line A0", "one G1", "share D1", "line G0", "one O", "line G2", "cross A1", "share D0", "two G1", "one D1", "cross A0", "two O", "cross G0", "line G1", "two D1", "one D0", "rest A0", "cross G2", "line O", "end A0", "rest A1", "two D0", "cross G1", "end A1")
AFTER_PROJECT = ("line D1", "cross O", "line D0")
HEADS = ((), ("rest G0", "rest G1", "rest G2", "rest O"), ("cross D1", "end O", "end G0"))
BEFORE_OUT = ()
BEFORE_MLP = ("end G1", "end G2", "cross D0")
MLP = (("rest D1",), ("rest D0", "end D0", "end D1"))
AFTER_DOWN = ("sibs D1", "sibs D0")
HIDDEN = (("pair D1",), ("pair D0",), (), ())
AFTER_GATE = (("sibs G0", "twos D1"), ("sibs G1",), ("pair G0", "sibs G2", "twos D0"))
BEFORE_NORM = ("pair G1", "twos G0")
AFTER_OUT = ("sibs O", "pair G2")
BEFORE_HEADS = ("fours D1",)
BACK_HEADS = (("twos G1", "pair O"), ("fours D0", "twos G2"), ("fours G0", "twos O"))
AFTER_QKV = ("sibs A0", "sibs A1", "fours G1", "pair A0", "pair A1")
LAST = (
    "tiny 0", "fours G2", "fours O", "tiny 1", "total D1", "total D0", "twos A0", "tiny 2", "twos A1", "total G0",
)
VERY_LAST = ("fours A0", "total G1", "tiny 3", "total G2", "total O", "fours A1", "total A0", "total A1")


def whole_kernel(order, names, *args):
    refs = dict(zip(names, args))
    w, links = Work(order, refs), Links(refs)
    links.greet()
    pack_own(links, refs)
    links.met()
    links.run(*BEGIN)
    w.start()
    applications(w, links)
    links.tinies[0] = w.small()
    links.run(*LAST)
    w.write_grad()
    links.run(*VERY_LAST)
    links.tiny_end()
    links.finish()


def finish_kernel(*refs):
    out, gin, sums, sumd, tiny, oout, ogin, ga, q, k, v, o, gm, g, u, d, rms = refs
    oout[...] = out[...]
    ogin[...] = gin[...]
    q[...] = sums[:, :QB]
    k[...] = sums[:, QB : QB + KB].T
    v[...] = sums[:, QB + KB : 120].T
    o[...] = jnp.concatenate([sums[:, 128 : 128 + OW], sums[:, 120:128]], axis=1)
    g[...] = sums[:, 256 : 256 + FB]
    u[...] = sums[:, 256 + FB : 256 + 2 * FB]
    d[...] = sumd[...]
    ga[...] = tiny[0:1, :].reshape(D)
    gm[...] = tiny[1:2, :].reshape(D)
    lane = lax.broadcasted_iota(jnp.int32, (1, 3), 1)
    for r in range(2):
        first, second, third = [tiny[2 + 3 * r + i : 3 + 3 * r + i, 0:3] for i in range(3)]
        squares = jnp.where(lane == 0, first, jnp.where(lane == 1, second, third))
        rms[r : r + 1, :] = jnp.sqrt(squares / (tiny[2:3, 128:131] * D))


def whole(x, length, ga, q, k, v, o, gm, g, u, d, ct):
    order = [2 * (b % 4) + b // 4 for b in range(NF)]
    cos, sin = rope_tables()
    ins = dict(
        length=length, x=x[0].T, ct=ct[0].T, ga=ga, gm=gm, cos=jnp.asarray(cos), sin=jnp.asarray(sin),
        q=q, k=k.T, v=v.T, o=o, g=g, u=u, d=d.T,
    )
    outs = dict(
        out=((D, T), BF), gin=((D, T), F32), sumN=((ROWS, 256 + 2 * FB), F32), sumD=((QB, LANES), F32), sumT=((8, D), F32)
    )
    scratch = dict(SCRATCH, **WEIGHTS, **GRADS, **rooms())
    names = list(ins) + list(outs) + list(scratch) + ["sent", "came"]
    vmem = pl.BlockSpec(memory_space=pltpu.VMEM)
    r = pl.pallas_call(
        functools.partial(whole_kernel, order, names),
        out_shape=[jax.ShapeDtypeStruct(*s) for s in outs.values()],
        in_specs=[pl.BlockSpec(memory_space=pltpu.SMEM)] + [vmem] * (len(ins) - 1),
        out_specs=[vmem] * len(outs),
        scratch_shapes=[pltpu.VMEM(*s) for s in scratch.values()]
        + [pltpu.SemaphoreType.DMA((COPIES,)), pltpu.SemaphoreType.DMA((COPIES,))],
        compiler_params=pltpu.CompilerParams(
            vmem_limit_bytes=VMEM_LIMIT, collective_id=0, has_side_effects=True
        ),
    )(*ins.values())
    rows = [
        ((D, T), BF), ((D, T), F32), ((D,), F32), (q.shape, F32), (k.shape[::-1], F32), (v.shape[::-1], F32),
        (o.shape, F32), ((D,), F32), (g.shape, F32), (u.shape, F32), (d.shape[::-1], F32), ((2, 3), F32),
    ]
    out, gin, ga, q, k, v, o, gm, g, u, d, rms = pl.pallas_call(
        finish_kernel,
        out_shape=[jax.ShapeDtypeStruct(*s) for s in rows],
        in_specs=[vmem] * len(outs),
        out_specs=[vmem] * len(rows),
    )(*r)
    return out.T[None], gin.T[None], ga, q, k.T, v.T, o, gm, g, u, d.T, rms


def by_collectives(x, length, ga, q, k, v, o, gm, g, u, d, ct):
    order = list(range(NF))
    full = [lax.all_gather(lax.all_gather(w, "fsdp", axis=1, tiled=True), "dp", axis=0, tiled=True) for w in (q, k, v, o, g, u, d)]
    packed = pack(order, *full)
    results = [local_compute(order, x[i].T, length[i : i + 1], ga, gm, ct[i].T, packed) for i in range(x.shape[0])]
    out = jnp.stack([r["out"].T for r in results])
    gin = jnp.stack([r["gin"].T for r in results])
    tiny = lax.psum(sum(r["tiny"] for r in results), ("dp", "fsdp"))
    terms = [unpack(order, r) for r in results]
    grads = [
        lax.psum_scatter(
            lax.psum_scatter(sum(t), "dp", scatter_dimension=0, tiled=True), "fsdp", scatter_dimension=1, tiled=True
        )
        for t in zip(*terms)
    ]
    rms = jnp.sqrt(tiny[2:8, 0].reshape(2, 3) / (tiny[2, 128] * D))
    gq, gk, gv, go, gg, gu, gd = grads
    return out, gin, tiny[0], gq, gk, gv, go, tiny[1], gg, gu, gd, rms


def solution(mesh):
    blocks = P("dp", "fsdp")
    slots = P(("dp", "fsdp"), None, None)
    in_specs = (slots, P(("dp", "fsdp")), P(), blocks, blocks, blocks, blocks, P(), blocks, blocks, blocks, slots)
    out_specs = (slots, slots, P(), blocks, blocks, blocks, blocks, P(), blocks, blocks, blocks, P())

    def on_device(*args):
        fits = mesh.shape["dp"] == 4 and mesh.shape["fsdp"] == 8 and args[0].shape[0] == 1
        return (whole if fits else by_collectives)(*args)

    return jax.shard_map(on_device, mesh=mesh, in_specs=in_specs, out_specs=out_specs, check_vma=False)
```

```python
import functools
import jax
import jax.numpy as jnp
import numpy as np
from jax import lax
from jax.experimental import pallas as pl
from jax.experimental.pallas import tpu as pltpu
from jax.sharding import PartitionSpec as P

D = 576
NQ = 9
NK = 3
GROUP = NQ // NK
H = 64
HALF = H // 2
FF = 1536
T = 512
NF = 8
QB = D // NF
KB = NK * H // NF
FB = FF // NF
EPS = 1e-05
ROPE_BASE = 10000.0
SCALE = H ** (-0.5)
NEG = -1e30
BLK = 256
VMEM_LIMIT = 63 * 2**20
ROWS = D // 4
LANES = FF // 4
OW = QB - 8
BF = jnp.bfloat16
F32 = jnp.float32


def dot(a, b, ca, cb):
    return lax.dot_general(a, b, (((ca,), (cb,)), ((), ())), preferred_element_type=F32)


def rope_tables():
    inverse = ROPE_BASE ** (-(2.0 * np.arange(HALF, dtype=np.float64)) / H)
    angles = inverse[:, None] * np.arange(T, dtype=np.float64)[None, :]
    return np.cos(angles).astype(np.float32), np.sin(angles).astype(np.float32)


def parts_of(row):
    hi = row.astype(BF).astype(F32)
    rest = row - hi
    mid = rest.astype(BF).astype(F32)
    return [hi, mid, rest - mid]


def lane_tiles():
    return [slice(128 * i, 128 * i + 128) for i in range(T // 128)]


class Work:
    def __init__(self, order, refs):
        self.order = order
        self.__dict__.update(refs)

    def start(self):
        count = self.length[0]
        place = lax.broadcasted_iota(jnp.int32, (8, T), 1)
        valid = (place < count).astype(F32)
        self.valid[...] = valid
        for ts in lane_tiles():
            self.S[0, :, ts] = self.x[:, ts].astype(F32)
            self.G[:, ts] = jnp.where(valid[0:1, ts] > 0.0, self.ct[:, ts].astype(F32), 0.0)
        self.gainA[...] = jnp.broadcast_to(self.ga[...].reshape(1, D), (128, D)).T
        self.gainM[...] = jnp.broadcast_to(self.gm[...].reshape(1, D), (128, D)).T
        row = lax.broadcasted_iota(jnp.int32, (H, 1024), 0)
        lane = lax.broadcasted_iota(jnp.int32, (H, 1024), 1)
        self.pick[...] = jnp.where(lane == 128 * (row // 8) + 120 + lax.rem(row, 8), 1.0, 0.0).astype(BF)
        self.gacc[...] = jnp.zeros_like(self.gacc)
        def blank(h, carry):
            self.QA[0, h, H:, :] = jnp.zeros((H, T), BF)
            self.QA[1, h, H:, :] = jnp.zeros((H, T), BF)
            self.DOA[h, H:, :] = jnp.zeros((H, T), BF)
            return carry

        lax.fori_loop(0, NQ, blank, 0)

        def clear(i, carry):
            rows = pl.ds(pl.multiple_of(i * 64, 64), 64)
            self.DA[rows, :] = jnp.zeros((64, 1024), BF)
            self.DO[rows, :] = jnp.zeros((64, D), BF)
            self.DD[rows, :] = jnp.zeros((64, FF), BF)
            for k in range(3):
                self.DG[k, rows, :] = jnp.zeros((64, 1024), BF)
            return carry

        lax.fori_loop(0, D // 64, clear, 0)

    def norm(self, src, r, gain, dst, rho_ref, row):
        total = jnp.zeros((8, T), F32)
        for i in range(0, D, 8):
            v = src[r, i : i + 8, :]
            total = total + v * v
        total = jnp.sum(total, axis=0, keepdims=True)
        if row is not None:
            self.stat[r, row : row + 1, :] = total
        rho = lax.rsqrt(total * (1.0 / D) + EPS)
        rho_ref[r, 0:1, :] = rho
        for i in range(0, D, 64):
            rows = slice(i, i + 64)
            wide = jnp.concatenate([gain[rows, :]] * 4, axis=1)
            dst[r, rows, :] = (src[r, rows, :] * rho * wide).astype(BF)

    def natural_rows(self, ref, base, width, first, count):
        pieces = []
        row = first
        while row < first + count:
            f, i = row // width, row % width
            n = min(width - i, first + count - row)
            at = 128 * self.order.index(f) + base + i
            pieces.append(ref[at : at + n, :])
            row += n
        return pieces[0] if len(pieces) == 1 else jnp.concatenate(pieces, axis=0)

    def prepare(self, r):
        self.norm(self.S, r, self.gainA, self.XA, self.rhoA, 0)

    def project(self, r):
        def part(c, carry):
            cs = pl.ds(pl.multiple_of(512 * c, 512), 512)
            self.Y[cs, :] = dot(self.WA[:, cs], self.XA[r], 0, 0)
            return carry

        for c in range(2):
            part(c, 0)
        cos, sin = self.cos[...], self.sin[...]
        one = jnp.ones((1, T), F32)
        place = lax.broadcasted_iota(jnp.int32, (1, T), 1)
        bias = jnp.where(place < self.length[0], 0.0, NEG)
        for h in range(NQ + NK):
            base, width, at = (0, QB, h) if h < NQ else (QB, KB, h - NQ)
            a = self.natural_rows(self.Y, base, width, H * at, HALF)
            b = self.natural_rows(self.Y, base, width, H * at + HALF, HALF)
            first, second = a * cos - b * sin, b * cos + a * sin
            if h < NQ:
                self.QA[r, h, 0:HALF, :] = (first * SCALE).astype(BF)
                self.QA[r, h, HALF:H, :] = (second * SCALE).astype(BF)
                self.QA[r, h, H : H + 16, :] = jnp.concatenate([one, jnp.zeros((15, T), F32)], axis=0).astype(BF)
            else:
                g = h - NQ
                key = jnp.concatenate([first, second], axis=0)
                self.KT[r, g] = key.astype(BF)
                v = jnp.concatenate(
                    [
                        self.natural_rows(self.Y, QB + KB, KB, H * g, HALF),
                        self.natural_rows(self.Y, QB + KB, KB, H * g + HALF, HALF),
                    ],
                    axis=0,
                )
                self.VT[g] = v.astype(BF)
                ones3 = jnp.ones((3, T), F32)
                tail = jnp.zeros((H - 4, T), F32)
                ktall = jnp.concatenate([key, bias, ones3, tail], axis=0)
                vtall = jnp.concatenate([v, jnp.zeros((1, T), F32), ones3, tail], axis=0)
                for ts in lane_tiles():
                    self.KTOK[r, g, ts, :] = ktall[:, ts].T.astype(BF)
                    self.VTOK[r, g, ts, :] = vtall[:, ts].T.astype(BF)

    def diagonal(self):
        key = lax.broadcasted_iota(jnp.int32, (BLK, BLK), 0)
        query = lax.broadcasted_iota(jnp.int32, (BLK, BLK), 1)
        return key <= query

    def attend(self, r, links):
        low, high = slice(0, BLK), slice(BLK, T)

        def head(h, carry):
            g = h // GROUP
            allowed = self.diagonal()
            at = pl.ds(pl.multiple_of(h * H, H), H)
            s = dot(self.KTOK[r, g, low, :], self.QA[r, h, :, low], 1, 0)
            s = jnp.where(allowed, s, NEG)
            top = jnp.max(s, axis=0, keepdims=True)
            p = jnp.exp(s - top)
            total = jnp.sum(p, axis=0, keepdims=True)
            o = dot(self.VT[g, :, low], p.astype(BF), 1, 0)
            self.AT[r, at, low] = (o * (1.0 / total)).astype(BF)
            lse0 = top + jnp.log(total)
            s0 = dot(self.KTOK[r, g, low, :], self.QA[r, h, :, high], 1, 0)
            s1 = dot(self.KTOK[r, g, high, :], self.QA[r, h, :, high], 1, 0)
            s1 = jnp.where(allowed, s1, NEG)
            top = jnp.maximum(jnp.max(s0, axis=0, keepdims=True), jnp.max(s1, axis=0, keepdims=True))
            p0 = jnp.exp(s0 - top)
            p1 = jnp.exp(s1 - top)
            total = jnp.sum(p0, axis=0, keepdims=True) + jnp.sum(p1, axis=0, keepdims=True)
            o = dot(self.VT[g, :, low], p0.astype(BF), 1, 0) + dot(self.VT[g, :, high], p1.astype(BF), 1, 0)
            self.AT[r, at, high] = (o * (1.0 / total)).astype(BF)
            lse1 = top + jnp.log(total)
            lse = jnp.concatenate([lse0, lse1], axis=1)
            rows = [jnp.ones((1, T), F32)] + parts_of(-lse) + [jnp.zeros((12, T), F32)]
            self.QA[r, h, H : H + 16, :] = jnp.concatenate(rows, axis=0).astype(BF)
            return carry

        def group(g, carry):
            [head(GROUP * g + k, 0) for k in range(GROUP)]
            links.run_if(r == 0, HEADS[g])
            return carry

        for g in range(NK):
            group(g, 0)

    def rest_of_output(self):
        self.WO[:, NF * OW :] = dot(self.WA[...], self.pick[...], 1, 1).astype(BF)

    def after(self, value, src, r, dst, to, row, squares):
        n = value.shape[0]
        dst[to, row : row + n, :] = src[r, row : row + n, :] + value
        for i in range(n // 8):
            part = value[8 * i : 8 * i + 8]
            squares = squares + part * part
        return squares

    def out_project(self, r):
        self.Y[0:D, :] = dot(self.WO[...], self.AT[r], 0, 0)
        squares = jnp.zeros((8, T), F32)
        for b in range(NF):
            f = self.order[b]
            squares = self.after(self.Y[OW * b : OW * b + OW, :], self.S, r, self.M, r, QB * f, squares)
            at = NF * OW + 8 * b
            squares = self.after(self.Y[at : at + 8, :], self.S, r, self.M, r, QB * f + OW, squares)
        self.stat[r, 1:2, :] = jnp.sum(squares, axis=0, keepdims=True)

    def mlp(self, r, links):
        self.norm(self.M, r, self.gainM, self.XM, self.rhoM, None)

        def half(y, carry):
            cs = pl.ds(pl.multiple_of(512 * y, 512), 512)

            def part(i, carry):
                to = pl.ds(pl.multiple_of(512 * i, 512), 512)
                self.Y[to, :] = dot(self.WG[i, :, cs], self.XM[r], 0, 0)
                return carry

            for i in range(3):
                part(i, 0)

            def block(z, carry):
                f = self.natural(y, z)
                for j in range(3):
                    gate_at, up_at = self.places(j)
                    gate = self.Y[pl.ds(pl.multiple_of(gate_at[0] * 512 + 128 * z + gate_at[1], 64), 64), :]
                    up = self.Y[pl.ds(pl.multiple_of(up_at[0] * 512 + 128 * z + up_at[1], 64), 64), :]
                    rows = pl.ds(pl.multiple_of(FB * f + 64 * j, 64), 64)
                    self.GATE[r, rows, :] = gate.astype(BF)
                    self.UP[r, rows, :] = up.astype(BF)
                    self.HID[r, rows, :] = (gate * jax.nn.sigmoid(gate) * up).astype(BF)
                return carry

            for z in range(4):
                block(z, 0)
            links.run_if(r == 0, MLP[y])
            return carry

        for y in range(2):
            half(y, 0)
        self.Y[0:D, :] = dot(self.WDT[...], self.HID[r], 1, 0)
        squares = jnp.zeros((8, T), F32)
        for b in range(NF):
            squares = self.after(self.Y[QB * b : QB * b + QB, :], self.M, r, self.S, r + 1, QB * self.order[b], squares)
        self.stat[r, 2:3, :] = jnp.sum(squares, axis=0, keepdims=True)

    def natural(self, y, z):
        return 2 * z + y if self.order[1] == 2 else 4 * y + z

    def places(self, j):
        return ((0, 0), (0, 64), (1, 0))[j], ((1, 64), (2, 0), (2, 64))[j]

    def write_output(self):
        valid = self.valid[0:1, :]
        for ts in lane_tiles():
            v = jnp.where(valid[:, ts] > 0.0, self.S[2, :, ts], 0.0)
            self.out[:, ts] = v.astype(BF)

    def pack_down(self):
        for k in range(NF // 2):
            rows = [self.G[QB * self.order[b] : QB * self.order[b] + QB, :] for b in (2 * k, 2 * k + 1)]
            self.GLD[2 * QB * k : 2 * QB * k + 2 * QB, :] = jnp.concatenate(rows, axis=0).astype(BF)

    def pack_out(self):
        tails = []
        for b in range(NF):
            at = QB * self.order[b]
            self.GLO[OW * b : OW * b + OW, :] = self.G[at : at + OW, :].astype(BF)
            tails.append(self.G[at + OW : at + QB, :])
        self.GLO[NF * OW : D, :] = jnp.concatenate(tails, axis=0).astype(BF)

    def add_term(self, dst, index, value):
        dst[index] = (value + dst[index].astype(F32)).astype(dst.dtype)

    def norm_back(self, src, r, rho_ref, gain, slot):
        rho = rho_ref[r, 0:1, :]
        total = jnp.zeros((8, T), F32)
        for i in range(0, D, 64):
            rows = slice(i, i + 64)
            wide = jnp.concatenate([gain[rows, :]] * 4, axis=1)
            e, v = self.E[rows, :], src[r, rows, :]
            product = e * v
            weighted = product * wide
            for k in range(0, 64, 8):
                total = total + weighted[k : k + 8]
            share = product * rho
            self.gacc[slot, rows, :] += share[:, :128] + share[:, 128:256] + share[:, 256:384] + share[:, 384:]
        mean = jnp.sum(total, axis=0, keepdims=True) * (1.0 / D)
        back = rho * rho * mean
        for i in range(0, D, 64):
            rows = slice(i, i + 64)
            wide = jnp.concatenate([gain[rows, :]] * 4, axis=1)
            self.G[rows, :] += rho * (self.E[rows, :] * wide - src[r, rows, :] * back)

    def mlp_back(self, r, links):
        self.pack_down()
        for c in range(2):
            cs = slice(768 * c, 768 * c + 768)
            self.add_term(self.DD, (slice(None), cs), dot(self.GLD[...], self.HID[r, cs, :], 1, 1))
        links.run_if(r == 0, AFTER_DOWN)

        def hidden(k, carry):
            rows = pl.ds(pl.multiple_of(2 * FB * k, 128), 2 * FB)
            self.Y[0 : 2 * FB, :] = dot(self.WDT[:, rows], self.GLD[...], 0, 0)
            for m in range(2):
                f = 2 * k + m
                b = k + 4 * m if self.order[1] == 2 else f
                for j in range(3):
                    at = pl.ds(pl.multiple_of(FB * f + 64 * j, 64), 64)
                    grad = self.Y[FB * m + 64 * j : FB * m + 64 * j + 64, :]
                    gate = self.GATE[r, at, :].astype(F32)
                    up = self.UP[r, at, :].astype(F32)
                    sig = jax.nn.sigmoid(gate)
                    silu = gate * sig
                    gate_at, up_at = self.places(j)
                    to = pl.ds(pl.multiple_of(1024 * gate_at[0] + 128 * b + gate_at[1], 64), 64)
                    self.DGU[to, :] = (grad * up * (sig + silu * (1.0 - sig))).astype(BF)
                    to = pl.ds(pl.multiple_of(1024 * up_at[0] + 128 * b + up_at[1], 64), 64)
                    self.DGU[to, :] = (grad * silu).astype(BF)
            links.run_if(r == 0, HIDDEN[k])
            return carry

        for k in range(4):
            hidden(k, 0)

        def matrix(i, carry):
            grad = self.DGU[pl.ds(pl.multiple_of(1024 * i, 1024), 1024), :]
            self.add_term(self.DG, (i,), dot(self.XM[r], grad, 1, 1))
            links.run_if(r == 0, AFTER_GATE[i])
            return carry

        for i in range(3):
            matrix(i, 0)
        self.E[...] = dot(self.WG[0], self.DGU[0:1024, :], 1, 0)

        def back(i, carry):
            grad = self.DGU[pl.ds(pl.multiple_of(1024 * i, 1024), 1024), :]
            self.E[...] = self.E[...] + dot(self.WG[i], grad, 1, 0)
            return carry

        for i in (1, 2):
            back(i, 0)
        links.run_if(r == 0, BEFORE_NORM)
        self.norm_back(self.M, r, self.rhoM, self.gainM, 1)

    def attend_back(self, r, links):
        self.pack_out()
        term = dot(self.AT[r], self.GLO[0:D, :], 1, 1)
        self.add_term(self.DO, (slice(None), slice(0, NF * OW)), term[:, : NF * OW])
        self.DO[:, NF * OW :] = term[:, NF * OW :].astype(BF)
        links.run_if(r == 0, AFTER_OUT)
        self.E[...] = dot(self.WO[...], self.GLO[0:D, :], 1, 0)
        links.run_if(r == 0, BEFORE_HEADS)
        for h in range(NQ):
            rows = slice(H * h, H * h + H)
            do = self.E[rows, :].astype(BF)
            self.DOA[h, 0:H, :] = do
            delta = jnp.sum(do.astype(F32) * self.AT[r, rows, :].astype(F32), axis=0, keepdims=True)
            rows = [jnp.zeros((1, T), F32)] + parts_of(-delta) + [jnp.zeros((12, T), F32)]
            self.DOA[h, H : H + 16, :] = jnp.concatenate(rows, axis=0).astype(BF)
        low, high = slice(0, BLK), slice(BLK, T)
        self.Y[D : D + 2 * NK * H, :] = jnp.zeros((2 * NK * H, T), F32)

        def head(h, carry):
            g = h // GROUP
            allowed = self.diagonal()
            at = pl.ds(pl.multiple_of(h * H, H), H)
            kat = pl.ds(pl.multiple_of(D + g * H, H), H)
            vat = pl.ds(pl.multiple_of(D + NK * H + g * H, H), H)
            q, do = self.QA[r, h], self.DOA[h]
            k0, k1 = self.KTOK[r, g, low, :], self.KTOK[r, g, high, :]
            v0, v1 = self.VTOK[r, g, low, :], self.VTOK[r, g, high, :]
            t0, t1 = self.KT[r, g, :, low], self.KT[r, g, :, high]

            p = jnp.where(allowed, jnp.exp(dot(k0, q[:, low], 1, 0)), 0.0)
            ds = (p * dot(v0, do[:, low], 1, 0)).astype(BF)
            p = p.astype(BF)
            self.Y[at, low] = dot(t0, ds, 1, 0) * SCALE
            dk0 = dot(q[0:H, low], ds, 1, 1)
            dv0 = dot(do[0:H, low], p, 1, 1)

            p = jnp.exp(dot(k0, q[:, high], 1, 0))
            ds = (p * dot(v0, do[:, high], 1, 0)).astype(BF)
            p = p.astype(BF)
            dq = dot(t0, ds, 1, 0)
            dk0 += dot(q[0:H, high], ds, 1, 1)
            dv0 += dot(do[0:H, high], p, 1, 1)

            p = jnp.where(allowed, jnp.exp(dot(k1, q[:, high], 1, 0)), 0.0)
            ds = (p * dot(v1, do[:, high], 1, 0)).astype(BF)
            p = p.astype(BF)
            self.Y[at, high] = (dq + dot(t1, ds, 1, 0)) * SCALE
            self.Y[kat, low] += dk0
            self.Y[vat, low] += dv0
            self.Y[kat, high] += dot(q[0:H, high], ds, 1, 1)
            self.Y[vat, high] += dot(do[0:H, high], p, 1, 1)
            return carry

        def group(g, carry):
            [head(GROUP * g + k, 0) for k in range(GROUP)]
            links.run_if(r == 0, BACK_HEADS[g])
            return carry

        for g in range(NK):
            group(g, 0)

    def project_back(self, r, links):
        cos, sin = self.cos[...], self.sin[...]
        for h in range(NQ + NK):
            first, second = slice(H * h, H * h + HALF), slice(H * h + HALF, H * h + H)
            a, b = self.Y[first, :], self.Y[second, :]
            self.Y[first, :] = a * cos + b * sin
            self.Y[second, :] = b * cos - a * sin
        for b in range(NF):
            f = self.order[b]
            rows = jnp.concatenate(
                [
                    self.Y[QB * f : QB * f + QB, :],
                    self.Y[D + KB * f : D + KB * f + KB, :],
                    self.Y[D + NK * H + KB * f : D + NK * H + KB * f + KB, :],
                    jnp.zeros((128 - QB - 2 * KB, T), F32),
                ],
                axis=0,
            )
            self.GLO[128 * b : 128 * b + 128, :] = rows.astype(BF)
        def part(c, carry):
            cs = pl.ds(pl.multiple_of(512 * c, 512), 512)
            term = dot(self.XA[r], self.GLO[cs, :], 1, 1) + dot(self.DO[:, NF * OW :], self.pick[:, cs], 1, 0)
            self.add_term(self.DA, (slice(None), cs), term)
            return carry

        for c in range(2):
            part(c, 0)
        links.run_if(r == 0, AFTER_QKV)
        self.E[...] = dot(self.WA[...], self.GLO[...], 1, 0)
        self.norm_back(self.S, r, self.rhoA, self.gainA, 0)

    def write_grad(self):
        for ts in lane_tiles():
            self.gin[:, ts] = self.G[:, ts]

    def small(self):
        valid = self.valid[0:1, :]
        rows = [jnp.sum(self.gacc[i].T, axis=0, keepdims=True) for i in range(2)]
        sums = jnp.sum(jnp.where(valid > 0.0, jnp.concatenate([self.stat[0, 0:3], self.stat[1, 0:3]], axis=0), 0.0), axis=1, keepdims=True)
        count = jnp.sum(valid, axis=1, keepdims=True)
        lane = lax.broadcasted_iota(jnp.int32, (6, D), 1)
        return jnp.concatenate(rows + [jnp.where(lane < 128, sums, count)], axis=0)


SCRATCH = dict(
    S=((3, D, T), F32), G=((D, T), F32), E=((D, T), F32), Y=((1536, T), F32),
    XA=((2, D, T), BF), XM=((2, D, T), BF), rhoA=((2, 8, T), F32), rhoM=((2, 8, T), F32),
    QA=((2, NQ, 128, T), BF), KT=((2, NK, H, T), BF), VT=((NK, H, T), BF),
    KTOK=((2, NK, T, 128), BF), VTOK=((2, NK, T, 128), BF), AT=((2, D, T), BF), M=((2, D, T), F32),
    GATE=((2, FF, T), BF), UP=((2, FF, T), BF), HID=((2, FF, T), BF),
    GLD=((D, T), BF), GLO=((1024, T), BF), DGU=((2 * FF, T), BF), DOA=((NQ, 128, T), BF),
    stat=((2, 8, T), F32), valid=((8, T), F32), gacc=((2, D, 128), F32), gainA=((D, 128), F32), gainM=((D, 128), F32), pick=((H, 1024), BF),
)
WEIGHTS = dict(WA=((D, 1024), BF), WO=((D, D), BF), WG=((3, D, 1024), BF), WDT=((D, FF), BF))
GRADS = dict(DA=((D, 1024), BF), DO=((D, D), BF), DG=((3, D, 1024), BF), DD=((D, FF), BF))

class Alone:
    def run_if(self, condition, steps):
        pass


def applications(w, links):
    def forward(r, carry):
        w.prepare(r)
        links.run_if(r == 0, BEFORE_PROJECT)
        w.project(r)
        links.run_if(r == 0, AFTER_PROJECT)
        w.attend(r, links)
        pl.when(r == 0)(w.rest_of_output)
        links.run_if(r == 0, BEFORE_OUT)
        w.out_project(r)
        links.run_if(r == 0, BEFORE_MLP)
        w.mlp(r, links)
        return carry

    def backward(i, carry):
        w.mlp_back(1 - i, links)
        w.attend_back(1 - i, links)
        w.project_back(1 - i, links)
        return carry

    lax.fori_loop(0, 2, forward, 0)
    w.write_output()
    lax.fori_loop(0, 2, backward, 0)


def compute_kernel(order, names, *refs):
    w = Work(order, dict(zip(names, refs)))
    w.start()
    applications(w, Alone())
    w.write_grad()
    w.tiny[...] = w.small()


def local_compute(order, x, length, ga, gm, ct, packed):
    cos, sin = rope_tables()
    ins = dict(length=length, x=x, ct=ct, ga=ga, gm=gm, cos=jnp.asarray(cos), sin=jnp.asarray(sin), **packed)
    outs = dict(out=((D, T), BF), gin=((D, T), F32), tiny=((8, D), F32), **GRADS)
    names = list(ins) + list(outs) + list(SCRATCH)
    vmem = pl.BlockSpec(memory_space=pltpu.VMEM)
    results = pl.pallas_call(
        functools.partial(compute_kernel, order, names),
        out_shape=[jax.ShapeDtypeStruct(*s) for s in outs.values()],
        in_specs=[pl.BlockSpec(memory_space=pltpu.SMEM)] + [vmem] * (len(ins) - 1),
        out_specs=[vmem] * len(outs),
        scratch_shapes=[pltpu.VMEM(*s) for s in SCRATCH.values()],
        compiler_params=pltpu.CompilerParams(vmem_limit_bytes=VMEM_LIMIT),
    )(*ins.values())
    return dict(zip(outs, results))


def pack(order, q, k, v, o, g, u, d):
    def cols(w, width):
        return w.reshape(w.shape[0], NF, width)[:, np.array(order)]
    ob = cols(o, QB)
    wa = jnp.concatenate([cols(q, QB), cols(k, KB), cols(v, KB), ob[:, :, OW:]], axis=2).reshape(D, 1024)
    wo = jnp.concatenate([ob[:, :, :OW].reshape(D, NF * OW), ob[:, :, OW:].reshape(D, D - NF * OW)], axis=1)
    wg = jnp.concatenate([cols(g, FB), cols(u, FB)], axis=2).reshape(D, NF, 3, 128)
    wg = wg.transpose(2, 0, 1, 3).reshape(3, D, 1024)
    wd = d.T.reshape(NF, QB, FF)[np.array(order)].reshape(D, FF)
    return dict(WA=wa, WO=wo, WG=wg, WDT=wd)


def unpack(order, r):
    back = np.argsort(np.array(order))
    a = r["DA"].astype(F32).reshape(D, NF, 128)[:, back]
    o = r["DO"][:, : NF * OW].astype(F32).reshape(D, NF, OW)[:, back]
    o = jnp.concatenate([o, a[:, :, 120:]], axis=2).reshape(D, D)
    g = r["DG"].astype(F32).reshape(3, D, NF, 128).transpose(1, 2, 0, 3).reshape(D, NF, 2 * FB)[:, back]
    d = r["DD"].astype(F32).reshape(NF, QB, FF)[back].reshape(D, FF).T
    return (
        a[:, :, :QB].reshape(D, D), a[:, :, QB : QB + KB].reshape(D, NK * H), a[:, :, QB + KB : 120].reshape(D, NK * H),
        o, g[:, :, :FB].reshape(D, FF), g[:, :, FB:].reshape(D, FF), d,
    )


PIECES = ("A0", "A1", "O", "G0", "G1", "G2", "D0", "D1")
CUT = dict(A0=(0, 80), A1=(80, ROWS - 80), D0=(0, 256), D1=(256, 128))
MESH = pl.DeviceIdType.MESH


def region(refs, piece, dp, y, z=0, count=4):
    ref, line = refs[piece[0]], 4 * y + z
    if piece[0] == "D":
        first, size = CUT[piece]
        rows = pl.ds(pl.multiple_of(QB * line, 16), QB * count)
        return ref.at[rows, pl.ds(pl.multiple_of(LANES * dp + first, 128), size)]
    width = OW if piece == "O" else 128
    first, size = CUT.get(piece, (0, ROWS))
    rows = pl.ds(pl.multiple_of(ROWS * dp + first, 16), size)
    lanes = pl.ds(pl.multiple_of(width * line, 128), width * count)
    return ref.at[int(piece[1]), rows, lanes] if piece[0] == "G" else ref.at[rows, lanes]


def shape_of(piece, count):
    if piece[0] == "D":
        return (QB * count, CUT[piece][1])
    return (CUT.get(piece, (0, ROWS))[1], (OW if piece == "O" else 128) * count)


def slip_shape(piece):
    return (QB + 8, CUT[piece][1]) if piece[0] == "D" else (CUT.get(piece, (0, ROWS))[1], 128)


def cut(piece, line, z):
    if piece == "O":
        return jnp.concatenate([line[:, OW * z : OW * z + OW]] * 2, axis=1)
    return jnp.concatenate([line[QB * z : QB * z + QB], jnp.zeros((8, line.shape[1]), F32)], axis=0)


def when(condition, action):
    if condition is None:
        action()
    else:
        pl.when(condition)(action)


class Links:
    def __init__(self, refs):
        self.__dict__.update(refs)
        self.weights = dict(A=refs["WA"], O=refs["WO"], G=refs["WG"], D=refs["WDT"])
        self.grads = dict(A=refs["DA"], O=refs["DO"], G=refs["DG"], D=refs["DD"])
        self.dp, f = lax.axis_index("dp"), lax.axis_index("fsdp")
        self.x, self.c = self.dp // 2, lax.rem(self.dp, 2)
        self.z, self.y = f // 2, lax.rem(f, 2)
        self.ny = 1 - self.y
        places = [(1 - self.x, self.ny), (self.x, self.ny), (1 - self.x, self.y), (self.x, self.y)]
        self.mine = [(2 * x + self.c, y) for x, y in places]
        self.theirs = [(2 * x + 1 - self.c, y) for x, y in places]
        self.far = 2 * (1 - self.x) + self.c
        self.other = 2 * self.x + 1 - self.c
        self.sib = (self.other, f)
        self.xn = (self.far, f)
        self.yn = (self.dp, 2 * self.z + 1 - self.y)
        self.peer = [None] + [lax.rem(self.z + k, 4) for k in (1, 2, 3)]
        self.zn = [None] + [(self.dp, 2 * self.peer[k] + self.y) for k in (1, 2, 3)]
        self.side = [None, (self.dp, 2 * (self.z + 1) + self.y), (self.dp, 2 * (self.z - 1) + self.y)]
        self.here = {(sign, t): (self.z + sign * t >= 0) & (self.z + sign * t < 4) for sign in (1, -1) for t in (1, 2, 3)}
        self.on = {(-1, 0): self.z < 3, (1, 0): self.z > 0}
        for sign, t in self.here:
            self.on[sign, t] = self.here[sign, t] & self.on[sign, 0]
        self.copies = {}
        self.used = 0

    def greet(self):
        for device in [self.sib, self.xn, self.yn] + self.zn[1:]:
            pl.semaphore_signal(pltpu.get_barrier_semaphore(), inc=1, device_id=device, device_id_type=MESH)

    def met(self):
        pl.semaphore_wait(pltpu.get_barrier_semaphore(), 6)

    def send(self, name, src, dst, device, condition=None):
        index = self.used
        self.used += 1

        def copy():
            return pltpu.make_async_remote_copy(
                src_ref=src(),
                dst_ref=dst(),
                send_sem=self.sent.at[index],
                recv_sem=self.came.at[index],
                device_id=device,
                device_id_type=MESH,
            )

        when(condition, lambda: copy().start())
        self.copies[name] = (copy, condition)

    def arrived(self, *names, condition=None):
        for name in names:
            when(condition, lambda name=name: self.copies[name][0]().wait_recv())

    def finish(self):
        for copy, condition in self.copies.values():
            when(condition, lambda copy=copy: copy().wait_send())

    def run_if(self, condition, steps):
        if steps:
            pl.when(condition)(functools.partial(self.run, *steps))

    def run(self, *steps):
        for step in steps:
            kind, piece = step.split()
            getattr(self, kind)(piece)


    def spread(self, tag, p, device, dp=None, y=None, z=0, count=4):
        block = lambda: region(self.weights, p, self.dp if dp is None else dp, self.y if y is None else y, z, count)
        self.send(("w", p, tag), block, block, device)

    def block(self, p, z):
        if p[0] in "OD":
            return getattr(self, "slip" + p).at[z]
        return region(self.weights, p, self.dp, self.y, z, 1)

    def hop(self, p, t):
        for tag, sign in (("r", -1), ("l", 1)):
            here = self.here.get((sign, t))
            if t > 0:
                self.arrived(("w", p, tag, t - 1), condition=here)
            block = lambda sign=sign: self.block(p, self.z + sign * t)
            if t < 3:
                self.send(("w", p, tag, t), block, block, self.side[-sign], self.on[sign, t])
            if p[0] in "AG" and t > 0:
                self.send(("w", p, "x", tag, t), block, block, self.xn, here)
                self.send(("w", p, "y", tag, t), block, block, self.yn, here)

    def own(self, p):
        for axis, device in (("x", self.xn), ("y", self.yn)):
            block = lambda: self.block(p, self.z)
            self.send(("w", p, axis, "r", 0), block, block, device)

    def share(self, p):
        self.hop(p, 0)

    def one(self, p):
        self.hop(p, 1)

    def two(self, p):
        self.hop(p, 2)

    def line(self, p):
        self.hop(p, 3)
        if p[0] in "OD":
            slips = [getattr(self, "slip" + p)[z].astype(F32) for z in range(4)]
            if p == "O":
                whole = jnp.concatenate([slip[:, :OW] for slip in slips], axis=1)
            else:
                whole = jnp.concatenate([slip[:QB] for slip in slips], axis=0)
            region(self.weights, p, self.dp, self.y)[...] = whole.astype(BF)
            self.spread("x", p, self.xn)
            self.spread("y", p, self.yn)
        self.spread("s", p, self.sib)

    def across(self, p, axis):
        if p[0] in "OD":
            self.arrived(("w", p, axis))
            return
        for t in range(4):
            for tag, sign in (("r", -1), ("l", 1)):
                if t > 0 or sign < 0:
                    self.arrived(("w", p, axis, tag, t), condition=self.here.get((sign, t)))

    def cross(self, p):
        self.across(p, "x")
        self.spread("xy", p, self.yn, dp=self.far, count=2)
        self.spread("sx", p, self.sib, dp=self.far)
        self.across(p, "y")
        self.spread("yx", p, self.xn, y=self.ny, z=2, count=2)
        self.spread("sy", p, self.sib, y=self.ny)

    def rest(self, p):
        self.arrived(("w", p, "xy"))
        self.spread("sxy", p, self.sib, dp=self.far, y=self.ny, count=2)
        self.arrived(("w", p, "yx"))
        self.spread("syx", p, self.sib, dp=self.far, y=self.ny, z=2, count=2)

    def end(self, p):
        self.arrived(*[("w", p, tag) for tag in ("s", "sx", "sy", "sxy", "syx")])


    def term(self, p, dp, y, z=0, count=4):
        return region(self.grads, p, dp, y, z, count)

    def add(self, p, dp, y, z, count, came):
        at = self.term(p, dp, y, z, count)
        at[...] = at[...] + came[...]

    def sibs(self, p):
        for i in range(4):
            src = lambda i=i: self.term(p, *self.theirs[i])
            self.send(("g", p, "s", i), src, lambda i=i: getattr(self, "one" + p).at[i], self.sib)

    def pair(self, p):
        for i in range(4):
            self.arrived(("g", p, "s", i))
            self.add(p, *self.mine[i], 0, 4, getattr(self, "one" + p).at[i])
            if i < 2:
                src = lambda i=i: self.term(p, *self.mine[i], 0, 2)
                self.send(("g", p, "y", i), src, lambda i=i: getattr(self, "twoy" + p).at[i], self.yn)
            if i in (0, 2):
                src = lambda i=i: self.term(p, *self.mine[i], 2, 2)
                self.send(("g", p, "x", i // 2), src, lambda i=i: getattr(self, "twox" + p).at[i // 2], self.xn)

    def twos(self, p):
        self.arrived(("g", p, "y", 0))
        self.add(p, self.far, self.y, 0, 2, getattr(self, "twoy" + p).at[0])
        src = lambda: self.term(p, self.far, self.y, 0, 2)
        self.send(("g", p, "yx"), src, lambda: getattr(self, "threex" + p), self.xn)
        self.arrived(("g", p, "x", 0))
        self.add(p, self.dp, self.ny, 2, 2, getattr(self, "twox" + p).at[0])
        src = lambda: self.term(p, self.dp, self.ny, 2, 2)
        self.send(("g", p, "xy"), src, lambda: getattr(self, "threey" + p), self.yn)

    def fours(self, p):
        self.arrived(("g", p, "y", 1), ("g", p, "x", 1), ("g", p, "yx"), ("g", p, "xy"))
        for z, two, three in ((0, "twoy", "threex"), (2, "twox", "threey")):
            at = self.term(p, self.dp, self.y, z, 2)
            at[...] = at[...] + getattr(self, two + p)[1] + getattr(self, three + p)[...]
        if p[0] in "OD":
            line = self.term(p, self.dp, self.y)[...].astype(F32)
            for z in range(4):
                getattr(self, "part" + p)[z] = cut(p, line, z).astype(BF)
        for k in (1, 3, 2):
            if p[0] in "OD":
                src = lambda k=k: getattr(self, "part" + p).at[self.peer[k]]
            else:
                src = lambda k=k: self.term(p, self.dp, self.y, self.peer[k], 1)
            self.send(("g", p, "z", k), src, lambda k=k: getattr(self, "four" + p).at[k - 1], self.zn[k])

    def total(self, p):
        own = getattr(self, "part" + p)[self.z] if p[0] in "OD" else self.term(p, self.dp, self.y, self.z, 1)[...]
        total = own.astype(F32)
        for k in (1, 2, 3):
            self.arrived(("g", p, "z", k))
            total = total + getattr(self, "four" + p)[k - 1].astype(F32)
        if p[0] == "D":
            first, size = CUT[p]
            self.sumD[:, first : first + size] = total[:QB, :]
        else:
            at = 128 * ("A", "O", "G0", "G1", "G2").index("A" if p[0] == "A" else p)
            first, size = CUT.get(p, (0, ROWS))
            self.sumN[first : first + size, at : at + 128] = total


    def tiny(self, step):
        step = int(step)
        if step > 0:
            self.arrived(("t", step - 1))
            self.tinies[step] = self.tinies[step - 1] + self.tinyin[step - 1]
        if step < 3:
            device = (self.sib, self.xn, self.yn)[step]
            self.send(("t", step), lambda: self.tinies.at[step], lambda: self.tinyin.at[step], device)
        else:
            for k in (1, 2, 3):
                self.send(("t", step, k), lambda: self.tinies.at[3], lambda k=k: self.tinyz.at[k], self.zn[k])

    def tiny_end(self):
        self.tinyz[0] = self.tinies[3]
        for k in (1, 2, 3):
            self.arrived(("t", 3, k))
        total = None
        for z in range(4):
            term = self.tinyz[lax.rem(self.z - z + 4, 4)]
            total = term if total is None else total + term
        self.sumT[...] = total


def rooms():
    shapes = {}
    for p in PIECES:
        shapes["one" + p] = ((4,) + shape_of(p, 4), BF)
        for room in ("twoy", "twox"):
            shapes[room + p] = ((2,) + shape_of(p, 2), BF)
        for room in ("threex", "threey"):
            shapes[room + p] = (shape_of(p, 2), BF)
        shapes["four" + p] = ((3,) + slip_shape(p), BF)
        if p[0] in "OD":
            shapes["slip" + p] = ((4,) + slip_shape(p), BF)
            shapes["part" + p] = ((4,) + slip_shape(p), BF)
    shapes["tinies"] = ((4, 8, D), F32)
    shapes["tinyin"] = ((3, 8, D), F32)
    shapes["tinyz"] = ((4, 8, D), F32)
    return shapes


COPIES = len(PIECES) * (6 + 14 + 7 + 13) + 6


def pack_own(links, refs):
    rows = lambda *names: [refs[n][...].astype(F32) for n in names]
    q, k, v, o, g, u, d = rows("q", "k", "v", "o", "g", "u", "d")
    gu = jnp.concatenate([g, u], axis=1)
    a = jnp.concatenate([q, k.T, v.T, o[:, OW:]], axis=1)
    whole = dict(A0=a[:80], A1=a[80:], G0=gu[:, :128], G1=gu[:, 128:256], G2=gu[:, 256:])
    for p in PIECES:
        if p == "O":
            links.slipO[links.z] = cut(p, o, 0).astype(BF)
        elif p[0] == "D":
            first, size = CUT[p]
            getattr(links, "slip" + p)[links.z] = cut(p, d[:, first : first + size], 0).astype(BF)
        else:
            region(links.weights, p, links.dp, links.y, links.z, 1)[...] = whole[p].astype(BF)


BEGIN = ("own A1", "share A1", "own A0", "share A0", "own G1", "own G2", "own G0", "share G0")
BEFORE_PROJECT = ("share G2", "one A1", "one A0", "share G1", "one G0", "one G2", "two A1", "two A0", "share O", "two G0", "two G2", "line A1", "line A0", "one G1", "share D1", "line G0", "one O", "line G2", "cross A1", "share D0", "two G1", "one D1", "cross A0", "two O", "cross G0", "line G1", "two D1", "one D0", "rest A0", "cross G2", "line O", "end A0", "rest A1", "two D0", "cross G1", "end A1")
AFTER_PROJECT = ("line D1", "cross O", "line D0")
HEADS = ((), ("rest G0", "rest G1", "rest G2", "rest O"), ("cross D1", "end O", "end G0"))
BEFORE_OUT = ()
BEFORE_MLP = ("end G1", "end G2", "cross D0")
MLP = (("rest D1",), ("rest D0", "end D0", "end D1"))
AFTER_DOWN = ("sibs D1", "sibs D0")
HIDDEN = (("pair D1",), (), ("pair D0",), ())
AFTER_GATE = (("sibs G0",), ("sibs G1", "twos D1"), ("sibs G2", "pair G0"))
BEFORE_NORM = ("twos D0", "pair G1")
AFTER_OUT = ("sibs O", "fours D1")
BEFORE_HEADS = ("twos G0",)
BACK_HEADS = (("pair G2", "pair O", "fours D0"), ("twos G1", "fours G0"), ("twos G2", "twos O"))
AFTER_QKV = ("sibs A0", "sibs A1", "fours G1", "pair A0", "pair A1")
LAST = ("tiny 0", "fours G2", "fours O", "tiny 1", "twos A0", "tiny 2", "twos A1", "total D1", "total D0", "total G0")
VERY_LAST = ("fours A0", "tiny 3", "total G1", "fours A1", "total G2", "total O", "total A0", "total A1")

def whole_kernel(order, names, *args):
    refs = dict(zip(names, args))
    w, links = Work(order, refs), Links(refs)
    links.greet()
    pack_own(links, refs)
    links.met()
    links.run(*BEGIN)
    w.start()
    applications(w, links)
    links.tinies[0] = w.small()
    links.run(*LAST)
    w.write_grad()
    links.run(*VERY_LAST)
    links.tiny_end()
    links.finish()


def finish_kernel(*refs):
    out, gin, sums, sumd, tiny, oout, ogin, ga, q, k, v, o, gm, g, u, d, rms = refs
    oout[...] = out[...]
    ogin[...] = gin[...]
    q[...] = sums[:, :QB]
    k[...] = sums[:, QB : QB + KB].T
    v[...] = sums[:, QB + KB : 120].T
    o[...] = jnp.concatenate([sums[:, 128 : 128 + OW], sums[:, 120:128]], axis=1)
    g[...] = sums[:, 256 : 256 + FB]
    u[...] = sums[:, 256 + FB : 256 + 2 * FB]
    d[...] = sumd[...]
    ga[...] = tiny[0:1, :].reshape(D)
    gm[...] = tiny[1:2, :].reshape(D)
    lane = lax.broadcasted_iota(jnp.int32, (1, 3), 1)
    for r in range(2):
        first, second, third = [tiny[2 + 3 * r + i : 3 + 3 * r + i, 0:3] for i in range(3)]
        squares = jnp.where(lane == 0, first, jnp.where(lane == 1, second, third))
        rms[r : r + 1, :] = jnp.sqrt(squares / (tiny[2:3, 128:131] * D))


def whole(x, length, ga, q, k, v, o, gm, g, u, d, ct):
    order = [2 * (b % 4) + b // 4 for b in range(NF)]
    cos, sin = rope_tables()
    ins = dict(
        length=length, x=x[0].T, ct=ct[0].T, ga=ga, gm=gm, cos=jnp.asarray(cos), sin=jnp.asarray(sin),
        q=q, k=k.T, v=v.T, o=o, g=g, u=u, d=d.T,
    )
    outs = dict(
        out=((D, T), BF), gin=((D, T), F32), sumN=((ROWS, 256 + 2 * FB), F32), sumD=((QB, LANES), F32), sumT=((8, D), F32)
    )
    scratch = dict(SCRATCH, **WEIGHTS, **GRADS, **rooms())
    names = list(ins) + list(outs) + list(scratch) + ["sent", "came"]
    vmem = pl.BlockSpec(memory_space=pltpu.VMEM)
    r = pl.pallas_call(
        functools.partial(whole_kernel, order, names),
        out_shape=[jax.ShapeDtypeStruct(*s) for s in outs.values()],
        in_specs=[pl.BlockSpec(memory_space=pltpu.SMEM)] + [vmem] * (len(ins) - 1),
        out_specs=[vmem] * len(outs),
        scratch_shapes=[pltpu.VMEM(*s) for s in scratch.values()]
        + [pltpu.SemaphoreType.DMA((COPIES,)), pltpu.SemaphoreType.DMA((COPIES,))],
        compiler_params=pltpu.CompilerParams(
            vmem_limit_bytes=VMEM_LIMIT, collective_id=0, has_side_effects=True
        ),
    )(*ins.values())
    rows = [
        ((D, T), BF), ((D, T), F32), ((D,), F32), (q.shape, F32), (k.shape[::-1], F32), (v.shape[::-1], F32),
        (o.shape, F32), ((D,), F32), (g.shape, F32), (u.shape, F32), (d.shape[::-1], F32), ((2, 3), F32),
    ]
    out, gin, ga, q, k, v, o, gm, g, u, d, rms = pl.pallas_call(
        finish_kernel,
        out_shape=[jax.ShapeDtypeStruct(*s) for s in rows],
        in_specs=[vmem] * len(outs),
        out_specs=[vmem] * len(rows),
    )(*r)
    return out.T[None], gin.T[None], ga, q, k.T, v.T, o, gm, g, u, d.T, rms


def by_collectives(x, length, ga, q, k, v, o, gm, g, u, d, ct):
    order = list(range(NF))
    full = [lax.all_gather(lax.all_gather(w, "fsdp", axis=1, tiled=True), "dp", axis=0, tiled=True) for w in (q, k, v, o, g, u, d)]
    packed = pack(order, *full)
    results = [local_compute(order, x[i].T, length[i : i + 1], ga, gm, ct[i].T, packed) for i in range(x.shape[0])]
    out = jnp.stack([r["out"].T for r in results])
    gin = jnp.stack([r["gin"].T for r in results])
    tiny = lax.psum(sum(r["tiny"] for r in results), ("dp", "fsdp"))
    terms = [unpack(order, r) for r in results]
    grads = [
        lax.psum_scatter(
            lax.psum_scatter(sum(t), "dp", scatter_dimension=0, tiled=True), "fsdp", scatter_dimension=1, tiled=True
        )
        for t in zip(*terms)
    ]
    rms = jnp.sqrt(tiny[2:8, 0].reshape(2, 3) / (tiny[2, 128] * D))
    gq, gk, gv, go, gg, gu, gd = grads
    return out, gin, tiny[0], gq, gk, gv, go, tiny[1], gg, gu, gd, rms


def solution(mesh):
    blocks = P("dp", "fsdp")
    slots = P(("dp", "fsdp"), None, None)
    in_specs = (slots, P(("dp", "fsdp")), P(), blocks, blocks, blocks, blocks, P(), blocks, blocks, blocks, slots)
    out_specs = (slots, slots, P(), blocks, blocks, blocks, blocks, P(), blocks, blocks, blocks, P())

    def on_device(*args):
        fits = mesh.shape["dp"] == 4 and mesh.shape["fsdp"] == 8 and args[0].shape[0] == 1
        return (whole if fits else by_collectives)(*args)

    return jax.shard_map(on_device, mesh=mesh, in_specs=in_specs, out_specs=out_specs, check_vma=False)
```

```python
import functools
import jax
import jax.numpy as jnp
import numpy as np
from jax import lax
from jax.experimental import pallas as pl
from jax.experimental.pallas import tpu as pltpu
from jax.sharding import PartitionSpec as P

D = 576
NQ = 9
NK = 3
GROUP = NQ // NK
H = 64
HALF = H // 2
FF = 1536
T = 512
NF = 8
QB = D // NF
KB = NK * H // NF
FB = FF // NF
EPS = 1e-05
ROPE_BASE = 10000.0
SCALE = H ** (-0.5)
NEG = -1e30
BLK = 256
VMEM_LIMIT = 63 * 2**20
ROWS = D // 4
LANES = FF // 4
OW = QB - 8
BF = jnp.bfloat16
F32 = jnp.float32


def dot(a, b, ca, cb):
    return lax.dot_general(a, b, (((ca,), (cb,)), ((), ())), preferred_element_type=F32)


def rope_tables():
    inverse = ROPE_BASE ** (-(2.0 * np.arange(HALF, dtype=np.float64)) / H)
    angles = inverse[:, None] * np.arange(T, dtype=np.float64)[None, :]
    return np.cos(angles).astype(np.float32), np.sin(angles).astype(np.float32)


def parts_of(row):
    hi = row.astype(BF).astype(F32)
    rest = row - hi
    mid = rest.astype(BF).astype(F32)
    return [hi, mid, rest - mid]


def lane_tiles():
    return [slice(128 * i, 128 * i + 128) for i in range(T // 128)]


class Work:
    def __init__(self, order, refs):
        self.order = order
        self.__dict__.update(refs)

    def start(self):
        count = self.length[0]
        place = lax.broadcasted_iota(jnp.int32, (8, T), 1)
        valid = (place < count).astype(F32)
        self.valid[...] = valid
        for ts in lane_tiles():
            self.S[0, :, ts] = self.x[:, ts].astype(F32)
            self.G[:, ts] = jnp.where(valid[0:1, ts] > 0.0, self.ct[:, ts].astype(F32), 0.0)
        self.gainA[...] = jnp.broadcast_to(self.ga[...].reshape(1, D), (128, D)).T
        self.gainM[...] = jnp.broadcast_to(self.gm[...].reshape(1, D), (128, D)).T
        row = lax.broadcasted_iota(jnp.int32, (H, 1024), 0)
        lane = lax.broadcasted_iota(jnp.int32, (H, 1024), 1)
        self.pick[...] = jnp.where(lane == 128 * (row // 8) + 120 + lax.rem(row, 8), 1.0, 0.0).astype(BF)
        self.gacc[...] = jnp.zeros_like(self.gacc)
        def blank(h, carry):
            self.QA[0, h, H:, :] = jnp.zeros((H, T), BF)
            self.QA[1, h, H:, :] = jnp.zeros((H, T), BF)
            self.DOA[h, H:, :] = jnp.zeros((H, T), BF)
            return carry

        lax.fori_loop(0, NQ, blank, 0)

        def clear(i, carry):
            rows = pl.ds(pl.multiple_of(i * 64, 64), 64)
            self.DA[rows, :] = jnp.zeros((64, 1024), BF)
            self.DO[rows, :] = jnp.zeros((64, D), BF)
            self.DD[rows, :] = jnp.zeros((64, FF), BF)
            for k in range(3):
                self.DG[k, rows, :] = jnp.zeros((64, 1024), BF)
            return carry

        lax.fori_loop(0, D // 64, clear, 0)

    def norm(self, src, r, gain, dst, rho_ref, row):
        total = jnp.zeros((8, T), F32)
        for i in range(0, D, 8):
            v = src[r, i : i + 8, :]
            total = total + v * v
        total = jnp.sum(total, axis=0, keepdims=True)
        if row is not None:
            self.stat[r, row : row + 1, :] = total
        rho = lax.rsqrt(total * (1.0 / D) + EPS)
        rho_ref[r, 0:1, :] = rho
        for i in range(0, D, 64):
            rows = slice(i, i + 64)
            wide = jnp.concatenate([gain[rows, :]] * 4, axis=1)
            dst[r, rows, :] = (src[r, rows, :] * rho * wide).astype(BF)

    def natural_rows(self, ref, base, width, first, count):
        pieces = []
        row = first
        while row < first + count:
            f, i = row // width, row % width
            n = min(width - i, first + count - row)
            at = 128 * self.order.index(f) + base + i
            pieces.append(ref[at : at + n, :])
            row += n
        return pieces[0] if len(pieces) == 1 else jnp.concatenate(pieces, axis=0)

    def prepare(self, r):
        self.norm(self.S, r, self.gainA, self.XA, self.rhoA, 0)

    def project(self, r):
        def part(c, carry):
            cs = pl.ds(pl.multiple_of(512 * c, 512), 512)
            self.Y[cs, :] = dot(self.WA[:, cs], self.XA[r], 0, 0)
            return carry

        for c in range(2):
            part(c, 0)
        cos, sin = self.cos[...], self.sin[...]
        one = jnp.ones((1, T), F32)
        place = lax.broadcasted_iota(jnp.int32, (1, T), 1)
        bias = jnp.where(place < self.length[0], 0.0, NEG)
        for h in range(NQ + NK):
            base, width, at = (0, QB, h) if h < NQ else (QB, KB, h - NQ)
            a = self.natural_rows(self.Y, base, width, H * at, HALF)
            b = self.natural_rows(self.Y, base, width, H * at + HALF, HALF)
            first, second = a * cos - b * sin, b * cos + a * sin
            if h < NQ:
                self.QA[r, h, 0:HALF, :] = (first * SCALE).astype(BF)
                self.QA[r, h, HALF:H, :] = (second * SCALE).astype(BF)
                self.QA[r, h, H : H + 16, :] = jnp.concatenate([one, jnp.zeros((15, T), F32)], axis=0).astype(BF)
            else:
                g = h - NQ
                key = jnp.concatenate([first, second], axis=0)
                self.KT[r, g] = key.astype(BF)
                v = jnp.concatenate(
                    [
                        self.natural_rows(self.Y, QB + KB, KB, H * g, HALF),
                        self.natural_rows(self.Y, QB + KB, KB, H * g + HALF, HALF),
                    ],
                    axis=0,
                )
                self.VT[g] = v.astype(BF)
                ones3 = jnp.ones((3, T), F32)
                tail = jnp.zeros((H - 4, T), F32)
                ktall = jnp.concatenate([key, bias, ones3, tail], axis=0)
                vtall = jnp.concatenate([v, jnp.zeros((1, T), F32), ones3, tail], axis=0)
                for ts in lane_tiles():
                    self.KTOK[r, g, ts, :] = ktall[:, ts].T.astype(BF)
                    self.VTOK[r, g, ts, :] = vtall[:, ts].T.astype(BF)

    def diagonal(self):
        key = lax.broadcasted_iota(jnp.int32, (BLK, BLK), 0)
        query = lax.broadcasted_iota(jnp.int32, (BLK, BLK), 1)
        return key <= query

    def attend(self, r, links):
        low, high = slice(0, BLK), slice(BLK, T)

        def head(h, carry):
            g = h // GROUP
            allowed = self.diagonal()
            at = pl.ds(pl.multiple_of(h * H, H), H)
            s = dot(self.KTOK[r, g, low, :], self.QA[r, h, :, low], 1, 0)
            s = jnp.where(allowed, s, NEG)
            top = jnp.max(s, axis=0, keepdims=True)
            p = jnp.exp(s - top)
            total = jnp.sum(p, axis=0, keepdims=True)
            o = dot(self.VT[g, :, low], p.astype(BF), 1, 0)
            self.AT[r, at, low] = (o * (1.0 / total)).astype(BF)
            lse0 = top + jnp.log(total)
            s0 = dot(self.KTOK[r, g, low, :], self.QA[r, h, :, high], 1, 0)
            s1 = dot(self.KTOK[r, g, high, :], self.QA[r, h, :, high], 1, 0)
            s1 = jnp.where(allowed, s1, NEG)
            top = jnp.maximum(jnp.max(s0, axis=0, keepdims=True), jnp.max(s1, axis=0, keepdims=True))
            p0 = jnp.exp(s0 - top)
            p1 = jnp.exp(s1 - top)
            total = jnp.sum(p0, axis=0, keepdims=True) + jnp.sum(p1, axis=0, keepdims=True)
            o = dot(self.VT[g, :, low], p0.astype(BF), 1, 0) + dot(self.VT[g, :, high], p1.astype(BF), 1, 0)
            self.AT[r, at, high] = (o * (1.0 / total)).astype(BF)
            lse1 = top + jnp.log(total)
            lse = jnp.concatenate([lse0, lse1], axis=1)
            rows = [jnp.ones((1, T), F32)] + parts_of(-lse) + [jnp.zeros((12, T), F32)]
            self.QA[r, h, H : H + 16, :] = jnp.concatenate(rows, axis=0).astype(BF)
            return carry

        def group(g, carry):
            [head(GROUP * g + k, 0) for k in range(GROUP)]
            links.run_if(r == 0, HEADS[g])
            return carry

        for g in range(NK):
            group(g, 0)

    def rest_of_output(self):
        self.WO[:, NF * OW :] = dot(self.WA[...], self.pick[...], 1, 1).astype(BF)

    def after(self, value, src, r, dst, to, row, squares):
        n = value.shape[0]
        dst[to, row : row + n, :] = src[r, row : row + n, :] + value
        for i in range(n // 8):
            part = value[8 * i : 8 * i + 8]
            squares = squares + part * part
        return squares

    def out_project(self, r):
        self.Y[0:D, :] = dot(self.WO[...], self.AT[r], 0, 0)
        squares = jnp.zeros((8, T), F32)
        for b in range(NF):
            f = self.order[b]
            squares = self.after(self.Y[OW * b : OW * b + OW, :], self.S, r, self.M, r, QB * f, squares)
            at = NF * OW + 8 * b
            squares = self.after(self.Y[at : at + 8, :], self.S, r, self.M, r, QB * f + OW, squares)
        self.stat[r, 1:2, :] = jnp.sum(squares, axis=0, keepdims=True)

    def mlp(self, r, links):
        self.norm(self.M, r, self.gainM, self.XM, self.rhoM, None)

        def half(y, carry):
            cs = pl.ds(pl.multiple_of(512 * y, 512), 512)

            def part(i, carry):
                to = pl.ds(pl.multiple_of(512 * i, 512), 512)
                self.Y[to, :] = dot(self.WG[i, :, cs], self.XM[r], 0, 0)
                return carry

            for i in range(3):
                part(i, 0)

            def block(z, carry):
                f = self.natural(y, z)
                for j in range(3):
                    gate_at, up_at = self.places(j)
                    gate = self.Y[pl.ds(pl.multiple_of(gate_at[0] * 512 + 128 * z + gate_at[1], 64), 64), :]
                    up = self.Y[pl.ds(pl.multiple_of(up_at[0] * 512 + 128 * z + up_at[1], 64), 64), :]
                    rows = pl.ds(pl.multiple_of(FB * f + 64 * j, 64), 64)
                    self.GATE[r, rows, :] = gate.astype(BF)
                    self.UP[r, rows, :] = up.astype(BF)
                    self.HID[r, rows, :] = (gate * jax.nn.sigmoid(gate) * up).astype(BF)
                return carry

            for z in range(4):
                block(z, 0)
            links.run_if(r == 0, MLP[y])
            return carry

        for y in range(2):
            half(y, 0)
        self.Y[0:D, :] = dot(self.WDT[...], self.HID[r], 1, 0)
        squares = jnp.zeros((8, T), F32)
        for b in range(NF):
            squares = self.after(self.Y[QB * b : QB * b + QB, :], self.M, r, self.S, r + 1, QB * self.order[b], squares)
        self.stat[r, 2:3, :] = jnp.sum(squares, axis=0, keepdims=True)

    def natural(self, y, z):
        return 2 * z + y if self.order[1] == 2 else 4 * y + z

    def places(self, j):
        return ((0, 0), (0, 64), (1, 0))[j], ((1, 64), (2, 0), (2, 64))[j]

    def write_output(self):
        valid = self.valid[0:1, :]
        for ts in lane_tiles():
            v = jnp.where(valid[:, ts] > 0.0, self.S[2, :, ts], 0.0)
            self.out[:, ts] = v.astype(BF)

    def pack_down(self):
        for k in range(NF // 2):
            rows = [self.G[QB * self.order[b] : QB * self.order[b] + QB, :] for b in (2 * k, 2 * k + 1)]
            self.GLD[2 * QB * k : 2 * QB * k + 2 * QB, :] = jnp.concatenate(rows, axis=0).astype(BF)

    def pack_out(self):
        tails = []
        for b in range(NF):
            at = QB * self.order[b]
            self.GLO[OW * b : OW * b + OW, :] = self.G[at : at + OW, :].astype(BF)
            tails.append(self.G[at + OW : at + QB, :])
        self.GLO[NF * OW : D, :] = jnp.concatenate(tails, axis=0).astype(BF)

    def add_term(self, dst, index, value):
        dst[index] = (value + dst[index].astype(F32)).astype(dst.dtype)

    def norm_back(self, src, r, rho_ref, gain, slot):
        rho = rho_ref[r, 0:1, :]
        total = jnp.zeros((8, T), F32)
        for i in range(0, D, 64):
            rows = slice(i, i + 64)
            wide = jnp.concatenate([gain[rows, :]] * 4, axis=1)
            e, v = self.E[rows, :], src[r, rows, :]
            product = e * v
            weighted = product * wide
            for k in range(0, 64, 8):
                total = total + weighted[k : k + 8]
            share = product * rho
            self.gacc[slot, rows, :] += share[:, :128] + share[:, 128:256] + share[:, 256:384] + share[:, 384:]
        mean = jnp.sum(total, axis=0, keepdims=True) * (1.0 / D)
        back = rho * rho * mean
        for i in range(0, D, 64):
            rows = slice(i, i + 64)
            wide = jnp.concatenate([gain[rows, :]] * 4, axis=1)
            self.G[rows, :] += rho * (self.E[rows, :] * wide - src[r, rows, :] * back)

    def mlp_back(self, r, links):
        self.pack_down()
        for c in range(2):
            cs = slice(768 * c, 768 * c + 768)
            self.add_term(self.DD, (slice(None), cs), dot(self.GLD[...], self.HID[r, cs, :], 1, 1))
        links.run_if(r == 0, AFTER_DOWN)

        def hidden(k, carry):
            rows = pl.ds(pl.multiple_of(2 * FB * k, 128), 2 * FB)
            self.Y[0 : 2 * FB, :] = dot(self.WDT[:, rows], self.GLD[...], 0, 0)
            for m in range(2):
                f = 2 * k + m
                b = k + 4 * m if self.order[1] == 2 else f
                for j in range(3):
                    at = pl.ds(pl.multiple_of(FB * f + 64 * j, 64), 64)
                    grad = self.Y[FB * m + 64 * j : FB * m + 64 * j + 64, :]
                    gate = self.GATE[r, at, :].astype(F32)
                    up = self.UP[r, at, :].astype(F32)
                    sig = jax.nn.sigmoid(gate)
                    silu = gate * sig
                    gate_at, up_at = self.places(j)
                    to = pl.ds(pl.multiple_of(1024 * gate_at[0] + 128 * b + gate_at[1], 64), 64)
                    self.DGU[to, :] = (grad * up * (sig + silu * (1.0 - sig))).astype(BF)
                    to = pl.ds(pl.multiple_of(1024 * up_at[0] + 128 * b + up_at[1], 64), 64)
                    self.DGU[to, :] = (grad * silu).astype(BF)
            links.run_if(r == 0, HIDDEN[k])
            return carry

        for k in range(4):
            hidden(k, 0)

        def matrix(i, carry):
            grad = self.DGU[pl.ds(pl.multiple_of(1024 * i, 1024), 1024), :]
            self.add_term(self.DG, (i,), dot(self.XM[r], grad, 1, 1))
            links.run_if(r == 0, AFTER_GATE[i])
            return carry

        for i in range(3):
            matrix(i, 0)
        self.E[...] = dot(self.WG[0], self.DGU[0:1024, :], 1, 0)

        def back(i, carry):
            grad = self.DGU[pl.ds(pl.multiple_of(1024 * i, 1024), 1024), :]
            self.E[...] = self.E[...] + dot(self.WG[i], grad, 1, 0)
            return carry

        for i in (1, 2):
            back(i, 0)
        links.run_if(r == 0, BEFORE_NORM)
        self.norm_back(self.M, r, self.rhoM, self.gainM, 1)

    def attend_back(self, r, links):
        self.pack_out()
        term = dot(self.AT[r], self.GLO[0:D, :], 1, 1)
        self.add_term(self.DO, (slice(None), slice(0, NF * OW)), term[:, : NF * OW])
        self.DO[:, NF * OW :] = term[:, NF * OW :].astype(BF)
        links.run_if(r == 0, AFTER_OUT)
        self.E[...] = dot(self.WO[...], self.GLO[0:D, :], 1, 0)
        links.run_if(r == 0, BEFORE_HEADS)
        for h in range(NQ):
            rows = slice(H * h, H * h + H)
            do = self.E[rows, :].astype(BF)
            self.DOA[h, 0:H, :] = do
            delta = jnp.sum(do.astype(F32) * self.AT[r, rows, :].astype(F32), axis=0, keepdims=True)
            rows = [jnp.zeros((1, T), F32)] + parts_of(-delta) + [jnp.zeros((12, T), F32)]
            self.DOA[h, H : H + 16, :] = jnp.concatenate(rows, axis=0).astype(BF)
        low, high = slice(0, BLK), slice(BLK, T)
        self.Y[D : D + 2 * NK * H, :] = jnp.zeros((2 * NK * H, T), F32)

        def head(h, carry):
            g = h // GROUP
            allowed = self.diagonal()
            at = pl.ds(pl.multiple_of(h * H, H), H)
            kat = pl.ds(pl.multiple_of(D + g * H, H), H)
            vat = pl.ds(pl.multiple_of(D + NK * H + g * H, H), H)
            q, do = self.QA[r, h], self.DOA[h]
            k0, k1 = self.KTOK[r, g, low, :], self.KTOK[r, g, high, :]
            v0, v1 = self.VTOK[r, g, low, :], self.VTOK[r, g, high, :]
            t0, t1 = self.KT[r, g, :, low], self.KT[r, g, :, high]

            p = jnp.where(allowed, jnp.exp(dot(k0, q[:, low], 1, 0)), 0.0)
            ds = (p * dot(v0, do[:, low], 1, 0)).astype(BF)
            p = p.astype(BF)
            self.Y[at, low] = dot(t0, ds, 1, 0) * SCALE
            dk0 = dot(q[0:H, low], ds, 1, 1)
            dv0 = dot(do[0:H, low], p, 1, 1)

            p = jnp.exp(dot(k0, q[:, high], 1, 0))
            ds = (p * dot(v0, do[:, high], 1, 0)).astype(BF)
            p = p.astype(BF)
            dq = dot(t0, ds, 1, 0)
            dk0 += dot(q[0:H, high], ds, 1, 1)
            dv0 += dot(do[0:H, high], p, 1, 1)

            p = jnp.where(allowed, jnp.exp(dot(k1, q[:, high], 1, 0)), 0.0)
            ds = (p * dot(v1, do[:, high], 1, 0)).astype(BF)
            p = p.astype(BF)
            self.Y[at, high] = (dq + dot(t1, ds, 1, 0)) * SCALE
            self.Y[kat, low] += dk0
            self.Y[vat, low] += dv0
            self.Y[kat, high] += dot(q[0:H, high], ds, 1, 1)
            self.Y[vat, high] += dot(do[0:H, high], p, 1, 1)
            return carry

        def group(g, carry):
            [head(GROUP * g + k, 0) for k in range(GROUP)]
            links.run_if(r == 0, BACK_HEADS[g])
            return carry

        for g in range(NK):
            group(g, 0)

    def project_back(self, r, links):
        cos, sin = self.cos[...], self.sin[...]
        for h in range(NQ + NK):
            first, second = slice(H * h, H * h + HALF), slice(H * h + HALF, H * h + H)
            a, b = self.Y[first, :], self.Y[second, :]
            self.Y[first, :] = a * cos + b * sin
            self.Y[second, :] = b * cos - a * sin
        for b in range(NF):
            f = self.order[b]
            rows = jnp.concatenate(
                [
                    self.Y[QB * f : QB * f + QB, :],
                    self.Y[D + KB * f : D + KB * f + KB, :],
                    self.Y[D + NK * H + KB * f : D + NK * H + KB * f + KB, :],
                    jnp.zeros((128 - QB - 2 * KB, T), F32),
                ],
                axis=0,
            )
            self.GLO[128 * b : 128 * b + 128, :] = rows.astype(BF)
        def part(c, carry):
            cs = pl.ds(pl.multiple_of(512 * c, 512), 512)
            term = dot(self.XA[r], self.GLO[cs, :], 1, 1) + dot(self.DO[:, NF * OW :], self.pick[:, cs], 1, 0)
            self.add_term(self.DA, (slice(None), cs), term)
            return carry

        for c in range(2):
            part(c, 0)
        links.run_if(r == 0, AFTER_QKV)
        self.E[...] = dot(self.WA[...], self.GLO[...], 1, 0)
        self.norm_back(self.S, r, self.rhoA, self.gainA, 0)

    def write_grad(self):
        for ts in lane_tiles():
            self.gin[:, ts] = self.G[:, ts]

    def small(self):
        valid = self.valid[0:1, :]
        rows = [jnp.sum(self.gacc[i].T, axis=0, keepdims=True) for i in range(2)]
        sums = jnp.sum(jnp.where(valid > 0.0, jnp.concatenate([self.stat[0, 0:3], self.stat[1, 0:3]], axis=0), 0.0), axis=1, keepdims=True)
        count = jnp.sum(valid, axis=1, keepdims=True)
        lane = lax.broadcasted_iota(jnp.int32, (6, D), 1)
        return jnp.concatenate(rows + [jnp.where(lane < 128, sums, count)], axis=0)


SCRATCH = dict(
    S=((3, D, T), F32), G=((D, T), F32), E=((D, T), F32), Y=((1536, T), F32),
    XA=((2, D, T), BF), XM=((2, D, T), BF), rhoA=((2, 8, T), F32), rhoM=((2, 8, T), F32),
    QA=((2, NQ, 128, T), BF), KT=((2, NK, H, T), BF), VT=((NK, H, T), BF),
    KTOK=((2, NK, T, 128), BF), VTOK=((2, NK, T, 128), BF), AT=((2, D, T), BF), M=((2, D, T), F32),
    GATE=((2, FF, T), BF), UP=((2, FF, T), BF), HID=((2, FF, T), BF),
    GLD=((D, T), BF), GLO=((1024, T), BF), DGU=((2 * FF, T), BF), DOA=((NQ, 128, T), BF),
    stat=((2, 8, T), F32), valid=((8, T), F32), gacc=((2, D, 128), F32), gainA=((D, 128), F32), gainM=((D, 128), F32), pick=((H, 1024), BF),
)
WEIGHTS = dict(WA=((D, 1024), BF), WO=((D, D), BF), WG=((3, D, 1024), BF), WDT=((D, FF), BF))
GRADS = dict(DA=((D, 1024), BF), DO=((D, D), BF), DG=((3, D, 1024), BF), DD=((D, FF), BF))

class Alone:
    def run_if(self, condition, steps):
        pass

    def written(self):
        pass


def applications(w, links):
    def forward(r, carry):
        w.prepare(r)
        links.run_if(r == 0, BEFORE_PROJECT)
        w.project(r)
        links.run_if(r == 0, AFTER_PROJECT)
        w.attend(r, links)
        pl.when(r == 0)(w.rest_of_output)
        links.run_if(r == 0, BEFORE_OUT)
        w.out_project(r)
        links.run_if(r == 0, BEFORE_MLP)
        w.mlp(r, links)
        return carry

    def backward(i, carry):
        w.mlp_back(1 - i, links)
        w.attend_back(1 - i, links)
        w.project_back(1 - i, links)
        return carry

    lax.fori_loop(0, 2, forward, 0)
    w.write_output()
    links.written()
    lax.fori_loop(0, 2, backward, 0)


def compute_kernel(order, names, *refs):
    w = Work(order, dict(zip(names, refs)))
    w.start()
    applications(w, Alone())
    w.write_grad()
    w.tiny[...] = w.small()


def local_compute(order, x, length, ga, gm, ct, packed):
    cos, sin = rope_tables()
    ins = dict(length=length, x=x, ct=ct, ga=ga, gm=gm, cos=jnp.asarray(cos), sin=jnp.asarray(sin), **packed)
    outs = dict(out=((D, T), BF), gin=((D, T), F32), tiny=((8, D), F32), **GRADS)
    names = list(ins) + list(outs) + list(SCRATCH)
    vmem = pl.BlockSpec(memory_space=pltpu.VMEM)
    results = pl.pallas_call(
        functools.partial(compute_kernel, order, names),
        out_shape=[jax.ShapeDtypeStruct(*s) for s in outs.values()],
        in_specs=[pl.BlockSpec(memory_space=pltpu.SMEM)] + [vmem] * (len(ins) - 1),
        out_specs=[vmem] * len(outs),
        scratch_shapes=[pltpu.VMEM(*s) for s in SCRATCH.values()],
        compiler_params=pltpu.CompilerParams(vmem_limit_bytes=VMEM_LIMIT),
    )(*ins.values())
    return dict(zip(outs, results))


def pack(order, q, k, v, o, g, u, d):
    def cols(w, width):
        return w.reshape(w.shape[0], NF, width)[:, np.array(order)]
    ob = cols(o, QB)
    wa = jnp.concatenate([cols(q, QB), cols(k, KB), cols(v, KB), ob[:, :, OW:]], axis=2).reshape(D, 1024)
    wo = jnp.concatenate([ob[:, :, :OW].reshape(D, NF * OW), ob[:, :, OW:].reshape(D, D - NF * OW)], axis=1)
    wg = jnp.concatenate([cols(g, FB), cols(u, FB)], axis=2).reshape(D, NF, 3, 128)
    wg = wg.transpose(2, 0, 1, 3).reshape(3, D, 1024)
    wd = d.T.reshape(NF, QB, FF)[np.array(order)].reshape(D, FF)
    return dict(WA=wa, WO=wo, WG=wg, WDT=wd)


def unpack(order, r):
    back = np.argsort(np.array(order))
    a = r["DA"].astype(F32).reshape(D, NF, 128)[:, back]
    o = r["DO"][:, : NF * OW].astype(F32).reshape(D, NF, OW)[:, back]
    o = jnp.concatenate([o, a[:, :, 120:]], axis=2).reshape(D, D)
    g = r["DG"].astype(F32).reshape(3, D, NF, 128).transpose(1, 2, 0, 3).reshape(D, NF, 2 * FB)[:, back]
    d = r["DD"].astype(F32).reshape(NF, QB, FF)[back].reshape(D, FF).T
    return (
        a[:, :, :QB].reshape(D, D), a[:, :, QB : QB + KB].reshape(D, NK * H), a[:, :, QB + KB : 120].reshape(D, NK * H),
        o, g[:, :, :FB].reshape(D, FF), g[:, :, FB:].reshape(D, FF), d,
    )


PIECES = ("A0", "A1", "O", "G0", "G1", "G2", "D0", "D1")
CUT = dict(A0=(0, 80), A1=(80, ROWS - 80), D0=(0, 256), D1=(256, 128))
MESH = pl.DeviceIdType.MESH


def region(refs, piece, dp, y, z=0, count=4):
    ref, line = refs[piece[0]], 4 * y + z
    if piece[0] == "D":
        first, size = CUT[piece]
        rows = pl.ds(pl.multiple_of(QB * line, 16), QB * count)
        return ref.at[rows, pl.ds(pl.multiple_of(LANES * dp + first, 128), size)]
    width = OW if piece == "O" else 128
    first, size = CUT.get(piece, (0, ROWS))
    rows = pl.ds(pl.multiple_of(ROWS * dp + first, 16), size)
    lanes = pl.ds(pl.multiple_of(width * line, 128), width * count)
    return ref.at[int(piece[1]), rows, lanes] if piece[0] == "G" else ref.at[rows, lanes]


def shape_of(piece, count):
    if piece[0] == "D":
        return (QB * count, CUT[piece][1])
    return (CUT.get(piece, (0, ROWS))[1], (OW if piece == "O" else 128) * count)


def slip_shape(piece):
    return (QB + 8, CUT[piece][1]) if piece[0] == "D" else (CUT.get(piece, (0, ROWS))[1], 128)


def cut(piece, line, z):
    if piece == "O":
        return jnp.concatenate([line[:, OW * z : OW * z + OW]] * 2, axis=1)
    return jnp.concatenate([line[QB * z : QB * z + QB], jnp.zeros((8, line.shape[1]), F32)], axis=0)


def when(condition, action):
    if condition is None:
        action()
    else:
        pl.when(condition)(action)


class Links:
    def __init__(self, refs):
        self.__dict__.update(refs)
        self.weights = dict(A=refs["WA"], O=refs["WO"], G=refs["WG"], D=refs["WDT"])
        self.grads = dict(A=refs["DA"], O=refs["DO"], G=refs["DG"], D=refs["DD"])
        self.dp, f = lax.axis_index("dp"), lax.axis_index("fsdp")
        self.x, self.c = self.dp // 2, lax.rem(self.dp, 2)
        self.z, self.y = f // 2, lax.rem(f, 2)
        self.ny = 1 - self.y
        places = [(1 - self.x, self.ny), (self.x, self.ny), (1 - self.x, self.y), (self.x, self.y)]
        self.mine = [(2 * x + self.c, y) for x, y in places]
        self.theirs = [(2 * x + 1 - self.c, y) for x, y in places]
        self.far = 2 * (1 - self.x) + self.c
        self.other = 2 * self.x + 1 - self.c
        self.sib = (self.other, f)
        self.xn = (self.far, f)
        self.yn = (self.dp, 2 * self.z + 1 - self.y)
        self.peer = [None] + [lax.rem(self.z + k, 4) for k in (1, 2, 3)]
        self.zn = [None] + [(self.dp, 2 * self.peer[k] + self.y) for k in (1, 2, 3)]
        self.side = [None, (self.dp, 2 * (self.z + 1) + self.y), (self.dp, 2 * (self.z - 1) + self.y)]
        self.here = {(sign, t): (self.z + sign * t >= 0) & (self.z + sign * t < 4) for sign in (1, -1) for t in (1, 2, 3)}
        self.on = {(-1, 0): self.z < 3, (1, 0): self.z > 0}
        for sign, t in self.here:
            self.on[sign, t] = self.here[sign, t] & self.on[sign, 0]
        self.copies = {}
        self.used = 0

    def written(self):
        pltpu.make_async_copy(self.out, self.outfar, self.home.at[0]).start()

    def turned(self):
        pltpu.make_async_copy(self.G, self.gin, self.home.at[1]).start()

    def greet(self):
        for device in [self.sib, self.xn, self.yn] + self.zn[1:]:
            pl.semaphore_signal(pltpu.get_barrier_semaphore(), inc=1, device_id=device, device_id_type=MESH)

    def met(self):
        pl.semaphore_wait(pltpu.get_barrier_semaphore(), 6)

    def send(self, name, src, dst, device, condition=None):
        index = self.used
        self.used += 1

        def copy():
            return pltpu.make_async_remote_copy(
                src_ref=src(),
                dst_ref=dst(),
                send_sem=self.sent.at[index],
                recv_sem=self.came.at[index],
                device_id=device,
                device_id_type=MESH,
            )

        when(condition, lambda: copy().start())
        self.copies[name] = (copy, condition)

    def arrived(self, *names, condition=None):
        for name in names:
            when(condition, lambda name=name: self.copies[name][0]().wait_recv())

    def finish(self):
        pltpu.make_async_copy(self.out, self.outfar, self.home.at[0]).wait()
        pltpu.make_async_copy(self.G, self.gin, self.home.at[1]).wait()
        for copy, condition in self.copies.values():
            when(condition, lambda copy=copy: copy().wait_send())

    def run_if(self, condition, steps):
        if steps:
            pl.when(condition)(functools.partial(self.run, *steps))

    def run(self, *steps):
        for step in steps:
            kind, piece = step.split()
            getattr(self, kind)(piece)


    def spread(self, tag, p, device, dp=None, y=None, z=0, count=4):
        block = lambda: region(self.weights, p, self.dp if dp is None else dp, self.y if y is None else y, z, count)
        self.send(("w", p, tag), block, block, device)

    def block(self, p, z):
        if p[0] in "OD":
            return getattr(self, "slip" + p).at[z]
        return region(self.weights, p, self.dp, self.y, z, 1)

    def hop(self, p, t):
        for tag, sign in (("r", -1), ("l", 1)):
            here = self.here.get((sign, t))
            if t > 0:
                self.arrived(("w", p, tag, t - 1), condition=here)
            block = lambda sign=sign: self.block(p, self.z + sign * t)
            if t < 3:
                self.send(("w", p, tag, t), block, block, self.side[-sign], self.on[sign, t])
            if p[0] in "AG" and t > 0:
                self.send(("w", p, "x", tag, t), block, block, self.xn, here)
                self.send(("w", p, "y", tag, t), block, block, self.yn, here)

    def own(self, p):
        for axis, device in (("x", self.xn), ("y", self.yn)):
            block = lambda: self.block(p, self.z)
            self.send(("w", p, axis, "r", 0), block, block, device)

    def share(self, p):
        self.hop(p, 0)

    def one(self, p):
        self.hop(p, 1)

    def two(self, p):
        self.hop(p, 2)

    def line(self, p):
        self.hop(p, 3)
        if p[0] in "OD":
            slips = [getattr(self, "slip" + p)[z].astype(F32) for z in range(4)]
            if p == "O":
                whole = jnp.concatenate([slip[:, :OW] for slip in slips], axis=1)
            else:
                whole = jnp.concatenate([slip[:QB] for slip in slips], axis=0)
            region(self.weights, p, self.dp, self.y)[...] = whole.astype(BF)
            self.spread("x", p, self.xn)
            self.spread("y", p, self.yn)
        self.spread("s", p, self.sib)

    def across(self, p, axis):
        if p[0] in "OD":
            self.arrived(("w", p, axis))
            return
        for t in range(4):
            for tag, sign in (("r", -1), ("l", 1)):
                if t > 0 or sign < 0:
                    self.arrived(("w", p, axis, tag, t), condition=self.here.get((sign, t)))

    def cross(self, p):
        self.across(p, "x")
        self.spread("xy", p, self.yn, dp=self.far, count=2)
        self.spread("sx", p, self.sib, dp=self.far)
        self.across(p, "y")
        self.spread("yx", p, self.xn, y=self.ny, z=2, count=2)
        self.spread("sy", p, self.sib, y=self.ny)

    def rest(self, p):
        self.arrived(("w", p, "xy"))
        self.spread("sxy", p, self.sib, dp=self.far, y=self.ny, count=2)
        self.arrived(("w", p, "yx"))
        self.spread("syx", p, self.sib, dp=self.far, y=self.ny, z=2, count=2)

    def end(self, p):
        self.arrived(*[("w", p, tag) for tag in ("s", "sx", "sy", "sxy", "syx")])


    def term(self, p, dp, y, z=0, count=4):
        return region(self.grads, p, dp, y, z, count)

    def add(self, p, dp, y, z, count, came):
        at = self.term(p, dp, y, z, count)
        at[...] = at[...] + came[...]

    def sibs(self, p):
        for i in range(4):
            src = lambda i=i: self.term(p, *self.theirs[i])
            self.send(("g", p, "s", i), src, lambda i=i: getattr(self, "one" + p).at[i], self.sib)

    def pair(self, p):
        for i in range(4):
            self.arrived(("g", p, "s", i))
            self.add(p, *self.mine[i], 0, 4, getattr(self, "one" + p).at[i])
            if i < 2:
                src = lambda i=i: self.term(p, *self.mine[i], 0, 2)
                self.send(("g", p, "y", i), src, lambda i=i: getattr(self, "twoy" + p).at[i], self.yn)
            if i in (0, 2):
                src = lambda i=i: self.term(p, *self.mine[i], 2, 2)
                self.send(("g", p, "x", i // 2), src, lambda i=i: getattr(self, "twox" + p).at[i // 2], self.xn)

    def twos(self, p):
        self.arrived(("g", p, "y", 0))
        self.add(p, self.far, self.y, 0, 2, getattr(self, "twoy" + p).at[0])
        src = lambda: self.term(p, self.far, self.y, 0, 2)
        self.send(("g", p, "yx"), src, lambda: getattr(self, "threex" + p), self.xn)
        self.arrived(("g", p, "x", 0))
        self.add(p, self.dp, self.ny, 2, 2, getattr(self, "twox" + p).at[0])
        src = lambda: self.term(p, self.dp, self.ny, 2, 2)
        self.send(("g", p, "xy"), src, lambda: getattr(self, "threey" + p), self.yn)

    def fours(self, p):
        self.arrived(("g", p, "y", 1), ("g", p, "x", 1), ("g", p, "yx"), ("g", p, "xy"))
        for z, two, three in ((0, "twoy", "threex"), (2, "twox", "threey")):
            at = self.term(p, self.dp, self.y, z, 2)
            at[...] = at[...] + getattr(self, two + p)[1] + getattr(self, three + p)[...]
        if p[0] in "OD":
            line = self.term(p, self.dp, self.y)[...].astype(F32)
            for z in range(4):
                getattr(self, "part" + p)[z] = cut(p, line, z).astype(BF)
        for k in (1, 3, 2):
            if p[0] in "OD":
                src = lambda k=k: getattr(self, "part" + p).at[self.peer[k]]
            else:
                src = lambda k=k: self.term(p, self.dp, self.y, self.peer[k], 1)
            self.send(("g", p, "z", k), src, lambda k=k: getattr(self, "four" + p).at[k - 1], self.zn[k])

    def total(self, p):
        own = getattr(self, "part" + p)[self.z] if p[0] in "OD" else self.term(p, self.dp, self.y, self.z, 1)[...]
        total = own.astype(F32)
        for k in (1, 2, 3):
            self.arrived(("g", p, "z", k))
            total = total + getattr(self, "four" + p)[k - 1].astype(F32)
        if p[0] == "D":
            first, size = CUT[p]
            self.sumD[:, first : first + size] = total[:QB, :]
        else:
            at = 128 * ("A", "O", "G0", "G1", "G2").index("A" if p[0] == "A" else p)
            first, size = CUT.get(p, (0, ROWS))
            self.sumN[first : first + size, at : at + 128] = total


    def tiny(self, step):
        step = int(step)
        if step > 0:
            self.arrived(("t", step - 1))
            self.tinies[step] = self.tinies[step - 1] + self.tinyin[step - 1]
        if step < 3:
            device = (self.sib, self.xn, self.yn)[step]
            self.send(("t", step), lambda: self.tinies.at[step], lambda: self.tinyin.at[step], device)
        else:
            for k in (1, 2, 3):
                self.send(("t", step, k), lambda: self.tinies.at[3], lambda k=k: self.tinyz.at[k], self.zn[k])

    def tiny_end(self):
        self.tinyz[0] = self.tinies[3]
        for k in (1, 2, 3):
            self.arrived(("t", 3, k))
        total = None
        for z in range(4):
            term = self.tinyz[lax.rem(self.z - z + 4, 4)]
            total = term if total is None else total + term
        self.sumT[...] = total


def rooms():
    shapes = {}
    for p in PIECES:
        shapes["one" + p] = ((4,) + shape_of(p, 4), BF)
        for room in ("twoy", "twox"):
            shapes[room + p] = ((2,) + shape_of(p, 2), BF)
        for room in ("threex", "threey"):
            shapes[room + p] = (shape_of(p, 2), BF)
        shapes["four" + p] = ((3,) + slip_shape(p), BF)
        if p[0] in "OD":
            shapes["slip" + p] = ((4,) + slip_shape(p), BF)
            shapes["part" + p] = ((4,) + slip_shape(p), BF)
    shapes["tinies"] = ((4, 8, D), F32)
    shapes["tinyin"] = ((3, 8, D), F32)
    shapes["tinyz"] = ((4, 8, D), F32)
    return shapes


COPIES = len(PIECES) * (6 + 14 + 7 + 13) + 6


def pack_own(links, refs):
    rows = lambda *names: [refs[n][...].astype(F32) for n in names]
    q, k, v, o, g, u, d = rows("q", "k", "v", "o", "g", "u", "d")
    gu = jnp.concatenate([g, u], axis=1)
    a = jnp.concatenate([q, k.T, v.T, o[:, OW:]], axis=1)
    whole = dict(A0=a[:80], A1=a[80:], G0=gu[:, :128], G1=gu[:, 128:256], G2=gu[:, 256:])
    for p in PIECES:
        if p == "O":
            links.slipO[links.z] = cut(p, o, 0).astype(BF)
        elif p[0] == "D":
            first, size = CUT[p]
            getattr(links, "slip" + p)[links.z] = cut(p, d[:, first : first + size], 0).astype(BF)
        else:
            region(links.weights, p, links.dp, links.y, links.z, 1)[...] = whole[p].astype(BF)


BEGIN = ("own A1", "share A1", "own A0", "share A0", "own G1", "own G2", "own G0", "share G0")
BEFORE_PROJECT = ("share G2", "one A1", "one A0", "share G1", "one G0", "one G2", "two A1", "two A0", "share O", "two G0", "two G2", "line A1", "line A0", "one G1", "share D1", "line G0", "one O", "line G2", "cross A1", "share D0", "two G1", "one D1", "cross A0", "two O", "cross G0", "line G1", "two D1", "one D0", "rest A0", "cross G2", "line O", "end A0", "rest A1", "two D0", "cross G1", "end A1")
AFTER_PROJECT = ("line D1", "cross O", "line D0")
HEADS = ((), ("rest G0", "rest G1", "rest G2", "rest O"), ("cross D1", "end O", "end G0"))
BEFORE_OUT = ()
BEFORE_MLP = ("end G1", "end G2", "cross D0")
MLP = (("rest D1",), ("rest D0", "end D0", "end D1"))
AFTER_DOWN = ("sibs D1", "sibs D0")
HIDDEN = (("pair D1",), (), ("pair D0",), ())
AFTER_GATE = (("sibs G0",), ("sibs G1", "twos D1"), ("sibs G2", "pair G0"))
BEFORE_NORM = ("twos D0", "pair G1")
AFTER_OUT = ("sibs O", "fours D1")
BEFORE_HEADS = ("twos G0",)
BACK_HEADS = (("pair G2", "twos G1", "pair O"), ("fours D0", "twos G2", "fours G0"), ("twos O", "fours G1"))
AFTER_QKV = ("sibs A0", "sibs A1", "pair A0", "pair A1")
LAST = ("tiny 0", "fours G2", "fours O", "tiny 1", "twos A0", "tiny 2", "twos A1", "total D1", "total D0", "total G0")
VERY_LAST = ("fours A0", "tiny 3", "total G1", "fours A1", "total G2", "total O", "total A0", "total A1")

def whole_kernel(order, names, *args):
    refs = dict(zip(names, args))
    w, links = Work(order, refs), Links(refs)
    links.greet()
    pack_own(links, refs)
    links.met()
    links.run(*BEGIN)
    w.start()
    applications(w, links)
    links.turned()
    links.tinies[0] = w.small()
    links.run(*LAST)
    links.run(*VERY_LAST)
    links.tiny_end()
    links.finish()


def finish_kernel(*refs):
    out, gin, sums, sumd, tiny, oout, ogin, ga, q, k, v, o, gm, g, u, d, rms = refs
    oout[...] = out[...]
    ogin[...] = gin[...]
    q[...] = sums[:, :QB]
    k[...] = sums[:, QB : QB + KB].T
    v[...] = sums[:, QB + KB : 120].T
    o[...] = jnp.concatenate([sums[:, 128 : 128 + OW], sums[:, 120:128]], axis=1)
    g[...] = sums[:, 256 : 256 + FB]
    u[...] = sums[:, 256 + FB : 256 + 2 * FB]
    d[...] = sumd[...]
    ga[...] = tiny[0:1, :].reshape(D)
    gm[...] = tiny[1:2, :].reshape(D)
    lane = lax.broadcasted_iota(jnp.int32, (1, 3), 1)
    for r in range(2):
        first, second, third = [tiny[2 + 3 * r + i : 3 + 3 * r + i, 0:3] for i in range(3)]
        squares = jnp.where(lane == 0, first, jnp.where(lane == 1, second, third))
        rms[r : r + 1, :] = jnp.sqrt(squares / (tiny[2:3, 128:131] * D))


def whole(x, length, ga, q, k, v, o, gm, g, u, d, ct):
    order = [2 * (b % 4) + b // 4 for b in range(NF)]
    cos, sin = rope_tables()
    ins = dict(
        length=length, x=x[0].T, ct=ct[0].T, ga=ga, gm=gm, cos=jnp.asarray(cos), sin=jnp.asarray(sin),
        q=q, k=k.T, v=v.T, o=o, g=g, u=u, d=d.T,
    )
    outs = dict(
        outfar=((D, T), BF), gin=((D, T), F32), sumN=((ROWS, 256 + 2 * FB), F32), sumD=((QB, LANES), F32), sumT=((8, D), F32)
    )
    scratch = dict(SCRATCH, out=((D, T), BF), **WEIGHTS, **GRADS, **rooms())
    names = list(ins) + list(outs) + list(scratch) + ["sent", "came", "home"]
    vmem = pl.BlockSpec(memory_space=pltpu.VMEM)
    r = pl.pallas_call(
        functools.partial(whole_kernel, order, names),
        out_shape=[jax.ShapeDtypeStruct(*s) for s in outs.values()],
        in_specs=[pl.BlockSpec(memory_space=pltpu.SMEM)] + [vmem] * (len(ins) - 1),
        out_specs=[pl.BlockSpec(memory_space=pl.ANY)] * 2 + [vmem] * (len(outs) - 2),
        scratch_shapes=[pltpu.VMEM(*s) for s in scratch.values()]
        + [pltpu.SemaphoreType.DMA((n,)) for n in (COPIES, COPIES, 2)],
        compiler_params=pltpu.CompilerParams(
            vmem_limit_bytes=VMEM_LIMIT, collective_id=0, has_side_effects=True
        ),
    )(*ins.values())
    rows = [
        ((D, T), BF), ((D, T), F32), ((D,), F32), (q.shape, F32), (k.shape[::-1], F32), (v.shape[::-1], F32),
        (o.shape, F32), ((D,), F32), (g.shape, F32), (u.shape, F32), (d.shape[::-1], F32), ((2, 3), F32),
    ]
    out, gin, ga, q, k, v, o, gm, g, u, d, rms = pl.pallas_call(
        finish_kernel,
        out_shape=[jax.ShapeDtypeStruct(*s) for s in rows],
        in_specs=[vmem] * len(outs),
        out_specs=[vmem] * len(rows),
    )(*r)
    return out.T[None], gin.T[None], ga, q, k.T, v.T, o, gm, g, u, d.T, rms


def by_collectives(x, length, ga, q, k, v, o, gm, g, u, d, ct):
    order = list(range(NF))
    full = [lax.all_gather(lax.all_gather(w, "fsdp", axis=1, tiled=True), "dp", axis=0, tiled=True) for w in (q, k, v, o, g, u, d)]
    packed = pack(order, *full)
    results = [local_compute(order, x[i].T, length[i : i + 1], ga, gm, ct[i].T, packed) for i in range(x.shape[0])]
    out = jnp.stack([r["out"].T for r in results])
    gin = jnp.stack([r["gin"].T for r in results])
    tiny = lax.psum(sum(r["tiny"] for r in results), ("dp", "fsdp"))
    terms = [unpack(order, r) for r in results]
    grads = [
        lax.psum_scatter(
            lax.psum_scatter(sum(t), "dp", scatter_dimension=0, tiled=True), "fsdp", scatter_dimension=1, tiled=True
        )
        for t in zip(*terms)
    ]
    rms = jnp.sqrt(tiny[2:8, 0].reshape(2, 3) / (tiny[2, 128] * D))
    gq, gk, gv, go, gg, gu, gd = grads
    return out, gin, tiny[0], gq, gk, gv, go, tiny[1], gg, gu, gd, rms


def solution(mesh):
    blocks = P("dp", "fsdp")
    slots = P(("dp", "fsdp"), None, None)
    in_specs = (slots, P(("dp", "fsdp")), P(), blocks, blocks, blocks, blocks, P(), blocks, blocks, blocks, slots)
    out_specs = (slots, slots, P(), blocks, blocks, blocks, blocks, P(), blocks, blocks, blocks, P())

    def on_device(*args):
        fits = mesh.shape["dp"] == 4 and mesh.shape["fsdp"] == 8 and args[0].shape[0] == 1
        return (whole if fits else by_collectives)(*args)

    return jax.shard_map(on_device, mesh=mesh, in_specs=in_specs, out_specs=out_specs, check_vma=False)
```
